32 devices in a mesh: seq: 4 (over z), tp: 8 (over y, x, core).
Axes of the slice: x: 2, y: 2, z: 4, core: 2. Of those that a mesh axis runs over, the one named last changes fastest.
Arguments:
- sequence_in: bfloat16 [1536, 2048], P('tp', 'seq')
- conv_weight: bfloat16 [3, 1536, 3, 1536], P(None, 'tp')
- norm_gain: float32 [3, 1536], P(None, 'tp'), may hold values from 0.1 to 1.9
- tissue_scale: float32 [367, 1536], replicated, may hold values from 0.3 to 3
- donor_offset: int32 [1024], P('seq'), may hold values from 0 to 511
- acceptor_owner: int32 [1024, 1], P('seq'), may hold values from 0 to 3; in each aligned block of 256 rows (0 to 255, 256 to 511, ...) at most 128 rows name the same one
- acceptor_offset: int32 [1024], P('seq'), may hold values from 0 to 511
- tissue: int32 [1024], P('seq'), may hold values from 0 to 366
- tower_grad: float32 [1536, 2048], P('tp', 'seq'), may hold values from -6 to 6
- score_grad: float32 [1024], P('seq'), may hold values from -24 to 24
Outputs:
- scores: float32 [1024], P('seq')
- input_grad: float32 [1536, 2048], P('tp', 'seq')
- weight_grad: float32 [3, 1536, 3, 1536], P(None, 'tp')
- gain_grad: float32 [3, 1536], P(None, 'tp')
The draws below stay inside these ranges and needn't reach their ends.
Inputs may be any that keep to these rules, and one draw needn't show every extreme that they name: `acceptor_owner`: among the 256 junctions of one index of seq, at most 128 have their acceptor on one index of seq.
All inputs are finite; a program needn't handle non-finite values.
Results may differ from the reference program's by a relative error of at most 0.025.
Values may be sent and summed in bfloat16 or wider, within the bound.
No kernel may reach another device: no remote copies, remote signals or barrier semaphores. Data moves between devices by JAX's collectives and lax.ppermute only.
A program may use at most 128 MiB of HBM per device.

```python
import math
import jax
import jax.numpy as jnp
import numpy as np
from jax import lax

CHANNELS = 1536
TISSUES = 367
LAYERS = 3
POS_DEV = 512
J_DEV = 256
POSITIONS = 2048
JUNCTIONS = 1024
CAP = 128
N_SEQ = 4


def draw_sequence_in(key, part):
    key_base, key_chan, key_pos = jax.random.split(key, 3)
    ramp = jnp.arange(CHANNELS, dtype=jnp.float32)[:, None] / CHANNELS
    chan_scale = jnp.exp(jnp.log(3.0) * ramp) * 10.0 ** (0.5 * jax.random.uniform(key_chan, (CHANNELS, 1), jnp.float32))
    pos_scale = 10.0 ** (0.5 * jax.random.uniform(key_pos, (1, POSITIONS), jnp.float32))
    base = jax.random.normal(key_base, (CHANNELS, POSITIONS), jnp.float32)
    return (0.25 * base * chan_scale * pos_scale).astype(jnp.bfloat16)


def draw_conv_weight(key, part):
    key_noise, key_left, key_right = jax.random.split(jax.random.fold_in(key, 17), 3)
    spread = (3.0 * CHANNELS) ** (-0.5)
    common = 1.5 * spread
    left = (2 * jax.random.randint(key_left, (LAYERS, CHANNELS, 1, 1), 0, 2) - 1).astype(jnp.float32)
    right = (2 * jax.random.randint(key_right, (LAYERS, 1, 3, CHANNELS), 0, 2) - 1).astype(jnp.float32)
    noise = jnp.clip(jax.random.normal(key_noise, (LAYERS, CHANNELS, 3, CHANNELS), jnp.float32), -4.0, 4.0)
    return (common * left * right + spread * noise).astype(jnp.bfloat16)


def plant(values, key, smallest, high):
    longest = values.shape.index(max(values.shape))
    spots = []
    for shift in (0, 1):
        where = [jax.random.randint(jax.random.fold_in(key, axis), (), 0, length) for axis, length in enumerate(values.shape)]
        where[longest] = (where[longest] + shift) % values.shape[longest]
        spots.append(tuple(where))
    return values.at[spots[0]].set(smallest).at[spots[1]].set(high)


def level_of(rng, dims, cuts, low, largest):
    level = 1.0
    for dim, parts in cuts:
        draws = jax.random.uniform(jax.random.fold_in(jax.random.fold_in(rng, 6), dim), (parts,), jnp.float32, low / len(cuts), largest / len(cuts))
        level = level * jnp.repeat(jnp.exp(draws), dims[dim] // parts).reshape((-1,) + (1,) * (len(dims) - 1 - dim))
    return level


def assign_block(key, own, number, rows, count, top, limit, skew):
    sequence = jax.random.permutation(key, count)
    packed, usual = load_shares(count, rows * top, limit, skew, True), load_shares(count, rows * top, limit, skew, False)
    places = jnp.arange(count)

    def named(sizes, offset_by):
        used = int((sizes > 0).sum())
        fixed = max(1, used // 4)
        moved = fixed + (places - fixed + offset_by * (used - fixed)) % max(1, count - fixed)
        return jnp.zeros((count,), jnp.int32).at[sequence[jnp.where(places < fixed, places, moved)]].set(jnp.asarray(sizes, jnp.int32))

    sizes = jnp.where(number % 4 == 0, named(packed, number // 4), named(usual, number - number // 4 - 1))
    mixed = jax.random.permutation(jax.random.fold_in(own, 3), count)
    giver, sink = mixed[0:count // 2 * 2:2], mixed[1:count // 2 * 2:2]
    slack = jnp.minimum(sizes[giver] - 1, limit - sizes[sink]) // 2
    slack = jnp.where((giver == sequence[0]) | (sink == sequence[0]) | (sizes[sink] == 0), 0, jnp.maximum(slack, 0))
    moved = jax.random.randint(jax.random.fold_in(own, 4), (count // 2,), 0, 1 << 20) % (slack + 1)
    sizes = sizes.at[giver].add(-moved).at[sink].add(moved)
    items = jnp.searchsorted(jnp.cumsum(sizes), jnp.arange(rows * top), side="right").astype(jnp.int32)
    grid = items.reshape(top, rows).T
    grid = grid[jax.random.permutation(jax.random.fold_in(own, 1), rows)]
    offset_by = jax.random.randint(jax.random.fold_in(own, 2), (rows, 1), 0, top)
    return jnp.take_along_axis(grid, (jnp.arange(top)[None, :] + offset_by) % top, axis=1)


def load_shares(amount, total, limit, lean, full):
    portions = [(1 << 20) // math.isqrt(standing ** lean) + 1 for standing in range(1, amount + 1)]
    largest = limit if full else min(limit, max(-(-total // amount), total * portions[0] // sum(portions)))
    least = 1 if total - largest >= amount - 1 else 0
    holding, surplus = [largest] + [least] * (amount - 1), total - largest - least * (amount - 1)
    while surplus > 0:
        free = [i for i in range(1, amount) if holding[i] < largest] or [i for i in range(1, amount) if holding[i] < limit]
        whole, budget = sum([portions[i] for i in free]), surplus
        for i in free:
            more = min(limit - holding[i], max(1, budget * portions[i] // whole), surplus)
            holding[i] = holding[i] + more
            surplus = surplus - more
    return np.array(holding)


def bell_draw(own_key, dims, scale, bound, shards=(), held_as=jnp.bfloat16):
    array = scale * jax.random.normal(own_key, dims, jnp.float32)
    if shards:
        array = array * level_of(own_key, dims, shards, -0.22, 0.18)
    return jnp.clip(array, -bound, bound).astype(held_as)


def setup_inputs(seed: int = 0) -> dict:
    keys = jax.random.split(jax.random.key(seed), 11)
    sequence_in = draw_sequence_in(jax.random.fold_in(keys[10], 71), 0)
    conv_weight = draw_conv_weight(jax.random.fold_in(keys[10], 71), 0)
    norm_gain = jnp.clip(1.0 + 0.18 * jax.random.normal(keys[2], (LAYERS, CHANNELS), jnp.float32), 0.1, 1.9)
    tissue_scale = jnp.clip(jnp.exp(jax.random.uniform(keys[3], (TISSUES, CHANNELS), jnp.float32, math.log(0.3), math.log(3.0))), 0.3, 3.0)
    donor_offset = plant(jax.random.randint(keys[4], (JUNCTIONS,), 0, POS_DEV), jax.random.fold_in(keys[4], 1), 0, POS_DEV - 1).astype(jnp.int32)
    acceptor_owner_keys = jax.random.split(jax.random.fold_in(keys[5], 1), JUNCTIONS // J_DEV)
    acceptor_owner_turns = jax.random.permutation(jax.random.fold_in(keys[5], 3), JUNCTIONS // J_DEV)
    acceptor_owner = jax.vmap(lambda own, number: assign_block(jax.random.fold_in(keys[5], 2), own, number, J_DEV, N_SEQ, 1, CAP, 2))(acceptor_owner_keys, acceptor_owner_turns).reshape((JUNCTIONS, 1))
    acceptor_offset = plant(jax.random.randint(keys[6], (JUNCTIONS,), 0, POS_DEV), jax.random.fold_in(keys[6], 1), 0, POS_DEV - 1).astype(jnp.int32)
    tissue = plant(jax.random.randint(keys[7], (JUNCTIONS,), 0, TISSUES), jax.random.fold_in(keys[7], 1), 0, TISSUES - 1).astype(jnp.int32)
    tower_grad = bell_draw(keys[8], (CHANNELS, POSITIONS), 1.0, 6.0, ((0, 8), (1, 4)), jnp.float32)
    score_grad = bell_draw(keys[9], (JUNCTIONS,), 4.0, 24.0, ((0, 4),), jnp.float32)
    return dict(sequence_in=sequence_in, conv_weight=conv_weight, norm_gain=norm_gain, tissue_scale=tissue_scale, donor_offset=donor_offset, acceptor_owner=acceptor_owner, acceptor_offset=acceptor_offset, tissue=tissue, tower_grad=tower_grad, score_grad=score_grad)


EPSILON = 1e-06

def gelu_fn(value):
    return jax.nn.gelu(value, approximate=True)

def forward_taps(weights, padded, reach, length):
    total = jnp.zeros((weights.shape[0], length), jnp.float32)
    for tap in range(3):
        total = total + jnp.dot(weights[:, tap, :], padded[:, tap * reach:tap * reach + length], preferred_element_type=jnp.float32)
    return total

def backward_taps(weights, grad_pad, reach, length):
    total = jnp.zeros((weights.shape[2], length), jnp.float32)
    for tap in range(3):
        total = total + lax.dot_general(weights[:, tap, :], grad_pad[:, (2 - tap) * reach:(2 - tap) * reach + length], (((0,), (0,)), ((), ())), preferred_element_type=jnp.float32)
    return total

def weight_taps(padded, grad_bf, reach, length):
    blocks = []
    for tap in range(3):
        blocks.append(lax.dot_general(grad_bf, padded[:, tap * reach:tap * reach + length], (((1,), (1,)), ((), ())), preferred_element_type=jnp.float32))
    return jnp.stack(blocks, axis=1)

def reference(sequence_in, conv_weight, norm_gain, tissue_scale, donor_offset, acceptor_owner, acceptor_offset, tissue, tower_grad, score_grad):
    length = POSITIONS
    state = sequence_in
    stored = []
    for layer in range(LAYERS):
        reach = 2 ** (layer + 3)
        stream = state.astype(jnp.float32)
        power = lax.optimization_barrier(jnp.sum(stream * stream, axis=0)) / CHANNELS
        inverse = 1.0 / jnp.sqrt(power + EPSILON)
        pre_act = stream * inverse[None, :] * norm_gain[layer][:, None]
        hidden = gelu_fn(pre_act).astype(jnp.bfloat16)
        padded = jnp.pad(hidden, ((0, 0), (reach, reach)))
        mixed = forward_taps(conv_weight[layer], padded, reach, length)
        stored.append((state, inverse, pre_act, padded))
        state = (stream + mixed).astype(jnp.bfloat16)
    final = state.astype(jnp.float32)
    owner = acceptor_owner[:, 0]
    donor_pos = jnp.arange(JUNCTIONS, dtype=jnp.int32) // J_DEV * POS_DEV + donor_offset
    accept_pos = owner * POS_DEV + acceptor_offset
    donor_cols = final[:, donor_pos].T
    accept_cols = final[:, accept_pos].T
    member = (tissue[:, None] == jnp.arange(TISSUES, dtype=jnp.int32)[None, :]).astype(jnp.float32)
    tissue_rows = jnp.dot(member, tissue_scale, precision=lax.Precision.HIGHEST)
    root = math.sqrt(CHANNELS)
    scores = lax.optimization_barrier(jnp.sum(donor_cols * accept_cols * tissue_rows, axis=1)) / root
    weight_j = score_grad / root
    donor_back = weight_j[:, None] * accept_cols * tissue_rows
    accept_back = weight_j[:, None] * donor_cols * tissue_rows
    upstream = tower_grad.at[:, donor_pos].add(donor_back.T)
    upstream = upstream.at[:, accept_pos].add(accept_back.T)
    weight_list = [None] * LAYERS
    gain_list = [None] * LAYERS
    for layer in reversed(range(LAYERS)):
        reach = 2 ** (layer + 3)
        old_state, inverse, pre_act, padded = stored[layer]
        stream = old_state.astype(jnp.float32)
        grad_bf = upstream.astype(jnp.bfloat16)
        grad_pad = jnp.pad(grad_bf, ((0, 0), (reach, reach)))
        weight_list[layer] = weight_taps(padded, grad_bf, reach, length)
        back_hidden = backward_taps(conv_weight[layer], grad_pad, reach, length)
        _, gelu_back = jax.vjp(gelu_fn, pre_act)
        back_pre = gelu_back(back_hidden)[0]
        gain_list[layer] = lax.optimization_barrier(jnp.sum(back_pre * stream * inverse[None, :], axis=1))
        back_norm = back_pre * norm_gain[layer][:, None]
        inner = lax.optimization_barrier(jnp.sum(back_norm * stream, axis=0))
        upstream = upstream + inverse[None, :] * back_norm - stream * (inverse ** 3)[None, :] * inner[None, :] / CHANNELS
    return (scores, upstream, jnp.stack(weight_list), jnp.stack(gain_list))
```

```python
import functools
import math

import jax
import jax.numpy as jnp
from jax import lax
from jax.experimental import pallas as pl
from jax.experimental.pallas import tpu as pltpu
from jax.sharding import PartitionSpec as P

LAYERS = 3
EPSILON = 1e-06
EDGE = 64
CHUNK = 384
ROWS = 16
K0 = math.sqrt(2.0 / math.pi)
K1 = K0 * 0.044715
F32 = jnp.float32
BF16 = jnp.bfloat16

VMEM = pl.BlockSpec(memory_space=pltpu.VMEM)
SMEM = pl.BlockSpec(memory_space=pltpu.SMEM)
HBM = pl.BlockSpec(memory_space=pl.ANY)


def params(**kw):
    return pltpu.CompilerParams(vmem_limit_bytes=40 * 1024 * 1024, **kw)


def reach_of(layer):
    return 2 ** (layer + 3)


def swap(x, axis, mask):
    count = lax.axis_size(axis)
    return lax.ppermute(x, axis, [(i, i ^ mask) for i in range(count)])


def gather_tp(x):
    if lax.axis_size("tp") == 8:
        far = [x] + [swap(x, "tp", m) for m in (2, 4, 6)]
        near = [swap(v, "tp", 1) for v in far]
        return [v for pair in zip(far, near) for v in pair]
    whole = lax.all_gather(x, "tp", axis=0)
    return [whole[i] for i in range(whole.shape[0])]


def tp_order(me):
    count = lax.axis_size("tp")
    steps = jnp.arange(count, dtype=jnp.int32)
    return me ^ steps if count == 8 else steps


def gather_seq(x):
    if lax.axis_size("seq") == 4:
        one = swap(x, "seq", 1)
        two = swap(x, "seq", 2)
        return [x, one, two, swap(x, "seq", 3)]
    whole = lax.all_gather(x, "seq", axis=0)
    return [whole[i] for i in range(whole.shape[0])]


def seq_order(me):
    count = lax.axis_size("seq")
    steps = jnp.arange(count, dtype=jnp.int32)
    return me ^ steps if count == 4 else steps


def roll(x, shift):
    width = x.shape[1]
    shift = shift % width
    return x if shift == 0 else pltpu.roll(x, shift, 1)


def own_part(x, length):
    return roll(x, -EDGE)[:, :length]


def in_sequence(seq_at, width, length, total):
    at = lax.broadcasted_iota(jnp.int32, (1, width), 1) + (seq_at * length - EDGE)
    return (at >= 0) & (at < total)


def prep_kernel(meta, seq_ref, tower_ref, first_ref, second_ref, gain_ref, state_ref, window_ref, *, n_tp, n_seq):
    ch, length = seq_ref.shape
    seq_at = meta[n_tp + n_seq + 1]
    even = lax.rem(seq_at, 2) == 0
    first = first_ref[...].astype(F32)
    second = second_ref[...].astype(F32)
    right = jnp.where(even, first, second)
    left = jnp.where(even, second, first)
    lane = lax.broadcasted_iota(jnp.int32, (ch, 128), 1)
    low = lane < EDGE
    rt, lt = right[:, :128], left[:, :128]
    edge = jnp.where(low, rt, roll(lt, EDGE))
    state = jnp.concatenate([seq_ref[...].astype(F32), edge], axis=1)
    state = roll(state, EDGE)
    gains = gain_ref[...]
    high = gains.astype(BF16).astype(F32)
    rest = gains - high
    middle = rest.astype(BF16).astype(F32)
    last = (rest - middle).astype(BF16).astype(F32)
    width = length + 2 * EDGE
    wide = lax.broadcasted_iota(jnp.int32, (ch, width), 1)
    for layer in range(LAYERS):
        state = jnp.where(wide == layer, high[:, layer : layer + 1], state)
        state = jnp.where(wide == LAYERS + layer, middle[:, layer : layer + 1], state)
        state = jnp.where(wide == width - 8 + layer, last[:, layer : layer + 1], state)
    state_ref[...] = state.astype(BF16)
    th = jnp.where(low, roll(rt, EDGE), lt)
    tl = jnp.where(low, right[:, 128:], roll(left[:, 128:], EDGE))
    window_ref[...] = roll(jnp.concatenate([tower_ref[...], th + tl], axis=1), EDGE)


def lookup_kernel(meta, table_ref, *refs, n_tp, n_seq):
    pieces = refs[:n_seq]
    rec_ref, rows_ref = refs[n_seq:]
    count = pieces[0].shape[1]
    for m in range(n_seq):
        at = meta[n_tp + m]
        rec_ref[:, pl.ds(pl.multiple_of(at * count, 128), count)] = pieces[m][...]
    table = table_ref[...]
    ch, tissues = table.shape
    high = table.astype(BF16)
    rest = table - high.astype(F32)
    middle = rest.astype(BF16)
    last = (rest - middle.astype(F32)).astype(BF16)
    stack = jnp.concatenate([high, middle, last], axis=0)
    which = rec_ref[2:3, :].astype(jnp.int32)
    hit = lax.broadcasted_iota(jnp.int32, (tissues, which.shape[1]), 0) == which
    got = jnp.dot(stack, jnp.where(hit, 1.0, 0.0).astype(BF16), preferred_element_type=F32)
    rows_ref[...] = got[:ch] + (got[ch : 2 * ch] + got[2 * ch :])


def forward_kernel(meta, w_ref, own_ref, *refs, layer, n_tp, n_seq, length):
    pieces, refs = refs[:n_tp], refs[n_tp:]
    if layer == 0:
        state_ref, hidden_ref, slope_ref, inverse_ref, gain_ref, held, weights, sem = refs
    else:
        gain_ref, state_ref, hidden_ref, slope_ref, inverse_ref, held, weights, sem = refs
    ch, width = pieces[0].shape
    channels = ch * n_tp
    reach = reach_of(layer)
    me, seq_at = meta[n_tp + n_seq], meta[n_tp + n_seq + 1]
    copy = pltpu.make_async_copy(w_ref.at[layer], weights, sem)
    copy.start()

    def add_power(j, acc):
        rows = pl.ds(pl.multiple_of(j * ROWS, ROWS), ROWS)
        for piece in pieces:
            x = piece[rows, :].astype(F32)
            sq = x * x
            for i in range(0, ROWS, 8):
                acc = acc + sq[i : i + 8]
        return acc

    acc = lax.fori_loop(0, ch // ROWS, add_power, jnp.zeros((8, width), F32))
    power = jnp.sum(acc, axis=0, keepdims=True) / channels
    inverse = 1.0 / jnp.sqrt(power + EPSILON)
    inverse_ref[...] = jnp.broadcast_to(inverse, (8, width))

    def activate(j, carry):
        rows = pl.ds(pl.multiple_of(j * ROWS, ROWS), ROWS)
        for m, piece in enumerate(pieces):
            at = meta[m]
            x = piece[rows, :].astype(F32)
            if layer == 0:
                front, back = x[:, :128], x[:, width - 128 :]
                cols = [
                    front[:, l : l + 1] + (front[:, LAYERS + l : LAYERS + l + 1] + back[:, 120 + l : 121 + l])
                    for l in range(LAYERS)
                ]
                lane = lax.broadcasted_iota(jnp.int32, (ROWS, 128), 1)
                gain_ref[at, rows, :] = jnp.where(lane == 0, cols[0], jnp.where(lane == 1, cols[1], cols[2]))
                gain = cols[0]
            else:
                gain = gain_ref[at, rows, layer : layer + 1]
            scaled = x * gain
            pre = scaled * inverse
            sq = pre * pre
            th = jnp.tanh(pre * (K0 + K1 * sq))
            half = 0.5 + 0.5 * th
            hidden = pre * half
            held[at, rows, :] = hidden.astype(BF16)
            slope = half + (hidden - hidden * th) * (K0 + (3.0 * K1) * sq)
            slope_ref[at, rows, :] = (slope * scaled).astype(BF16)
        return carry

    lax.fori_loop(0, ch // ROWS, activate, 0)
    hidden_ref[...] = own_part(held[me].astype(F32), length).astype(BF16)
    copy.wait()
    every = held[...].reshape(channels, width)
    total = own_ref[...].astype(F32)
    for tap in range(3):
        part = jnp.dot(weights[tap * ch : (tap + 1) * ch, :], every, preferred_element_type=F32)
        total = total + roll(part, (1 - tap) * reach)
    total = jnp.where(in_sequence(seq_at, width, length, n_seq * length), total, 0.0).astype(BF16)
    if layer == LAYERS - 1:
        state_ref[...] = own_part(total.astype(F32), length).astype(BF16)
    else:
        state_ref[...] = total


def send_back(layer, upstream, meta, weights, slope_ref, taps, grad_ref, out_refs, score, n_tp, n_seq, length):
    ch, width = upstream.shape
    reach = reach_of(layer)
    me, seq_at = meta[n_tp + n_seq], meta[n_tp + n_seq + 1]
    grad = jnp.where(in_sequence(seq_at, width, length, n_seq * length), upstream, 0.0)
    grad = grad.astype(BF16).astype(F32)
    grad_ref[...] = own_part(grad, length).astype(BF16)
    for tap in range(3):
        taps[tap * ch : (tap + 1) * ch, :] = roll(grad, (tap - 1) * reach).astype(BF16)
    inner = jnp.zeros((8, width), F32)
    parts = CHUNK // ch
    chunks = ch * n_tp // CHUNK
    for r in range(chunks):
        at = (me // 2) ^ r if n_tp == 8 else r
        cols = pl.ds(pl.multiple_of(at * CHUNK, 128), CHUNK)
        part = lax.dot_general(
            weights[:, cols], taps[...], (((0,), (0,)), ((), ())), preferred_element_type=F32
        )
        for q in range(parts):
            prod = part[q * ch : (q + 1) * ch] * slope_ref[at * parts + q].astype(F32)
            inner = inner + jnp.sum(prod.reshape(ch // 8, 8, width), axis=0)
        if n_tp == 8:
            keep_ref, send_ref = out_refs
            zero = lax.rem(me, 2) == 0
            keep_ref[r] = jnp.where(zero, part[:ch], part[ch:]).astype(BF16)
            send_ref[r * ch : (r + 1) * ch, :] = jnp.where(zero, part[ch:], part[:ch]).astype(BF16)
        else:
            for q in range(parts):
                out_refs[0][at * parts + q] = part[q * ch : (q + 1) * ch].astype(BF16)
    row = lax.broadcasted_iota(jnp.int32, (8, width), 0)
    extra = jnp.where(row == 0, jnp.sum(inner, axis=0, keepdims=True), 0.0)
    if score is not None:
        score = jnp.concatenate([score, jnp.zeros((1, width - score.shape[1]), F32)], axis=1)
        extra = jnp.where(row == 1, score, extra)
    if n_tp == 8:
        out_refs[1][n_tp // 2 * ch :, :] = split_rows(extra)
    else:
        out_refs[1][...] = extra


def split_rows(x):
    high = x.astype(BF16).astype(F32)
    return jnp.concatenate([high, x - high], axis=0).astype(BF16)


def join_rows(x):
    x = x.astype(F32)
    return x[:8] + x[8:]


def junction_kernel(meta, w_ref, window_ref, rec_ref, rows_ref, slope_ref, *refs, n_tp, n_seq, root):
    pieces, refs = refs[:n_seq], refs[n_seq:]
    up_ref, grad_ref, *refs = refs
    *out_refs, weights, taps, donors, sem = refs
    ch, length = pieces[0].shape
    width = window_ref.shape[1]
    count = rec_ref.shape[1]
    share = count // n_seq
    me, seq_at = meta[n_tp + n_seq], meta[n_tp + n_seq + 1]
    copy = pltpu.make_async_copy(w_ref.at[LAYERS - 1], weights, sem)
    copy.start()
    donor = rec_ref[0:1, :].astype(jnp.int32)
    accept = rec_ref[1:2, :].astype(jnp.int32)
    weight = rec_ref[3:4, :] / root
    place = lax.broadcasted_iota(jnp.int32, (length, count), 0)
    accepts = jnp.zeros((ch, count), F32)
    for m in range(n_seq):
        at = meta[n_tp + m]
        cols = pl.ds(pl.multiple_of(at * share, 128), share)
        block = pieces[m][...]
        mine = rec_ref[0:1, cols].astype(jnp.int32) - at * length
        hit = lax.broadcasted_iota(jnp.int32, (length, share), 0) == mine
        donors[:, cols] = jnp.dot(block, jnp.where(hit, 1.0, 0.0).astype(BF16), preferred_element_type=F32)
        hit = place == accept - at * length
        accepts = accepts + jnp.dot(block, jnp.where(hit, 1.0, 0.0).astype(BF16), preferred_element_type=F32)
    rows = rows_ref[...]
    product = donors[...] * accepts * rows
    scored = jnp.sum(product, axis=0, keepdims=True) / root
    score = jnp.zeros((1, share), F32)
    for m in range(n_seq):
        score = jnp.where(seq_at == m, scored[:, m * share : (m + 1) * share], score)
    scale = rows * weight
    upstream = window_ref[...]
    spot = lax.broadcasted_iota(jnp.int32, (width, count), 0) + (seq_at * length - EDGE)
    for values, where in ((accepts * scale, donor), (donors[...] * scale, accept)):
        high = values.astype(BF16)
        low = (values - high.astype(F32)).astype(BF16)
        hit = jnp.where(spot == where, 1.0, 0.0).astype(BF16)
        both = lax.dot_general(
            jnp.concatenate([high, low], axis=0), hit, (((1,), (1,)), ((), ())), preferred_element_type=F32
        )
        upstream = upstream + (both[:ch] + both[ch:])
    up_ref[...] = upstream
    copy.wait()
    send_back(
        LAYERS - 1, upstream, meta, weights, slope_ref, taps, grad_ref, out_refs, score, n_tp, n_seq, length
    )


def pair_kernel(keep_ref, send_ref, got_ref, own_ref, *far_refs):
    count, ch, width = keep_ref.shape
    extra = join_rows(send_ref[count * ch :, :]) + join_rows(got_ref[count * ch :, :])
    split = split_rows(extra)
    for r in range(count):
        total = keep_ref[r].astype(F32) + got_ref[r * ch : (r + 1) * ch, :].astype(F32)
        if r == 0:
            own_ref[:ch, :] = total
            own_ref[ch:, :] = join_rows(split)
        else:
            far_refs[r - 1][:ch, :] = total.astype(BF16)
            far_refs[r - 1][ch:, :] = split


def backward_kernel(meta, w_ref, *refs, layer, n_far, n_tp, n_seq, length):
    own_ref, refs = refs[0], refs[1:]
    far, refs = refs[:n_far], refs[n_far:]
    up_ref, state_ref, inverse_ref, gain_ref, *refs = refs
    last = layer == 0
    if last:
        out_ref, part_ref = refs
    else:
        slope_ref, up_out, part_ref, grad_ref, *out_refs, weights, taps, sem = refs
        copy = pltpu.make_async_copy(w_ref.at[layer - 1], weights, sem)
        copy.start()
    if layer == LAYERS - 1:
        if last:
            score_ref = None
        else:
            score_ref, *out_refs = out_refs
    ch, width = up_ref.shape
    channels = ch * n_tp
    me = meta[n_tp + n_seq]
    sums = [own_ref[ch:, :]] + [join_rows(f[ch:, :]) for f in far]
    if n_far:
        extra = (sums[0] + sums[1]) + (sums[2] + sums[3])
    else:
        extra = sums[0]
    inner = extra[0:1, :]
    if layer == LAYERS - 1:
        score_ref[...] = extra
    inverse = inverse_ref[0:1, :]
    gain = gain_ref[me, :, layer : layer + 1]
    back = own_ref[:ch, :]
    for f in far:
        back = back + f[:ch, :].astype(F32)
    x = state_ref[...].astype(F32)
    pre = x * inverse * gain
    sq = pre * pre
    th = jnp.tanh(pre * (K0 + K1 * sq))
    half = 0.5 + 0.5 * th
    back = back * (half + (pre * half) * (1.0 - th) * (K0 + (3.0 * K1) * sq))
    lane = lax.broadcasted_iota(jnp.int32, (1, width), 1)
    mine = (lane >= EDGE) & (lane < EDGE + length)
    part = jnp.sum(jnp.where(mine, back * x * inverse, 0.0), axis=1, keepdims=True)
    part_ref[...] = jnp.broadcast_to(part, part_ref.shape)
    upstream = up_ref[...] + (inverse * gain) * back - x * (inverse * inverse * inverse * inner / channels)
    if last:
        out_ref[...] = own_part(upstream, length)
    else:
        up_out[...] = upstream
        copy.wait()
        send_back(
            layer - 1, upstream, meta, weights, slope_ref, taps, grad_ref, out_refs, None, n_tp, n_seq, length
        )


def weight_kernel(meta, *refs, layer, n_tp, n_seq):
    pieces, refs = refs[:n_seq], refs[n_seq:]
    every_ref, refs = refs[0], refs[1:]
    out_ref, whole, taps = refs[-3:]
    ch, length = pieces[0].shape
    reach = reach_of(layer)
    total = n_seq * length

    @pl.when(pl.program_id(0) == 0)
    def _():
        for m in range(n_seq):
            at = meta[n_tp + m]
            whole[:, pl.ds(pl.multiple_of(at * length, 128), length)] = pieces[m][...]
        grad = whole[...].astype(F32)
        lane = lax.broadcasted_iota(jnp.int32, (1, total), 1)
        taps[:ch, :] = jnp.where(lane < total - reach, roll(grad, -reach), 0.0).astype(BF16)
        taps[ch : 2 * ch, :] = whole[...]
        taps[2 * ch :, :] = jnp.where(lane >= reach, roll(grad, reach), 0.0).astype(BF16)

    acc = None
    for s in range(n_seq):
        block = every_ref[s].reshape(CHUNK, length)
        part = lax.dot_general(
            taps[:, s * length : (s + 1) * length],
            block,
            (((1,), (1,)), ((), ())),
            preferred_element_type=F32,
        )
        acc = part if acc is None else acc + part
    out_ref[...] = acc.reshape(3, ch, CHUNK)


def local(
    sequence_in,
    conv_weight,
    norm_gain,
    tissue_scale,
    donor_offset,
    acceptor_owner,
    acceptor_offset,
    tissue,
    tower_grad,
    score_grad,
):
    ch, length = sequence_in.shape
    n_tp, n_seq = lax.axis_size("tp"), lax.axis_size("seq")
    channels, total = ch * n_tp, length * n_seq
    width = length + 2 * EDGE
    share = donor_offset.shape[0]
    count = share * n_seq
    paired = n_tp == 8
    n_far = 3 if paired else 0
    me = lax.axis_index("tp").astype(jnp.int32)
    seq_at = lax.axis_index("seq").astype(jnp.int32)
    meta = jnp.concatenate([tp_order(me), seq_order(seq_at), jnp.stack([me, seq_at])])
    sizes = dict(n_tp=n_tp, n_seq=n_seq)
    weights = conv_weight.transpose(0, 2, 1, 3).reshape(LAYERS, 3 * ch, channels)

    high = lax.reduce_precision(tower_grad, 8, 7)
    low = tower_grad - high

    def edge(lanes):
        return jnp.concatenate(
            [
                sequence_in[:, lanes],
                high[:, lanes].astype(BF16),
                low[:, lanes].astype(BF16),
                jnp.zeros((ch, EDGE), BF16),
            ],
            axis=1,
        )

    left, right = edge(slice(0, EDGE)), edge(slice(length - EDGE, length))
    even = seq_at % 2 == 0
    first = lax.ppermute(jnp.where(even, right, left), "seq", [(i, i ^ 1) for i in range(n_seq)])
    pairs = [(i, i + 1) for i in range(1, n_seq - 1, 2)]
    second = lax.ppermute(jnp.where(even, left, right), "seq", pairs + [(j, i) for i, j in pairs])
    gain_cols = jnp.pad(norm_gain.T, ((0, 0), (0, 128 - LAYERS)))
    state, window = pl.pallas_call(
        functools.partial(prep_kernel, **sizes),
        out_shape=(jax.ShapeDtypeStruct((ch, width), BF16), jax.ShapeDtypeStruct((ch, width), F32)),
        in_specs=[SMEM] + [VMEM] * 5,
        out_specs=(VMEM, VMEM),
        compiler_params=params(),
        name="prep",
    )(meta, sequence_in, tower_grad, first, second, gain_cols)

    record = jnp.stack(
        [
            (donor_offset + seq_at * length).astype(F32),
            (acceptor_owner[:, 0] * length + acceptor_offset).astype(F32),
            tissue.astype(F32),
            score_grad,
        ]
        + [jnp.zeros((share,), F32)] * 4
    )
    table = lax.dynamic_slice_in_dim(tissue_scale, me * ch, ch, 1).T
    pad = -table.shape[1] % 128
    table = jnp.pad(table, ((0, 0), (0, pad)))
    records, rows = pl.pallas_call(
        functools.partial(lookup_kernel, **sizes),
        out_shape=(jax.ShapeDtypeStruct((8, count), F32), jax.ShapeDtypeStruct((ch, count), F32)),
        in_specs=[SMEM] + [VMEM] * (1 + n_seq),
        out_specs=(VMEM, VMEM),
        compiler_params=params(),
        name="lookup",
    )(meta, table, *gather_seq(record))

    stored = []
    gains = None
    for layer in range(LAYERS):
        pieces = gather_tp(state)
        final = layer == LAYERS - 1
        shapes = [
            jax.ShapeDtypeStruct((ch, length if final else width), BF16),
            jax.ShapeDtypeStruct((ch, length), BF16),
            jax.ShapeDtypeStruct((n_tp, ch, width), BF16),
            jax.ShapeDtypeStruct((8, width), F32),
        ]
        inputs = [meta, weights, state, *pieces]
        if layer == 0:
            shapes.append(jax.ShapeDtypeStruct((n_tp, ch, 128), F32))
        else:
            inputs.append(gains)
        got = pl.pallas_call(
            functools.partial(forward_kernel, layer=layer, length=length, **sizes),
            out_shape=shapes,
            in_specs=[SMEM, HBM] + [VMEM] * (len(inputs) - 2),
            out_specs=[VMEM] * len(shapes),
            scratch_shapes=[
                pltpu.VMEM((n_tp, ch, width), BF16),
                pltpu.VMEM((3 * ch, channels), BF16),
                pltpu.SemaphoreType.DMA,
            ],
            compiler_params=params(),
            name="forward",
        )(*inputs)
        if layer == 0:
            gains = got[4]
        every = lax.all_gather(got[1], ("seq", "tp"), axis=0).reshape(n_seq, n_tp, ch, length)
        stored.append((state, got[2], got[3], every))
        state = got[0]

    def product_shapes():
        if paired:
            return [
                jax.ShapeDtypeStruct((n_tp // 2, ch, width), BF16),
                jax.ShapeDtypeStruct((n_tp // 2 * ch + 16, width), BF16),
            ]
        return [jax.ShapeDtypeStruct((n_tp, ch, width), BF16), jax.ShapeDtypeStruct((8, width), F32)]

    def scratch():
        return [pltpu.VMEM((3 * ch, channels), BF16), pltpu.VMEM((3 * ch, width), BF16)]

    def reduce_tp(products):
        if not paired:
            whole, extra = products
            own = lax.psum_scatter(whole.reshape(channels, width), "tp", scatter_dimension=0, tiled=True)
            return [jnp.concatenate([own.astype(F32), lax.psum(extra, "tp")], axis=0)]
        keep, send = products
        got = swap(send, "tp", 1)
        far = jax.ShapeDtypeStruct((ch + 16, width), BF16)
        own, *far = pl.pallas_call(
            pair_kernel,
            out_shape=[jax.ShapeDtypeStruct((ch + 8, width), F32), far, far, far],
            in_specs=[VMEM] * 3,
            out_specs=[VMEM] * 4,
            compiler_params=params(),
            name="pair",
        )(keep, send, got)
        return [own] + [swap(v, "tp", 2 * r + 2) for r, v in enumerate(far)]

    blocks = gather_seq(state)
    shapes = [jax.ShapeDtypeStruct((ch, width), F32), jax.ShapeDtypeStruct((ch, length), BF16)] + product_shapes()
    upstream, grad, *products = pl.pallas_call(
        functools.partial(junction_kernel, root=math.sqrt(channels), **sizes),
        out_shape=shapes,
        in_specs=[SMEM, HBM] + [VMEM] * (4 + n_seq),
        out_specs=[VMEM] * len(shapes),
        scratch_shapes=scratch() + [pltpu.VMEM((ch, count), F32), pltpu.SemaphoreType.DMA],
        compiler_params=params(),
        name="junction",
    )(meta, weights, window, records, rows, stored[-1][1], *blocks)

    parts = [None] * LAYERS
    weight_grad = None
    scores = None
    for layer in reversed(range(LAYERS)):
        state, _, inverse, every = stored[layer]
        grads = gather_seq(grad)
        sums = reduce_tp(products)
        inputs = [meta, weights, *sums, upstream, state, inverse, gains]
        part_shape = jax.ShapeDtypeStruct((ch, 128), F32)
        if layer == 0:
            shapes = [jax.ShapeDtypeStruct((ch, length), F32), part_shape]
            extra_scratch = []
        else:
            inputs.append(stored[layer - 1][1])
            shapes = [jax.ShapeDtypeStruct((ch, width), F32), part_shape, jax.ShapeDtypeStruct((ch, length), BF16)]
            if layer == LAYERS - 1:
                shapes.append(jax.ShapeDtypeStruct((8, width), F32))
            shapes += product_shapes()
            extra_scratch = scratch() + [pltpu.SemaphoreType.DMA]
        got = pl.pallas_call(
            functools.partial(backward_kernel, layer=layer, n_far=n_far, length=length, **sizes),
            out_shape=shapes,
            in_specs=[SMEM, HBM] + [VMEM] * (len(inputs) - 2),
            out_specs=[VMEM] * len(shapes),
            scratch_shapes=extra_scratch,
            compiler_params=params(),
            name="backward",
        )(*inputs)
        parts[layer] = got[1]

        extra = [] if weight_grad is None else [weight_grad]
        weight_grad = pl.pallas_call(
            functools.partial(weight_kernel, layer=layer, **sizes),
            grid=(channels // CHUNK,),
            out_shape=jax.ShapeDtypeStruct((LAYERS, 3, ch, channels), F32),
            in_specs=[SMEM]
            + [pl.BlockSpec((ch, length), lambda i: (0, 0))] * n_seq
            + [pl.BlockSpec((n_seq, CHUNK // ch, ch, length), lambda i: (0, i, 0, 0))]
            + [HBM] * len(extra),
            out_specs=pl.BlockSpec((None, 3, ch, CHUNK), functools.partial(lambda i, layer: (layer, 0, 0, i), layer=layer)),
            scratch_shapes=[pltpu.VMEM((ch, total), BF16), pltpu.VMEM((3 * ch, total), BF16)],
            input_output_aliases={n_seq + 2: 0} if extra else {},
            compiler_params=params(),
            name="weight",
        )(meta, *grads, every, *extra)

        if layer == 0:
            input_grad = got[0]
        else:
            upstream, grad, products = got[0], got[2], got[3:]
            if layer == LAYERS - 1:
                scores, products = products[0][1, :share], products[1:]
    columns = jnp.pad(jnp.stack([p[:, 0] for p in parts]), ((0, 8 - LAYERS), (0, 0)))
    pieces = gather_seq(columns)
    if len(pieces) == 4:
        gain_grad = (pieces[0] + pieces[1]) + (pieces[2] + pieces[3])
    else:
        gain_grad = sum(pieces)
    return (scores, input_grad, weight_grad.transpose(0, 2, 1, 3), gain_grad[:LAYERS])


def solution(mesh):
    return jax.shard_map(
        local,
        mesh=mesh,
        in_specs=(
            P("tp", "seq"),
            P(None, "tp", None, None),
            P(None, "tp"),
            P(),
            P("seq"),
            P("seq", None),
            P("seq"),
            P("seq"),
            P("tp", "seq"),
            P("seq"),
        ),
        out_specs=(P("seq"), P("tp", "seq"), P(None, "tp", None, None), P(None, "tp")),
        check_vma=False,
    )
```

```python
import functools
import math

import jax
import jax.numpy as jnp
from jax import lax
from jax.experimental import pallas as pl
from jax.experimental.pallas import tpu as pltpu
from jax.sharding import PartitionSpec as P

LAYERS = 3
EPSILON = 1e-06
EDGE = 64
SPARE = 56
CHUNK = 384
ROWS = 16
K0 = math.sqrt(2.0 / math.pi)
K1 = K0 * 0.044715
F32 = jnp.float32
BF16 = jnp.bfloat16

VMEM = pl.BlockSpec(memory_space=pltpu.VMEM)
SMEM = pl.BlockSpec(memory_space=pltpu.SMEM)
HBM = pl.BlockSpec(memory_space=pltpu.HBM)


def params(mib=24):
    return pltpu.CompilerParams(vmem_limit_bytes=mib * 1024 * 1024)


def cost(flops, nbytes, special=0):
    return pl.CostEstimate(flops=flops, bytes_accessed=nbytes, transcendentals=special)


def tie(first, then):
    out = lax.optimization_barrier((tuple(first), tuple(then)))
    return list(out[0]), list(out[1])


def reach_of(layer):
    return 2 ** (layer + 3)


def swap(x, axis, mask):
    count = lax.axis_size(axis)
    return lax.ppermute(x, axis, [(i, i ^ mask) for i in range(count)])


def gather_tp(x):
    if lax.axis_size("tp") == 8:
        far = [x] + [swap(x, "tp", m) for m in (2, 4, 6)]
        near = [swap(v, "tp", 1) for v in far]
        return [v for pair in zip(far, near) for v in pair]
    whole = lax.all_gather(x, "tp", axis=0)
    return [whole[i] for i in range(whole.shape[0])]


def tp_order(me):
    count = lax.axis_size("tp")
    steps = jnp.arange(count, dtype=jnp.int32)
    return me ^ steps if count == 8 else steps


def gather_seq(x):
    if lax.axis_size("seq") == 4:
        one = swap(x, "seq", 1)
        two = swap(x, "seq", 2)
        return [x, one, two, swap(x, "seq", 3)]
    whole = lax.all_gather(x, "seq", axis=0)
    return [whole[i] for i in range(whole.shape[0])]


def seq_order(me):
    count = lax.axis_size("seq")
    steps = jnp.arange(count, dtype=jnp.int32)
    return me ^ steps if count == 4 else steps


def roll(x, shift):
    shift = shift % x.shape[1]
    return x if shift == 0 else pltpu.roll(x, shift, 1)


def position(shape, dim, length):
    at = lax.broadcasted_iota(jnp.int32, shape, dim)
    return jnp.where(at < length + EDGE, at, at - (length + 2 * EDGE))


def in_sequence(seq_at, width, length, total):
    at = position((1, width), 1, length) + seq_at * length
    return (at >= 0) & (at < total)


def halo_kernel(meta, tower_ref, first_ref, second_ref, gain_ref, halo_ref, window_ref, *, n_tp, n_seq):
    ch = tower_ref.shape[0]
    even = lax.rem(meta[n_tp + n_seq + 1], 2) == 0
    first = first_ref[...].astype(F32)
    second = second_ref[...].astype(F32)
    right = jnp.where(even, first, second)
    left = jnp.where(even, second, first)
    lane = lax.broadcasted_iota(jnp.int32, (ch, 128), 1)
    low = lane < EDGE
    halo = jnp.where(low, right[:, :128], roll(left[:, :128], EDGE))
    gains = gain_ref[...]
    high = gains.astype(BF16).astype(F32)
    rest = gains - high
    middle = rest.astype(BF16).astype(F32)
    last = rest - middle
    for k, part in enumerate((high, middle, last)):
        for layer in range(LAYERS):
            halo = jnp.where(lane == SPARE + k * LAYERS + layer, part[:, layer : layer + 1], halo)
    halo_ref[...] = halo.astype(BF16)
    length = tower_ref.shape[1]
    window_ref[:, :length] = tower_ref[...]
    th = jnp.where(low, roll(right[:, :128], EDGE), left[:, :128])
    tl = jnp.where(low, right[:, 128:], roll(left[:, 128:], EDGE))
    window_ref[:, length:] = th + tl


def lookup_kernel(meta, table_ref, *refs, n_tp, n_seq):
    pieces = refs[:n_seq]
    rec_ref, rows_ref = refs[n_seq:]
    count = pieces[0].shape[1]
    for m in range(n_seq):
        at = meta[n_tp + m]
        rec_ref[:, pl.ds(pl.multiple_of(at * count, 128), count)] = pieces[m][...]
    table = table_ref[...]
    ch, tissues = table.shape
    high = table.astype(BF16)
    rest = table - high.astype(F32)
    middle = rest.astype(BF16)
    last = (rest - middle.astype(F32)).astype(BF16)
    stack = jnp.concatenate([high, middle, last], axis=0)
    which = rec_ref[2:3, :].astype(jnp.int32)
    hit = lax.broadcasted_iota(jnp.int32, (tissues, which.shape[1]), 0) == which
    got = jnp.dot(stack, jnp.where(hit, 1.0, 0.0).astype(BF16), preferred_element_type=F32)
    rows_ref[...] = got[:ch] + (got[ch : 2 * ch] + got[2 * ch :])


def load(piece, rows):
    if isinstance(piece, tuple):
        return jnp.concatenate([part[rows, :].astype(F32) for part in piece], axis=1)
    return piece[rows, :].astype(F32)


def blocks_of(refs, layer, n_tp):
    if layer == 0:
        return list(zip(refs[:n_tp], refs[n_tp : 2 * n_tp])), refs[2 * n_tp :]
    return list(refs[:n_tp]), refs[n_tp:]


def forward_kernel(meta, w_ref, *refs, layer, n_tp, n_seq, length):
    own = refs[:2] if layer == 0 else refs[0]
    pieces, refs = blocks_of(refs[2 if layer == 0 else 1 :], layer, n_tp)
    if layer == 0:
        state_ref, inverse_ref, hidden_ref, gain_ref, *refs = refs
    else:
        gain_ref, *refs = refs
        if layer == 1:
            before_ref, *refs = refs
        state_ref, inverse_ref, *refs = refs
        *hidden_refs, held, weights, sem = refs
    if layer == 0:
        held, weights, sem = refs
    _, ch, width = held.shape
    channels = ch * n_tp
    reach = reach_of(layer)
    me, seq_at = meta[n_tp + n_seq], meta[n_tp + n_seq + 1]
    copy = pltpu.make_async_copy(w_ref.at[layer], weights, sem)
    copy.start()

    def add_power(j, acc):
        rows = pl.ds(pl.multiple_of(j * ROWS, ROWS), ROWS)
        for piece in pieces:
            x = load(piece, rows)
            sq = x * x
            for i in range(0, ROWS, 8):
                acc = acc + sq[i : i + 8]
        return acc

    acc = lax.fori_loop(0, ch // ROWS, add_power, jnp.zeros((8, width), F32))
    power = jnp.sum(acc, axis=0, keepdims=True) / channels
    inverse = 1.0 / jnp.sqrt(power + EPSILON)
    inverse_ref[...] = jnp.broadcast_to(inverse, (8, width))

    def activate(j, carry):
        rows = pl.ds(pl.multiple_of(j * ROWS, ROWS), ROWS)
        for m, piece in enumerate(pieces):
            at = meta[m]
            x = load(piece, rows)
            if layer == 0:
                halo = x[:, length:]
                cols = [
                    halo[:, SPARE + l : SPARE + l + 1]
                    + (
                        halo[:, SPARE + LAYERS + l : SPARE + LAYERS + l + 1]
                        + halo[:, SPARE + 2 * LAYERS + l : SPARE + 2 * LAYERS + l + 1]
                    )
                    for l in range(LAYERS)
                ]
                lane = lax.broadcasted_iota(jnp.int32, (ROWS, 128), 1)
                gain_ref[at, rows, :] = jnp.where(lane == 0, cols[0], jnp.where(lane == 1, cols[1], cols[2]))
                gain = cols[0]
            else:
                gain = gain_ref[at, rows, layer : layer + 1]
            pre = x * gain * inverse
            th = jnp.tanh(pre * (K0 + K1 * (pre * pre)))
            held[at, rows, :] = (pre * (0.5 + 0.5 * th)).astype(BF16)
        return carry

    lax.fori_loop(0, ch // ROWS, activate, 0)
    if layer == 0:
        hidden_ref[...] = held[me, :, :length]
    elif layer == 1:
        hidden_refs[0][:ch, :] = before_ref[...]
        hidden_refs[0][ch:, :] = held[me, :, :length]
    elif len(hidden_refs) == 1:
        hidden_refs[0][...] = held[me, :, :length]
    else:
        core = lax.rem(me, 2)
        for i in range(n_tp // 2):
            hidden_refs[0][i] = held[2 * i + core, :, :length]
            hidden_refs[1][i] = held[2 * i + 1 - core, :, :length]
    copy.wait()
    every = held[...].reshape(channels, width)
    total = load(own, slice(None))
    for tap in range(3):
        part = jnp.dot(weights[tap * ch : (tap + 1) * ch, :], every, preferred_element_type=F32)
        total = total + roll(part, (1 - tap) * reach)
    total = jnp.where(in_sequence(seq_at, width, length, n_seq * length), total, 0.0).astype(BF16)
    state_ref[...] = total[:, : state_ref.shape[1]]


def slope_kernel(meta, gain_ref, inverse_ref, *refs, layer, n_tp):
    pieces, (slope_ref, held, sems) = blocks_of(refs, layer, n_tp)
    _, ch, width = held.shape
    inverse = inverse_ref[0:1, :width]
    copies = []
    for m, piece in enumerate(pieces):
        at = meta[m]

        def derive(j, carry, m=m, piece=piece, at=at):
            rows = pl.ds(pl.multiple_of(j * ROWS, ROWS), ROWS)
            scaled = load(piece, rows)[:, :width] * gain_ref[at, rows, layer : layer + 1]
            pre = scaled * inverse
            sq = pre * pre
            th = jnp.tanh(pre * (K0 + K1 * sq))
            half = 0.5 + 0.5 * th
            hidden = pre * half
            slope = half + (hidden - hidden * th) * (K0 + (3.0 * K1) * sq)
            held[m, rows, :] = (slope * scaled).astype(BF16)
            return carry

        lax.fori_loop(0, ch // ROWS, derive, 0, unroll=2)
        copies.append(pltpu.make_async_copy(held.at[m], slope_ref.at[at], sems.at[m]))
        copies[-1].start()
    for copy in copies:
        copy.wait()


def send_back(layer, upstream, meta, weights, slopes, taps, grad_ref, out_refs, score, n_tp, n_seq, length):
    ch, width = upstream.shape
    wide = taps.shape[1]
    reach = reach_of(layer)
    me, seq_at = meta[n_tp + n_seq], meta[n_tp + n_seq + 1]
    grad = jnp.where(in_sequence(seq_at, width, length, n_seq * length), upstream, 0.0)
    grad = grad.astype(BF16).astype(F32)
    grad_ref[...] = grad[:, :length].astype(BF16)
    for tap in range(3):
        taps[tap * ch : (tap + 1) * ch, :] = roll(grad, (tap - 1) * reach)[:, :wide].astype(BF16)
    for copy in slopes[1:]:
        copy.wait()
    inner = jnp.zeros((8, wide), F32)
    parts = CHUNK // ch
    chunks = ch * n_tp // CHUNK
    for r in range(chunks):
        at = (me // 2) ^ r if n_tp == 8 else r
        cols = pl.ds(pl.multiple_of(at * CHUNK, 128), CHUNK)
        part = lax.dot_general(weights[:, cols], taps[...], (((0,), (0,)), ((), ())), preferred_element_type=F32)
        for q in range(parts):
            prod = part[q * ch : (q + 1) * ch] * slopes[0][at * parts + q].astype(F32)
            inner = inner + jnp.sum(prod.reshape(ch // 8, 8, wide), axis=0)
        if n_tp == 8:
            keep_ref, send_ref = out_refs
            zero = lax.rem(me, 2) == 0
            keep_ref[r] = jnp.where(zero, part[:ch], part[ch:]).astype(BF16)
            send_ref[r * ch : (r + 1) * ch, :] = jnp.where(zero, part[ch:], part[:ch]).astype(BF16)
        else:
            for q in range(parts):
                out_refs[0][at * parts + q] = part[q * ch : (q + 1) * ch].astype(BF16)
    row = lax.broadcasted_iota(jnp.int32, (8, wide), 0)
    extra = jnp.where(row == 0, jnp.sum(inner, axis=0, keepdims=True), 0.0)
    if score is not None:
        score = jnp.concatenate([score, jnp.zeros((1, wide - score.shape[1]), F32)], axis=1)
        extra = jnp.where(row == 1, score, extra)
    if n_tp == 8:
        out_refs[1][n_tp // 2 * ch :, :] = split_rows(extra)
    else:
        out_refs[1][...] = extra


def split_rows(x):
    high = x.astype(BF16).astype(F32)
    return jnp.concatenate([high, x - high], axis=0).astype(BF16)


def join_rows(x):
    x = x.astype(F32)
    return x[:8] + x[8:]


def fetch(layer, w_ref, slope_ref, weights, slopes, sems):
    copies = [
        pltpu.make_async_copy(w_ref.at[layer], weights, sems.at[0]),
        pltpu.make_async_copy(slope_ref, slopes, sems.at[1]),
    ]
    for copy in copies:
        copy.start()
    return [slopes] + copies


def junction_kernel(meta, w_ref, slope_ref, window_ref, rec_ref, rows_ref, *refs, n_tp, n_seq, root):
    pieces, refs = refs[:n_seq], refs[n_seq:]
    up_ref, grad_ref, *refs = refs
    *out_refs, weights, taps, slopes, donors, sems = refs
    ch, length = pieces[0].shape
    width = window_ref.shape[1]
    count = rec_ref.shape[1]
    share = count // n_seq
    seq_at = meta[n_tp + n_seq + 1]
    slopes = fetch(LAYERS - 1, w_ref, slope_ref, weights, slopes, sems)
    donor = rec_ref[0:1, :].astype(jnp.int32)
    accept = rec_ref[1:2, :].astype(jnp.int32)
    weight = rec_ref[3:4, :] / root
    place = lax.broadcasted_iota(jnp.int32, (length, count), 0)
    accepts = jnp.zeros((ch, count), F32)
    for m in range(n_seq):
        at = meta[n_tp + m]
        cols = pl.ds(pl.multiple_of(at * share, 128), share)
        block = pieces[m][...]
        mine = rec_ref[0:1, cols].astype(jnp.int32) - at * length
        hit = lax.broadcasted_iota(jnp.int32, (length, share), 0) == mine
        donors[:, cols] = jnp.dot(block, jnp.where(hit, 1.0, 0.0).astype(BF16), preferred_element_type=F32)
        hit = place == accept - at * length
        accepts = accepts + jnp.dot(block, jnp.where(hit, 1.0, 0.0).astype(BF16), preferred_element_type=F32)
    rows = rows_ref[...]
    product = donors[...] * accepts * rows
    scored = jnp.sum(product, axis=0, keepdims=True) / root
    score = jnp.zeros((1, share), F32)
    for m in range(n_seq):
        score = jnp.where(seq_at == m, scored[:, m * share : (m + 1) * share], score)
    scale = rows * weight
    upstream = window_ref[...]
    spot = position((width, count), 0, length) + seq_at * length
    for values, where in ((accepts * scale, donor), (donors[...] * scale, accept)):
        high = values.astype(BF16)
        low = (values - high.astype(F32)).astype(BF16)
        hit = jnp.where(spot == where, 1.0, 0.0).astype(BF16)
        both = lax.dot_general(
            jnp.concatenate([high, low], axis=0), hit, (((1,), (1,)), ((), ())), preferred_element_type=F32
        )
        upstream = upstream + (both[:ch] + both[ch:])
    up_ref[...] = upstream
    send_back(LAYERS - 1, upstream, meta, weights, slopes, taps, grad_ref, out_refs, score, n_tp, n_seq, length)


def pair_kernel(keep_ref, send_ref, got_ref, own_ref, *far_refs):
    count, ch, width = keep_ref.shape
    extra = join_rows(send_ref[count * ch :, :]) + join_rows(got_ref[count * ch :, :])
    split = split_rows(extra)
    for r in range(count):
        total = keep_ref[r].astype(F32) + got_ref[r * ch : (r + 1) * ch, :].astype(F32)
        if r == 0:
            own_ref[:ch, :] = total
            own_ref[ch:, :] = join_rows(split)
        else:
            far_refs[r - 1][:ch, :] = total.astype(BF16)
            far_refs[r - 1][ch:, :] = split


def backward_kernel(meta, *refs, layer, n_far, n_tp, n_seq, length):
    last = layer == 0
    if last:
        slopes = None
    else:
        w_ref, slope_ref, *refs = refs
        *refs, weights, taps, slopes, sems = refs
        slopes = fetch(layer - 1, w_ref, slope_ref, weights, slopes, sems)
    own_ref, refs = refs[0], refs[1:]
    far, refs = refs[:n_far], refs[n_far:]
    up_ref, state_ref, inverse_ref, gain_ref, *refs = refs
    out_ref, part_ref, *refs = refs
    if not last:
        grad_ref, *out_refs = refs
        if layer == LAYERS - 1:
            score_ref, *out_refs = out_refs
    ch, width = state_ref.shape
    channels = ch * n_tp
    sums = [own_ref[ch:, :]] + [join_rows(f[ch:, :]) for f in far]
    extra = (sums[0] + sums[1]) + (sums[2] + sums[3]) if n_far else sums[0]
    inner = extra[0:1, :]
    if layer == LAYERS - 1:
        score_ref[...] = extra
    inverse = inverse_ref[0:1, :width]
    gain = gain_ref[:, layer : layer + 1]
    back = own_ref[:ch, :]
    for f in far:
        back = back + f[:ch, :].astype(F32)
    x = state_ref[...].astype(F32)
    pre = x * gain * inverse
    sq = pre * pre
    th = jnp.tanh(pre * (K0 + K1 * sq))
    half = 0.5 + 0.5 * th
    back = back * (half + (pre * half) * (1.0 - th) * (K0 + (3.0 * K1) * sq))
    mine = back * x * inverse
    part = jnp.sum(mine[:, :length], axis=1, keepdims=True)
    part_ref[...] = jnp.broadcast_to(part, part_ref.shape)
    upstream = up_ref[:, :width] + (inverse * gain) * back - x * (inverse * inverse * inverse * inner / channels)
    out_ref[...] = upstream
    if not last:
        send_back(layer - 1, upstream, meta, weights, slopes, taps, grad_ref, out_refs, None, n_tp, n_seq, length)


def weight_kernel(meta, *refs, layer, n_tp, n_seq, swapped):
    pieces, refs = refs[:n_seq], refs[n_seq:]
    count = 2 * n_seq if swapped else 1
    sources, refs = refs[:count], refs[count:]
    out_ref, whole, taps, held, done, in_sems, out_sems = refs[-7:]
    ch, length = pieces[0].shape
    reach = reach_of(layer)
    total = n_seq * length
    parts = CHUNK // ch
    chunks = ch * n_tp // CHUNK
    core = lax.rem(meta[n_tp + n_seq], 2)

    def arrive(i):
        slot = i % 2
        if not swapped:
            source = sources[0]
            if len(source.shape) == 5:
                source = source.at[:, i * parts : (i + 1) * parts, layer]
            else:
                source = source.at[:, i * parts : (i + 1) * parts]
            return [pltpu.make_async_copy(source, held.at[slot], in_sems.at[slot, 0])]
        copies = []
        for m in range(n_seq):
            for q in range(2):
                where = core if q == 0 else 1 - core
                copies.append(
                    pltpu.make_async_copy(
                        sources[2 * m + q].at[i], held.at[slot, meta[n_tp + m], where], in_sems.at[slot, 2 * m + q]
                    )
                )
        return copies

    def leave(i):
        cols = pl.ds(i * CHUNK, CHUNK)
        return pltpu.make_async_copy(done.at[i % 2], out_ref.at[layer, :, :, cols], out_sems.at[i % 2])

    for copy in arrive(0):
        copy.start()
    for m in range(n_seq):
        at = meta[n_tp + m]
        whole[:, pl.ds(pl.multiple_of(at * length, 128), length)] = pieces[m][...]
    grad = whole[...].astype(F32)
    lane = lax.broadcasted_iota(jnp.int32, (1, total), 1)
    taps[:ch, :] = jnp.where(lane < total - reach, roll(grad, -reach), 0.0).astype(BF16)
    taps[ch : 2 * ch, :] = whole[...]
    taps[2 * ch :, :] = jnp.where(lane >= reach, roll(grad, reach), 0.0).astype(BF16)
    for i in range(chunks):
        if i + 1 < chunks:
            for copy in arrive(i + 1):
                copy.start()
        for copy in arrive(i):
            copy.wait()
        acc = None
        for s in range(n_seq):
            part = lax.dot_general(
                taps[:, s * length : (s + 1) * length],
                held[i % 2, s].reshape(CHUNK, length),
                (((1,), (1,)), ((), ())),
                preferred_element_type=F32,
            )
            acc = part if acc is None else acc + part
        if i >= 2:
            leave(i - 2).wait()
        done[i % 2] = acc.reshape(3, ch, CHUNK)
        leave(i).start()
    for i in range(max(0, chunks - 2), chunks):
        leave(i).wait()


def local(
    sequence_in,
    conv_weight,
    norm_gain,
    tissue_scale,
    donor_offset,
    acceptor_owner,
    acceptor_offset,
    tissue,
    tower_grad,
    score_grad,
):
    ch, length = sequence_in.shape
    n_tp, n_seq = lax.axis_size("tp"), lax.axis_size("seq")
    channels, total = ch * n_tp, length * n_seq
    width = length + 2 * EDGE
    share = donor_offset.shape[0]
    count = share * n_seq
    paired = n_tp == 8
    swapped = paired and n_seq == 4
    n_far = 3 if paired else 0
    me = lax.axis_index("tp").astype(jnp.int32)
    seq_at = lax.axis_index("seq").astype(jnp.int32)
    meta = jnp.concatenate([tp_order(me), seq_order(seq_at), jnp.stack([me, seq_at])])
    sizes = dict(n_tp=n_tp, n_seq=n_seq)
    weights = conv_weight.transpose(0, 2, 1, 3).reshape(LAYERS, 3 * ch, channels)
    conv_flops = 6 * ch * channels * width

    def call(kernel, inputs, shapes, scratch=(), hbm_in=(), hbm_out=(), estimate=None, mib=24, **kw):
        return pl.pallas_call(
            kernel,
            out_shape=list(shapes),
            in_specs=[SMEM] + [HBM if i in hbm_in else VMEM for i in range(len(inputs))],
            out_specs=[HBM if i in hbm_out else VMEM for i in range(len(shapes))],
            scratch_shapes=list(scratch),
            compiler_params=params(mib),
            cost_estimate=estimate,
            **kw,
        )(meta, *inputs)

    def array(shape, dtype=BF16):
        return jax.ShapeDtypeStruct(shape, dtype)

    high = lax.reduce_precision(tower_grad, 8, 7)
    low = tower_grad - high

    def edge(lanes):
        return jnp.concatenate(
            [
                sequence_in[:, lanes],
                high[:, lanes].astype(BF16),
                low[:, lanes].astype(BF16),
                jnp.zeros((ch, EDGE), BF16),
            ],
            axis=1,
        )

    left, right = edge(slice(0, EDGE)), edge(slice(length - EDGE, length))
    even = seq_at % 2 == 0
    first = lax.ppermute(jnp.where(even, right, left), "seq", [(i, i ^ 1) for i in range(n_seq)])
    pairs = [(i, i + 1) for i in range(1, n_seq - 1, 2)]
    second = lax.ppermute(jnp.where(even, left, right), "seq", pairs + [(j, i) for i, j in pairs])
    gain_cols = jnp.pad(norm_gain.T, ((0, 0), (0, 128 - LAYERS)))
    halo, window = call(
        functools.partial(halo_kernel, **sizes),
        [tower_grad, first, second, gain_cols],
        [array((ch, 128)), array((ch, width), F32)],
        name="halo",
    )

    def forward(layer, own, pieces, extra, shapes):
        inputs = [weights, *own, *pieces, *extra]
        return call(
            functools.partial(forward_kernel, layer=layer, length=length, **sizes),
            inputs,
            shapes,
            scratch=[
                pltpu.VMEM((n_tp, ch, width), BF16),
                pltpu.VMEM((3 * ch, channels), BF16),
                pltpu.SemaphoreType.DMA,
            ],
            hbm_in=(0,),
            estimate=cost(conv_flops, 4 * channels * width, channels * width),
            name="forward",
        )

    def slope(layer, pieces, inverse):
        wide = length if layer == 0 else width
        return call(
            functools.partial(slope_kernel, layer=layer, n_tp=n_tp),
            [gains, inverse, *pieces],
            [array((n_tp, ch, wide))],
            scratch=[pltpu.VMEM((n_tp, ch, wide), BF16), pltpu.SemaphoreType.DMA((n_tp,))],
            hbm_out=(0,),
            estimate=cost(40 * channels * wide, 4 * channels * wide, channels * wide),
            name="slope",
        )[0]

    blocks0 = gather_tp(sequence_in) + gather_tp(halo)
    state1, inverse0, hidden0, gains = forward(
        0,
        [sequence_in, halo],
        blocks0,
        [],
        [array((ch, width)), array((8, width), F32), array((ch, length)), array((n_tp, ch, 128), F32)],
    )

    record = jnp.stack(
        [
            (donor_offset + seq_at * length).astype(F32),
            (acceptor_owner[:, 0] * length + acceptor_offset).astype(F32),
            tissue.astype(F32),
            score_grad,
        ]
        + [jnp.zeros((share,), F32)] * 4
    )
    table = lax.dynamic_slice_in_dim(tissue_scale, me * ch, ch, 1).T
    table = jnp.pad(table, ((0, 0), (0, -table.shape[1] % 128)))
    records, rows = call(
        functools.partial(lookup_kernel, **sizes),
        [table, *gather_seq(record)],
        [array((8, count), F32), array((ch, count), F32)],
        name="lookup",
    )

    blocks1 = gather_tp(state1)
    slope0 = slope(0, blocks0, inverse0)
    blocks1, (records, rows, slope0) = tie(blocks1, [records, rows, slope0])
    state2, inverse1, hidden = forward(
        1, [state1], blocks1, [gains, hidden0], [array((ch, width)), array((8, width), F32), array((2 * ch, length))]
    )
    every = lax.all_gather(hidden, ("seq", "tp"), axis=0).reshape(n_seq, n_tp, 2, ch, length)

    blocks2 = gather_tp(state2)
    slope1 = slope(1, blocks1, inverse1)
    blocks2, (slope1,) = tie(blocks2, [slope1])
    half = array((n_tp // 2, ch, length))
    state3, inverse2, *halves = forward(
        2,
        [state2],
        blocks2,
        [gains],
        [array((ch, length)), array((8, width), F32)] + ([half, half] if swapped else [array((ch, length))]),
    )
    slope2 = slope(2, blocks2, inverse2)

    def product_shapes(layer):
        wide = length if layer == 0 else width
        if paired:
            return [array((n_tp // 2, ch, wide)), array((n_tp // 2 * ch + 16, wide))]
        return [array((n_tp, ch, wide)), array((8, wide), F32)]

    def scratch(layer):
        wide = length if layer == 0 else width
        return [
            pltpu.VMEM((3 * ch, channels), BF16),
            pltpu.VMEM((3 * ch, wide), BF16),
            pltpu.VMEM((n_tp, ch, wide), BF16),
        ]

    def reduce_tp(products):
        if not paired:
            whole, extra = products
            own = lax.psum_scatter(whole.reshape(channels, -1), "tp", scatter_dimension=0, tiled=True)
            return [jnp.concatenate([own.astype(F32), lax.psum(extra, "tp")], axis=0)]
        keep, send = products
        wide = keep.shape[2]
        got = swap(send, "tp", 1)
        far = array((ch + 16, wide))
        own, *far = pl.pallas_call(
            pair_kernel,
            out_shape=[array((ch + 8, wide), F32), far, far, far],
            in_specs=[VMEM] * 3,
            out_specs=[VMEM] * 4,
            compiler_params=params(),
            name="pair",
        )(keep, send, got)
        return [own] + [swap(v, "tp", 2 * r + 2) for r, v in enumerate(far)]

    pieces = gather_seq(state3)
    pieces, halves = tie(pieces, halves)
    upstream, grad2, *products = call(
        functools.partial(junction_kernel, root=math.sqrt(channels), **sizes),
        [weights, slope2, window, records, rows, *pieces],
        [array((ch, width), F32), array((ch, length))] + product_shapes(2),
        scratch=scratch(2) + [pltpu.VMEM((ch, count), F32), pltpu.SemaphoreType.DMA((2,))],
        hbm_in=(0, 1),
        estimate=cost(4 * conv_flops, 4 * channels * width),
        mib=32,
        name="junction",
    )

    if swapped:
        one, two = swap(halves[0], "seq", 1), swap(halves[0], "seq", 2)
    else:
        last = [lax.all_gather(halves[0], ("seq", "tp"), axis=0).reshape(n_seq, n_tp, ch, length)]

    def backward(layer, sums, upstream, state, inverse, slopes):
        wide = length if layer == 0 else width
        inputs = [*sums, upstream, state, inverse, gain_cols]
        shapes = [array((ch, wide), F32), array((ch, 128), F32)]
        extra, hbm = [], ()
        if layer > 0:
            inputs = [weights, slopes, *inputs]
            hbm = (0, 1)
            shapes.append(array((ch, length)))
            if layer == LAYERS - 1:
                shapes.append(array((8, width), F32))
            shapes += product_shapes(layer - 1)
            extra = scratch(layer - 1) + [pltpu.SemaphoreType.DMA((2,))]
        return call(
            functools.partial(backward_kernel, layer=layer, n_far=n_far, length=length, **sizes),
            inputs,
            shapes,
            scratch=extra,
            hbm_in=hbm,
            estimate=cost(conv_flops, 4 * channels * width),
            name="backward",
        )

    def weigh(layer, grads, sources, before):
        inputs = [*grads, *sources, *before]
        flops = 6 * ch * channels * total
        return call(
            functools.partial(weight_kernel, layer=layer, swapped=len(sources) > 1, **sizes),
            inputs,
            [array((LAYERS, 3, ch, channels), F32)],
            scratch=[
                pltpu.VMEM((ch, total), BF16),
                pltpu.VMEM((3 * ch, total), BF16),
                pltpu.VMEM((2, n_seq, CHUNK // ch, ch, length), BF16),
                pltpu.VMEM((2, 3, ch, CHUNK), F32),
                pltpu.SemaphoreType.DMA((2, 2 * n_seq)),
                pltpu.SemaphoreType.DMA((2,)),
            ],
            hbm_in=range(n_seq, len(inputs)),
            hbm_out=(0,),
            estimate=cost(2 * flops, 2 * channels * total),
            input_output_aliases={len(inputs): 0} if before else {},
            name="weight",
        )[0]

    sums = reduce_tp(products)
    if swapped:
        sums, (one, two) = tie(sums, [one, two])
        three = swap(two, "seq", 1)
    upstream, part2, grad1, score_rows, *products = backward(2, sums, upstream, state2, inverse2, slope1)
    scores = score_rows[1, :share]

    grads = gather_seq(grad2)
    sums = reduce_tp(products)
    if swapped:
        mine = [halves[0], one, two, three]
        near = [halves[1]] + [swap(v, "tp", 1) for v in mine[1:]]
        last = [v for pair in zip(mine, near) for v in pair]
    sums, got = tie(sums, grads + last)
    grads, last = got[:n_seq], got[n_seq:]
    upstream, part1, grad0, *products = backward(1, sums, upstream, state1, inverse1, slope0)

    weight_grad = weigh(2, grads, last, [])
    grads = gather_seq(grad1)
    sums = reduce_tp(products)
    sums, got = tie(sums, grads + [weight_grad, every])
    grads, weight_grad, every = got[:n_seq], got[n_seq], got[n_seq + 1]
    input_grad, part0 = backward(0, sums, upstream, sequence_in, inverse0, None)

    weight_grad = weigh(1, grads, [every], [weight_grad])
    columns = jnp.pad(jnp.stack([p[:, 0] for p in (part0, part1, part2)]), ((0, 8 - LAYERS), (0, 0)))
    pieces = gather_seq(columns)
    if len(pieces) == 4:
        gain_grad = (pieces[0] + pieces[1]) + (pieces[2] + pieces[3])
    else:
        gain_grad = sum(pieces)
    weight_grad = weigh(0, gather_seq(grad0), [every], [weight_grad])
    return (scores, input_grad, weight_grad.transpose(0, 2, 1, 3), gain_grad[:LAYERS])


def solution(mesh):
    return jax.shard_map(
        local,
        mesh=mesh,
        in_specs=(
            P("tp", "seq"),
            P(None, "tp", None, None),
            P(None, "tp"),
            P(),
            P("seq"),
            P("seq", None),
            P("seq"),
            P("seq"),
            P("tp", "seq"),
            P("seq"),
        ),
        out_specs=(P("seq"), P("tp", "seq"), P(None, "tp", None, None), P(None, "tp")),
        check_vma=False,
    )
```

```python
import functools
import math

import jax
import jax.numpy as jnp
from jax import lax
from jax.experimental import pallas as pl
from jax.experimental.pallas import tpu as pltpu
from jax.sharding import PartitionSpec as P

LAYERS = 3
EPSILON = 1e-06
EDGE = 64
SPARE = 56
CHUNK = 384
ROWS = 16
K0 = math.sqrt(2.0 / math.pi)
K1 = K0 * 0.044715
F32 = jnp.float32
BF16 = jnp.bfloat16

VMEM = pl.BlockSpec(memory_space=pltpu.VMEM)
SMEM = pl.BlockSpec(memory_space=pltpu.SMEM)
HBM = pl.BlockSpec(memory_space=pltpu.HBM)

TP = ("pair", "side")


def params(mib=24):
    return pltpu.CompilerParams(vmem_limit_bytes=mib * 1024 * 1024)


def cost(flops, nbytes, special=0):
    return pl.CostEstimate(flops=flops, bytes_accessed=nbytes, transcendentals=special)


def tie(first, then):
    out = lax.optimization_barrier((tuple(first), tuple(then)))
    return list(out[0]), list(out[1])


def reach_of(layer):
    return 2 ** (layer + 3)


def size_of(axis):
    return math.prod(lax.axis_size(name) for name in axis) if isinstance(axis, tuple) else lax.axis_size(axis)


def swap(x, axis, mask):
    return lax.ppermute(x, axis, [(i, i ^ mask) for i in range(size_of(axis))])


def gather_tp(x):
    if size_of(TP) == 8:
        far = [x] + [swap(x, TP, m) for m in (2, 4, 6)]
        near = [swap(v, TP, 1) for v in far]
        return [v for pair in zip(far, near) for v in pair]
    whole = lax.all_gather(x, TP, axis=0)
    return [whole[i] for i in range(whole.shape[0])]


def tp_order(me):
    count = size_of(TP)
    steps = jnp.arange(count, dtype=jnp.int32)
    return me ^ steps if count == 8 else steps


def gather_seq(x):
    if size_of("seq") == 4:
        two = swap(x, "seq", 2)
        return [x, swap(x, "seq", 1), two, swap(two, "seq", 1)]
    whole = lax.all_gather(x, "seq", axis=0)
    return [whole[i] for i in range(whole.shape[0])]


def seq_order(me):
    count = size_of("seq")
    steps = jnp.arange(count, dtype=jnp.int32)
    return me ^ steps if count == 4 else steps


def roll(x, shift):
    shift = shift % x.shape[1]
    return x if shift == 0 else pltpu.roll(x, shift, 1)


def position(shape, dim, length):
    at = lax.broadcasted_iota(jnp.int32, shape, dim)
    return jnp.where(at < length + EDGE, at, at - (length + 2 * EDGE))


def in_sequence(seq_at, width, length, total):
    at = position((1, width), 1, length) + seq_at * length
    return (at >= 0) & (at < total)


def record_kernel(donor_ref, owner_ref, accept_ref, tissue_ref, grad_ref, out_ref, *, span):
    row = lax.broadcasted_iota(jnp.int32, (16, out_ref.shape[1]), 0)
    out = jnp.zeros(row.shape, F32)
    values = []
    for x in (donor_ref[...], owner_ref[...] * span + accept_ref[...], tissue_ref[...]):
        values += [(x >> 8).astype(F32), (x & 255).astype(F32)]
    grad = grad_ref[...]
    high = grad.astype(BF16).astype(F32)
    middle = (grad - high).astype(BF16).astype(F32)
    values += [high, middle, grad - high - middle]
    for k, value in enumerate(values):
        value = jnp.concatenate([value, jnp.zeros((1, row.shape[1] - value.shape[1]), F32)], axis=1)
        out = jnp.where(row == k, value, out)
    out_ref[...] = out.astype(BF16)


def edge_kernel(meta, seq_ref, tower_ref, first_ref, second_ref, states, grads, sems, *, n_tp, n_seq):
    ch, length = seq_ref.shape
    copies = []
    for i, start in enumerate((0, length - 128)):
        copies.append(pltpu.make_async_copy(seq_ref.at[:, start : start + 128], states.at[i], sems.at[2 * i]))
        copies.append(pltpu.make_async_copy(tower_ref.at[:, start : start + 128], grads.at[i], sems.at[2 * i + 1]))
    for copy in copies:
        copy.start()
    for copy in copies:
        copy.wait()
    even = lax.rem(meta[n_tp + n_seq + 1], 2) == 0
    low = lax.broadcasted_iota(jnp.int32, (ch, 128), 1) < EDGE

    def pack(state, grad):
        high = grad.astype(BF16).astype(F32)
        return [jnp.where(low, state, roll(high, EDGE)), jnp.where(low, grad - high, 0.0)]

    left = pack(states[0].astype(F32), grads[0])
    right = pack(roll(states[1].astype(F32), EDGE), roll(grads[1], EDGE))
    for i in range(2):
        first_ref[:, i * 128 : (i + 1) * 128] = jnp.where(even, right[i], left[i]).astype(BF16)
        second_ref[:, i * 128 : (i + 1) * 128] = jnp.where(even, left[i], right[i]).astype(BF16)


def window_kernel(
    meta, seq_ref, first_ref, second_ref, gain_ref, state_ref, halo_ref, held, sem, *, n_tp, n_seq
):
    ch, length = held.shape
    copy = pltpu.make_async_copy(seq_ref, held, sem)
    copy.start()
    even = lax.rem(meta[n_tp + n_seq + 1], 2) == 0
    first = first_ref[...].astype(F32)
    second = second_ref[...].astype(F32)
    right = jnp.where(even, first, second)
    left = jnp.where(even, second, first)
    lane = lax.broadcasted_iota(jnp.int32, (ch, 128), 1)
    low = lane < EDGE
    halo = jnp.where(low, right[:, :128], roll(left[:, :128], EDGE))
    gains = gain_ref[...]
    high = gains.astype(BF16).astype(F32)
    rest = gains - high
    middle = rest.astype(BF16).astype(F32)
    for k, part in enumerate((high, middle, rest - middle)):
        for layer in range(LAYERS):
            halo = jnp.where(lane == SPARE + k * LAYERS + layer, part[:, layer : layer + 1], halo)
    state_ref[:, length:] = halo.astype(BF16)
    th = jnp.where(low, roll(right[:, :128], EDGE), left[:, :128])
    tl = jnp.where(low, right[:, 128:], roll(left[:, 128:], EDGE))
    halo_ref[...] = th + tl
    copy.wait()
    state_ref[:, :length] = held[...]


def forward_kernel(meta, w_ref, own_ref, *refs, layer, n_tp, n_seq, length):
    pieces, refs = refs[:n_tp], refs[n_tp:]
    *refs, held, slopes, weights, sems = refs
    if layer == 0:
        state_ref, slope_ref, inverse_ref, hidden_ref, gain_ref = refs
    elif layer < LAYERS - 1:
        gain_ref, state_ref, slope_ref, inverse_ref, hidden_ref = refs
    else:
        gain_ref, digit_ref, state_ref, slope_ref, inverse_ref, hidden_ref = refs
    _, ch, width = held.shape
    wide = slopes.shape[2]
    channels = ch * n_tp
    reach = reach_of(layer)
    me, seq_at = meta[n_tp + n_seq], meta[n_tp + n_seq + 1]
    copy = pltpu.make_async_copy(w_ref.at[layer], weights, sems.at[0])
    copy.start()

    def add_power(j, acc):
        rows = pl.ds(pl.multiple_of(j * ROWS, ROWS), ROWS)
        for piece in pieces:
            x = piece[rows, :].astype(F32)
            sq = x * x
            for i in range(0, ROWS, 8):
                acc = acc + sq[i : i + 8]
        return acc

    acc = lax.fori_loop(0, ch // ROWS, add_power, jnp.zeros((8, width), F32))
    power = jnp.sum(acc, axis=0, keepdims=True) / channels
    inverse = 1.0 / jnp.sqrt(power + EPSILON)
    inverse_ref[...] = jnp.broadcast_to(inverse, (8, width))

    def activate(j, carry):
        rows = pl.ds(pl.multiple_of(j * ROWS, ROWS), ROWS)
        for m, piece in enumerate(pieces):
            at = meta[m]
            x = piece[rows, :].astype(F32)
            if layer == 0:
                halo = x[:, length:]
                cols = [
                    halo[:, SPARE + l : SPARE + l + 1]
                    + (
                        halo[:, SPARE + LAYERS + l : SPARE + LAYERS + l + 1]
                        + halo[:, SPARE + 2 * LAYERS + l : SPARE + 2 * LAYERS + l + 1]
                    )
                    for l in range(LAYERS)
                ]
                lane = lax.broadcasted_iota(jnp.int32, (ROWS, 128), 1)
                gain_ref[at, rows, :] = jnp.where(lane == 0, cols[0], jnp.where(lane == 1, cols[1], cols[2]))
                gain = cols[0]
            else:
                gain = gain_ref[at, rows, layer : layer + 1]
            scaled = x * gain
            pre = scaled * inverse
            sq = pre * pre
            th = jnp.tanh(pre * (K0 + K1 * sq))
            half = 0.5 + 0.5 * th
            hidden = pre * half
            held[at, rows, :] = hidden.astype(BF16)
            slope = half + (hidden - hidden * th) * (K0 + (3.0 * K1) * sq)
            slopes[at, rows, :] = (slope * scaled)[:, :wide].astype(BF16)
        return carry

    lax.fori_loop(0, ch // ROWS, activate, 0)
    leave = pltpu.make_async_copy(slopes, slope_ref, sems.at[1])
    leave.start()
    if layer == 0 and n_tp == 8:
        for i in range(n_tp // 2):
            hidden_ref[i] = held[2 * i + lax.rem(me, 2), :, :length]
    else:
        hidden_ref[...] = held[me, :, :length]
    copy.wait()
    every = held[...].reshape(channels, width)
    total = own_ref[...].astype(F32)
    for tap in range(3):
        part = jnp.dot(weights[tap * ch : (tap + 1) * ch, :], every, preferred_element_type=F32)
        total = total + roll(part, (1 - tap) * reach)
    total = jnp.where(in_sequence(seq_at, width, length, n_seq * length), total, 0.0).astype(BF16)
    if layer < LAYERS - 1:
        state_ref[...] = total
    else:
        state_ref[:ch, :] = total[:, :length]
        state_ref[ch:, :] = digit_ref[...]
    leave.wait()


def send_back(layer, upstream, meta, weights, slopes, taps, grad_ref, out_refs, score, n_tp, n_seq, length):
    ch, width = upstream.shape
    wide = taps.shape[1]
    reach = reach_of(layer)
    me, seq_at = meta[n_tp + n_seq], meta[n_tp + n_seq + 1]
    grad = jnp.where(in_sequence(seq_at, width, length, n_seq * length), upstream, 0.0)
    grad = grad.astype(BF16).astype(F32)
    grad_ref[...] = grad[:, :length].astype(BF16)
    for tap in range(3):
        taps[tap * ch : (tap + 1) * ch, :] = roll(grad, (tap - 1) * reach)[:, :wide].astype(BF16)
    for copy in slopes[1:]:
        copy.wait()
    inner = jnp.zeros((8, wide), F32)
    parts = CHUNK // ch
    chunks = ch * n_tp // CHUNK
    for r in range(chunks):
        at = (me // 2) ^ r if n_tp == 8 else r
        cols = pl.ds(pl.multiple_of(at * CHUNK, 128), CHUNK)
        part = lax.dot_general(weights[:, cols], taps[...], (((0,), (0,)), ((), ())), preferred_element_type=F32)
        for q in range(parts):
            prod = part[q * ch : (q + 1) * ch] * slopes[0][at * parts + q].astype(F32)
            inner = inner + jnp.sum(prod.reshape(ch // 8, 8, wide), axis=0)
        if n_tp == 8:
            keep_ref, send_ref = out_refs
            zero = lax.rem(me, 2) == 0
            keep_ref[r] = jnp.where(zero, part[:ch], part[ch:]).astype(BF16)
            send_ref[r * ch : (r + 1) * ch, :] = jnp.where(zero, part[ch:], part[:ch]).astype(BF16)
        else:
            for q in range(parts):
                out_refs[0][at * parts + q] = part[q * ch : (q + 1) * ch].astype(BF16)
    row = lax.broadcasted_iota(jnp.int32, (8, wide), 0)
    extra = jnp.where(row == 0, jnp.sum(inner, axis=0, keepdims=True), 0.0)
    if score is not None:
        score = jnp.concatenate([score, jnp.zeros((1, wide - score.shape[1]), F32)], axis=1)
        extra = jnp.where(row == 1, score, extra)
    if n_tp == 8:
        out_refs[1][n_tp // 2 * ch :, :] = split_rows(extra)
    else:
        out_refs[1][...] = extra


def split_rows(x):
    high = x.astype(BF16).astype(F32)
    return jnp.concatenate([high, x - high], axis=0).astype(BF16)


def join_rows(x):
    x = x.astype(F32)
    return x[:8] + x[8:]


def fetch(layer, w_ref, slope_ref, weights, slopes, sems):
    copies = [
        pltpu.make_async_copy(w_ref.at[layer], weights, sems.at[0]),
        pltpu.make_async_copy(slope_ref, slopes, sems.at[1]),
    ]
    for copy in copies:
        copy.start()
    return [slopes] + copies


def junction_kernel(meta, w_ref, slope_ref, tower_ref, halo_ref, table_ref, *refs, n_tp, n_seq, share, root):
    pieces, refs = refs[:n_seq], refs[n_seq:]
    up_ref, grad_ref, *refs = refs
    *out_refs, weights, taps, slopes, donors, rec_ref, tower, sems = refs
    ch, length = tower.shape
    width = length + 2 * EDGE
    count = share * n_seq
    tower_copy = pltpu.make_async_copy(tower_ref, tower, sems.at[2])
    tower_copy.start()
    seq_at = meta[n_tp + n_seq + 1]
    slopes = fetch(LAYERS - 1, w_ref, slope_ref, weights, slopes, sems)
    for m in range(n_seq):
        at = meta[n_tp + m]
        digits = pieces[m][ch:, :share].astype(F32)
        row = lax.broadcasted_iota(jnp.int32, (8, share), 0)
        first = (digits[0:1] * 256.0 + digits[1:2]) + (at * length).astype(F32)
        second = digits[2:3] * 256.0 + digits[3:4]
        third = digits[4:5] * 256.0 + digits[5:6]
        fourth = digits[6:7] + (digits[7:8] + digits[8:9])
        record = jnp.where(row == 0, first, jnp.where(row == 1, second, jnp.where(row == 2, third, fourth)))
        rec_ref[:, pl.ds(pl.multiple_of(at * share, 128), share)] = record
    table = table_ref[...]
    high = table.astype(BF16)
    rest = table - high.astype(F32)
    middle = rest.astype(BF16)
    last = (rest - middle.astype(F32)).astype(BF16)
    hit = lax.broadcasted_iota(jnp.int32, (table.shape[0], count), 0) == rec_ref[2:3, :].astype(jnp.int32)
    hit = jnp.where(hit, 1.0, 0.0).astype(BF16)
    rows = sum(
        lax.dot_general(part, hit, (((0,), (0,)), ((), ())), preferred_element_type=F32)
        for part in (last, middle, high)
    )
    donor = rec_ref[0:1, :].astype(jnp.int32)
    accept = rec_ref[1:2, :].astype(jnp.int32)
    weight = rec_ref[3:4, :] / root
    place = lax.broadcasted_iota(jnp.int32, (length, count), 0)
    accepts = jnp.zeros((ch, count), F32)
    for m in range(n_seq):
        at = meta[n_tp + m]
        cols = pl.ds(pl.multiple_of(at * share, 128), share)
        block = pieces[m][:ch, :]
        mine = rec_ref[0:1, cols].astype(jnp.int32) - at * length
        hit = lax.broadcasted_iota(jnp.int32, (length, share), 0) == mine
        donors[:, cols] = jnp.dot(block, jnp.where(hit, 1.0, 0.0).astype(BF16), preferred_element_type=F32)
        hit = place == accept - at * length
        accepts = accepts + jnp.dot(block, jnp.where(hit, 1.0, 0.0).astype(BF16), preferred_element_type=F32)
    product = donors[...] * accepts * rows
    scored = jnp.sum(product, axis=0, keepdims=True) / root
    score = jnp.zeros((1, share), F32)
    for m in range(n_seq):
        score = jnp.where(seq_at == m, scored[:, m * share : (m + 1) * share], score)
    scale = rows * weight
    tower_copy.wait()
    upstream = jnp.concatenate([tower[...], halo_ref[...]], axis=1)
    spot = position((width, count), 0, length) + seq_at * length
    for values, where in ((accepts * scale, donor), (donors[...] * scale, accept)):
        high = values.astype(BF16)
        low = (values - high.astype(F32)).astype(BF16)
        hit = jnp.where(spot == where, 1.0, 0.0).astype(BF16)
        both = lax.dot_general(
            jnp.concatenate([high, low], axis=0), hit, (((1,), (1,)), ((), ())), preferred_element_type=F32
        )
        upstream = upstream + (both[:ch] + both[ch:])
    up_ref[...] = upstream
    send_back(LAYERS - 1, upstream, meta, weights, slopes, taps, grad_ref, out_refs, score, n_tp, n_seq, length)


def pair_kernel(keep_ref, send_ref, got_ref, own_ref, *far_refs):
    count, ch, width = keep_ref.shape
    extra = join_rows(send_ref[count * ch :, :]) + join_rows(got_ref[count * ch :, :])
    split = split_rows(extra)
    for r in range(count):
        total = keep_ref[r].astype(F32) + got_ref[r * ch : (r + 1) * ch, :].astype(F32)
        if r == 0:
            own_ref[:ch, :] = total
            own_ref[ch:, :] = join_rows(split)
        else:
            far_refs[r - 1][:ch, :] = total.astype(BF16)
            far_refs[r - 1][ch:, :] = split


def backward_kernel(meta, *refs, layer, n_far, n_tp, n_seq, length):
    last = layer == 0
    if last:
        slopes = None
    else:
        w_ref, slope_ref, *refs = refs
        *refs, weights, taps, slopes, sems = refs
        slopes = fetch(layer - 1, w_ref, slope_ref, weights, slopes, sems)
    own_ref, refs = refs[0], refs[1:]
    far, refs = refs[:n_far], refs[n_far:]
    up_ref, state_ref, inverse_ref, gain_ref, *refs = refs
    out_ref, part_ref, *refs = refs
    if not last:
        grad_ref, *out_refs = refs
        if layer == LAYERS - 1:
            score_ref, *out_refs = out_refs
    ch, width = state_ref.shape
    channels = ch * n_tp
    sums = [own_ref[ch:, :]] + [join_rows(f[ch:, :]) for f in far]
    extra = (sums[0] + sums[1]) + (sums[2] + sums[3]) if n_far else sums[0]
    inner = extra[0:1, :]
    if layer == LAYERS - 1:
        score_ref[...] = extra
    inverse = inverse_ref[0:1, :width]
    gain = gain_ref[:, layer : layer + 1]
    back = own_ref[:ch, :]
    for f in far:
        back = back + f[:ch, :].astype(F32)
    x = state_ref[...].astype(F32)
    pre = x * gain * inverse
    sq = pre * pre
    th = jnp.tanh(pre * (K0 + K1 * sq))
    half = 0.5 + 0.5 * th
    back = back * (half + (pre * half) * (1.0 - th) * (K0 + (3.0 * K1) * sq))
    mine = back * x * inverse
    part = jnp.sum(mine[:, :length], axis=1, keepdims=True)
    part_ref[...] = jnp.broadcast_to(part, part_ref.shape)
    upstream = up_ref[:, :width] + (inverse * gain) * back - x * (inverse * inverse * inverse * inner / channels)
    out_ref[...] = upstream
    if not last:
        send_back(layer - 1, upstream, meta, weights, slopes, taps, grad_ref, out_refs, None, n_tp, n_seq, length)


def weight_kernel(meta, *refs, layer, path, n_tp, n_seq):
    pieces, refs = refs[:n_seq], refs[n_seq:]
    *sources, out_ref, whole, taps, held, done, in_sems, out_sems = refs
    ch, length = pieces[0].shape
    reach = reach_of(layer)
    total = n_seq * length
    parts = CHUNK // ch
    chunks = ch * n_tp // CHUNK
    me = meta[n_tp + n_seq]
    core = lax.rem(me, 2)

    def chunk_at(r):
        return r if path == "whole" else (me // 2) ^ r

    def lanes(m):
        return pl.ds(pl.multiple_of(meta[n_tp + m] * length, 128), length)

    def arrive(r):
        copies = []

        def add(source, side, where):
            copies.append(
                pltpu.make_async_copy(source, held.at[r, side, :, where], in_sems.at[r, len(copies)])
            )

        if path == "whole":
            for s in range(n_seq):
                for q in range(parts):
                    add(sources[0].at[s, r * parts + q], q, pl.ds(s * length, length))
        else:
            for s in range(n_seq):
                for q in range(2):
                    add(sources[q].at[s, chunk_at(r)], core if q == 0 else 1 - core, pl.ds(s * length, length))
        return copies

    def leave(r):
        cols = pl.ds(pl.multiple_of(chunk_at(r) * CHUNK, 128), CHUNK)
        return pltpu.make_async_copy(done.at[r % 2], out_ref.at[layer, :, :, cols], out_sems.at[r % 2])

    for r in range(chunks):
        for copy in arrive(r):
            copy.start()
    for m in range(n_seq):
        whole[:, lanes(m)] = pieces[m][...]
    grad = whole[...].astype(F32)
    lane = lax.broadcasted_iota(jnp.int32, (1, total), 1)
    taps[:ch, :] = jnp.where(lane < total - reach, roll(grad, -reach), 0.0).astype(BF16)
    taps[ch : 2 * ch, :] = whole[...]
    taps[2 * ch :, :] = jnp.where(lane >= reach, roll(grad, reach), 0.0).astype(BF16)
    for r in range(chunks):
        for copy in arrive(r):
            copy.wait()
        if r >= 2:
            leave(r - 2).wait()
        product = lax.dot_general(
            taps[...], held[r].reshape(CHUNK, total), (((1,), (1,)), ((), ())), preferred_element_type=F32
        )
        done[r % 2] = product.reshape(3, ch, CHUNK)
        leave(r).start()
    for r in range(max(0, chunks - 2), chunks):
        leave(r).wait()


def local(
    sequence_in,
    conv_weight,
    norm_gain,
    tissue_scale,
    donor_offset,
    acceptor_owner,
    acceptor_offset,
    tissue,
    tower_grad,
    score_grad,
):
    ch, length = sequence_in.shape
    n_tp, n_seq = size_of(TP), size_of("seq")
    channels, total = ch * n_tp, length * n_seq
    width = length + 2 * EDGE
    share = donor_offset.shape[0]
    count = share * n_seq
    paired = n_tp == 8
    n_far = 3 if paired else 0
    me = lax.axis_index(TP).astype(jnp.int32)
    seq_at = lax.axis_index("seq").astype(jnp.int32)
    meta = jnp.concatenate([tp_order(me), seq_order(seq_at), jnp.stack([me, seq_at])])
    sizes = dict(n_tp=n_tp, n_seq=n_seq)
    weights = conv_weight.transpose(0, 2, 1, 3).reshape(LAYERS, 3 * ch, channels)
    conv_flops = 6 * ch * channels * width

    def call(kernel, inputs, shapes, scratch=(), hbm_in=(), hbm_out=(), estimate=None, mib=24, **kw):
        inputs = [pltpu.with_memory_space_constraint(x, pltpu.HBM) if i in hbm_in else x for i, x in enumerate(inputs)]
        return pl.pallas_call(
            kernel,
            out_shape=[pltpu.HBM(x.shape, x.dtype) if i in hbm_out else x for i, x in enumerate(shapes)],
            in_specs=[SMEM] + [HBM if i in hbm_in else VMEM for i in range(len(inputs))],
            out_specs=[HBM if i in hbm_out else VMEM for i in range(len(shapes))],
            scratch_shapes=list(scratch),
            compiler_params=params(mib),
            cost_estimate=estimate,
            **kw,
        )(meta, *inputs)

    def array(shape, dtype=BF16):
        return jax.ShapeDtypeStruct(shape, dtype)

    edges = array((ch, 256))
    first, second = call(
        functools.partial(edge_kernel, **sizes),
        [sequence_in, tower_grad],
        [edges, edges],
        scratch=[pltpu.VMEM((2, ch, 128), BF16), pltpu.VMEM((2, ch, 128), F32), pltpu.SemaphoreType.DMA((4,))],
        hbm_in=(0, 1),
        name="edge",
    )
    pairs = [(i, i + 1) for i in range(1, n_seq - 1, 2)]
    first = lax.ppermute(first, "seq", [(i, i ^ 1) for i in range(n_seq)])
    second = lax.ppermute(second, "seq", pairs + [(j, i) for i, j in pairs])
    gain_cols = jnp.pad(norm_gain.T, ((0, 0), (0, 128 - LAYERS)))
    state, halo_grad = call(
        functools.partial(window_kernel, **sizes),
        [sequence_in, first, second, gain_cols],
        [array((ch, width)), array((ch, 128), F32)],
        scratch=[pltpu.VMEM((ch, length), BF16), pltpu.SemaphoreType.DMA],
        hbm_in=(0,),
        name="window",
    )

    record = pl.pallas_call(
        functools.partial(record_kernel, span=length),
        out_shape=array((16, length)),
        in_specs=[VMEM] * 5,
        out_specs=VMEM,
        compiler_params=params(),
        name="record",
    )(*(x.reshape(1, share) for x in (donor_offset, acceptor_owner, acceptor_offset, tissue, score_grad)))
    table = lax.dynamic_slice_in_dim(tissue_scale, me * ch, ch, 1)
    table = jnp.pad(table, ((0, -table.shape[0] % 128), (0, 0)))

    def forward(layer, own, extra):
        wide = length if layer == 0 else width
        final = layer == LAYERS - 1
        shapes = [
            array((ch + 16, length) if final else (ch, width)),
            array((n_tp, ch, wide)),
            array((8, width), F32),
            array((n_tp // 2, ch, length) if layer == 0 and paired else (ch, length)),
        ]
        if layer == 0:
            shapes.append(array((n_tp, ch, 128), F32))
        return call(
            functools.partial(forward_kernel, layer=layer, length=length, **sizes),
            [weights, own, *gather_tp(own), *extra],
            shapes,
            scratch=[
                pltpu.VMEM((n_tp, ch, width), BF16),
                pltpu.VMEM((n_tp, ch, wide), BF16),
                pltpu.VMEM((3 * ch, channels), BF16),
                pltpu.SemaphoreType.DMA((2,)),
            ],
            hbm_in=(0,),
            hbm_out=(1,),
            estimate=cost(conv_flops, 4 * channels * width, channels * width),
            name="forward",
        )

    state1, slope0, inverse0, hidden0, gains = forward(0, state, [])
    state2, slope1, inverse1, hidden1 = forward(1, state1, [gains])
    state3, slope2, inverse2, hidden2 = forward(2, state2, [gains, record])
    slopes = [slope0, slope1, slope2]
    stored = [(sequence_in, inverse0), (state1, inverse1), (state2, inverse2)]
    planned = paired and n_seq == 4

    if planned:
        pieces = gather_seq(state3)
        first = lax.all_gather(hidden0, "seq", axis=0)
        rest = jnp.concatenate([hidden1, hidden2], axis=0)
        rest = lax.all_gather(rest, ("seq", "pair"), axis=0).reshape(n_seq, n_tp // 2, 2, ch, length)
    else:
        pieces = gather_seq(state3)
        everything = [
            [lax.all_gather(h, ("seq",) + TP, axis=0).reshape(n_seq, n_tp, ch, length)]
            for h in (hidden0, hidden1, hidden2)
        ]

    def product_shapes(layer):
        wide = length if layer == 0 else width
        if paired:
            return [array((n_tp // 2, ch, wide)), array((n_tp // 2 * ch + 16, wide))]
        return [array((n_tp, ch, wide)), array((8, wide), F32)]

    def scratch(layer):
        wide = length if layer == 0 else width
        return [
            pltpu.VMEM((3 * ch, channels), BF16),
            pltpu.VMEM((3 * ch, wide), BF16),
            pltpu.VMEM((n_tp, ch, wide), BF16),
        ]

    def reduce_tp(products):
        if not paired:
            whole, extra = products
            own = lax.psum_scatter(whole.reshape(channels, -1), TP, scatter_dimension=0, tiled=True)
            return [jnp.concatenate([own.astype(F32), lax.psum(extra, TP)], axis=0)]
        keep, send = products
        wide = keep.shape[2]
        got = swap(send, TP, 1)
        far = array((ch + 16, wide))
        own, *far = pl.pallas_call(
            pair_kernel,
            out_shape=[array((ch + 8, wide), F32), far, far, far],
            in_specs=[VMEM] * 3,
            out_specs=[VMEM] * 4,
            compiler_params=params(),
            name="pair",
        )(keep, send, got)
        return [own] + [swap(v, TP, 2 * r + 2) for r, v in enumerate(far)]

    upstream, grad2, *products = call(
        functools.partial(junction_kernel, share=share, root=math.sqrt(channels), **sizes),
        [weights, slopes[2], tower_grad, halo_grad, table, *pieces],
        [array((ch, width), F32), array((ch, length))] + product_shapes(2),
        scratch=scratch(2)
        + [
            pltpu.VMEM((ch, count), F32),
            pltpu.VMEM((8, count), F32),
            pltpu.VMEM((ch, length), F32),
            pltpu.SemaphoreType.DMA((3,)),
        ],
        hbm_in=(0, 1, 2),
        estimate=cost(4 * conv_flops, 4 * channels * width),
        mib=32,
        name="junction",
    )

    def backward(layer, sums, upstream):
        state, inverse = stored[layer]
        wide = length if layer == 0 else width
        inputs = [*sums, upstream, state, inverse, gain_cols]
        shapes = [array((ch, wide), F32), array((ch, 128), F32)]
        extra, hbm = [], ()
        if layer > 0:
            inputs = [weights, slopes[layer - 1], *inputs]
            hbm = (0, 1)
            shapes.append(array((ch, length)))
            if layer == LAYERS - 1:
                shapes.append(array((8, width), F32))
            shapes += product_shapes(layer - 1)
            extra = scratch(layer - 1) + [pltpu.SemaphoreType.DMA((2,))]
        return call(
            functools.partial(backward_kernel, layer=layer, n_far=n_far, length=length, **sizes),
            inputs,
            shapes,
            scratch=extra,
            hbm_in=hbm,
            estimate=cost(conv_flops, 4 * channels * width),
            name="backward",
        )

    def weigh(layer, path, grads, sources, before):
        inputs = [*grads, *sources, *before]
        return call(
            functools.partial(weight_kernel, layer=layer, path=path, **sizes),
            inputs,
            [array((LAYERS, 3, ch, channels), F32)],
            scratch=[
                pltpu.VMEM((ch, total), BF16),
                pltpu.VMEM((3 * ch, total), BF16),
                pltpu.VMEM((channels // CHUNK, CHUNK // ch, ch, total), BF16),
                pltpu.VMEM((2, 3, ch, CHUNK), F32),
                pltpu.SemaphoreType.DMA((channels // CHUNK, n_seq * (CHUNK // ch))),
                pltpu.SemaphoreType.DMA((2,)),
            ],
            hbm_in=range(n_seq, len(inputs)),
            hbm_out=(0,),
            estimate=cost(6 * ch * channels * total, 2 * channels * total),
            mib=32,
            input_output_aliases={len(inputs): 0} if before else {},
            name="weight",
        )[0]

    sums = reduce_tp(products)
    upstream, part2, grad1, score_rows, *products = backward(2, sums, upstream)
    scores = score_rows[1, :share]

    grads2 = gather_seq(grad2)
    sums = reduce_tp(products)
    if planned:
        near = swap(first, TP, 1)
        sums, (first, near) = tie(sums, [first, near])
    upstream, part1, grad0, *products = backward(1, sums, upstream)

    grads1 = gather_seq(grad1)
    sums = reduce_tp(products)
    if planned:
        sums, grads2 = tie(sums, grads2)
    input_grad, part0 = backward(0, sums, upstream)

    columns = jnp.pad(jnp.stack([p[:, 0] for p in (part0, part1, part2)]), ((0, 8 - LAYERS), (0, 0)))
    pieces = gather_seq(columns)
    if len(pieces) == 4:
        gain_grad = (pieces[0] + pieces[1]) + (pieces[2] + pieces[3])
    else:
        gain_grad = sum(pieces)

    grads0 = gather_seq(grad0)
    if planned:
        weight_grad = weigh(0, "pair", grads0, [first, near], [])
        (rest,), got = tie([rest], [weight_grad, gain_grad, *grads1])
        weight_grad, gain_grad, grads1 = got[0], got[1], got[2:]
        for layer, grads in ((1, grads1), (2, grads2)):
            mine = rest[:, :, layer - 1]
            weight_grad = weigh(layer, "pair", grads, [mine, swap(mine, TP, 1)], [weight_grad])
    else:
        weight_grad = weigh(0, "whole", grads0, everything[0], [])
        weight_grad = weigh(1, "whole", grads1, everything[1], [weight_grad])
        weight_grad = weigh(2, "whole", grads2, everything[2], [weight_grad])
    return (scores, input_grad, weight_grad.transpose(0, 2, 1, 3), gain_grad[:LAYERS])


def solution(mesh):
    tp = mesh.shape["tp"]
    pairs = jax.sharding.Mesh(mesh.devices.reshape(mesh.shape["seq"], tp // 2, 2), ("seq",) + TP)
    return jax.shard_map(
        local,
        mesh=pairs,
        in_specs=(
            P(TP, "seq"),
            P(None, TP, None, None),
            P(None, TP),
            P(),
            P("seq"),
            P("seq", None),
            P("seq"),
            P("seq"),
            P(TP, "seq"),
            P("seq"),
        ),
        out_specs=(P("seq"), P(TP, "seq"), P(None, TP, None, None), P(None, TP)),
        check_vma=False,
    )
```

```python
import functools
import math

import jax
import jax.numpy as jnp
from jax import lax
from jax.experimental import pallas as pl
from jax.experimental.pallas import tpu as pltpu
from jax.sharding import PartitionSpec as P

LAYERS = 3
EPSILON = 1e-06
EDGE = 64
SPARE = 56
CHUNK = 384
ROWS = 16
K0 = math.sqrt(2.0 / math.pi)
K1 = K0 * 0.044715
F32 = jnp.float32
BF16 = jnp.bfloat16

VMEM = pl.BlockSpec(memory_space=pltpu.VMEM)
SMEM = pl.BlockSpec(memory_space=pltpu.SMEM)
HBM = pl.BlockSpec(memory_space=pltpu.HBM)

TP = ("pair", "side")


def params(mib=24):
    return pltpu.CompilerParams(vmem_limit_bytes=mib * 1024 * 1024)


def cost(flops, nbytes, special=0):
    return pl.CostEstimate(flops=flops, bytes_accessed=nbytes, transcendentals=special)


def tie(first, then):
    out = lax.optimization_barrier((tuple(first), tuple(then)))
    return list(out[0]), list(out[1])


def reach_of(layer):
    return 2 ** (layer + 3)


def size_of(axis):
    return math.prod(lax.axis_size(name) for name in axis) if isinstance(axis, tuple) else lax.axis_size(axis)


def swap(x, axis, mask):
    return lax.ppermute(x, axis, [(i, i ^ mask) for i in range(size_of(axis))])


def gather_tp(x):
    if size_of(TP) == 8:
        half = x.shape[0] // 2
        along_x, along_y = swap(x, TP, 2), swap(x, TP, 4)
        corner = [swap(along_x[:half], TP, 4), swap(along_y[half:], TP, 2)]
        far = [x, along_x, along_y, *corner]
        near = [swap(v, TP, 1) for v in far]
        return far + near
    whole = lax.all_gather(x, TP, axis=0)
    return [whole[i] for i in range(whole.shape[0])]


def tp_order(me):
    count = size_of(TP)
    steps = jnp.arange(count, dtype=jnp.int32)
    return me ^ steps if count == 8 else steps


def gather_seq(x):
    if size_of("seq") == 4:
        one, two = swap(x, "seq", 1), swap(x, "seq", 2)
        return [x, one, two, swap(two, "seq", 1)]
    whole = lax.all_gather(x, "seq", axis=0)
    return [whole[i] for i in range(whole.shape[0])]


def seq_order(me):
    count = size_of("seq")
    steps = jnp.arange(count, dtype=jnp.int32)
    return me ^ steps if count == 4 else steps


def roll(x, shift):
    shift = shift % x.shape[1]
    return x if shift == 0 else pltpu.roll(x, shift, 1)


def position(shape, dim, length):
    at = lax.broadcasted_iota(jnp.int32, shape, dim)
    return jnp.where(at < length + EDGE, at, at - (length + 2 * EDGE))


def in_sequence(seq_at, width, length, total):
    at = position((1, width), 1, length) + seq_at * length
    return (at >= 0) & (at < total)


def stack_kernel(*refs):
    *pieces, out_ref, sems = refs
    rows = out_ref.shape[0] // len(pieces)
    copies = [
        pltpu.make_async_copy(piece.at[:rows], out_ref.at[i * rows : (i + 1) * rows], sems.at[i])
        for i, piece in enumerate(pieces)
    ]
    for copy in copies:
        copy.start()
    for copy in copies:
        copy.wait()


def record_kernel(donor_ref, owner_ref, accept_ref, tissue_ref, grad_ref, out_ref, *, span):
    row = lax.broadcasted_iota(jnp.int32, (16, out_ref.shape[1]), 0)
    out = jnp.zeros(row.shape, F32)
    values = []
    for x in (donor_ref[...], owner_ref[...] * span + accept_ref[...], tissue_ref[...]):
        values += [(x >> 8).astype(F32), (x & 255).astype(F32)]
    grad = grad_ref[...]
    high = grad.astype(BF16).astype(F32)
    middle = (grad - high).astype(BF16).astype(F32)
    values += [high, middle, grad - high - middle]
    for k, value in enumerate(values):
        value = jnp.concatenate([value, jnp.zeros((1, row.shape[1] - value.shape[1]), F32)], axis=1)
        out = jnp.where(row == k, value, out)
    out_ref[...] = out.astype(BF16)


def edge_kernel(meta, seq_ref, tower_ref, first_ref, second_ref, states, grads, sems, *, n_tp, n_seq):
    ch, length = seq_ref.shape
    copies = []
    for i, start in enumerate((0, length - 128)):
        copies.append(pltpu.make_async_copy(seq_ref.at[:, start : start + 128], states.at[i], sems.at[2 * i]))
        copies.append(pltpu.make_async_copy(tower_ref.at[:, start : start + 128], grads.at[i], sems.at[2 * i + 1]))
    for copy in copies:
        copy.start()
    for copy in copies:
        copy.wait()
    even = lax.rem(meta[n_tp + n_seq + 1], 2) == 0
    low = lax.broadcasted_iota(jnp.int32, (ch, 128), 1) < EDGE

    def pack(state, grad):
        high = grad.astype(BF16).astype(F32)
        return [jnp.where(low, state, roll(high, EDGE)), jnp.where(low, grad - high, 0.0)]

    left = pack(states[0].astype(F32), grads[0])
    right = pack(roll(states[1].astype(F32), EDGE), roll(grads[1], EDGE))
    for i in range(2):
        first_ref[:, i * 128 : (i + 1) * 128] = jnp.where(even, right[i], left[i]).astype(BF16)
        second_ref[:, i * 128 : (i + 1) * 128] = jnp.where(even, left[i], right[i]).astype(BF16)


def window_kernel(
    meta, seq_ref, first_ref, second_ref, gain_ref, state_ref, halo_ref, held, sem, *, n_tp, n_seq
):
    ch, length = held.shape
    copy = pltpu.make_async_copy(seq_ref, held, sem)
    copy.start()
    even = lax.rem(meta[n_tp + n_seq + 1], 2) == 0
    first = first_ref[...].astype(F32)
    second = second_ref[...].astype(F32)
    right = jnp.where(even, first, second)
    left = jnp.where(even, second, first)
    lane = lax.broadcasted_iota(jnp.int32, (ch, 128), 1)
    low = lane < EDGE
    halo = jnp.where(low, right[:, :128], roll(left[:, :128], EDGE))
    gains = gain_ref[...]
    high = gains.astype(BF16).astype(F32)
    rest = gains - high
    middle = rest.astype(BF16).astype(F32)
    for k, part in enumerate((high, middle, rest - middle)):
        for layer in range(LAYERS):
            halo = jnp.where(lane == SPARE + k * LAYERS + layer, part[:, layer : layer + 1], halo)
    state_ref[:, length:] = halo.astype(BF16)
    th = jnp.where(low, roll(right[:, :128], EDGE), left[:, :128])
    tl = jnp.where(low, right[:, 128:], roll(left[:, 128:], EDGE))
    halo_ref[...] = th + tl
    copy.wait()
    state_ref[:, :length] = held[...]


def chunks_of(refs, n_tp, ch):
    half = ch // 2
    count = 10 if n_tp == 8 else n_tp
    places = (0, 2, 4, 6, 6, 1, 3, 5, 7, 7) if n_tp == 8 else range(n_tp)
    chunks = []
    for i, place in enumerate(places):
        if refs[i].shape[0] == ch:
            chunks += [(place, refs[i], 0, 0), (place, refs[i], half, half)]
        else:
            chunks.append((place, refs[i], 0, half * (i % 5 - 3)))
    return chunks, refs[count:]


def forward_kernel(meta, w_ref, own_ref, *refs, layer, n_tp, n_seq, length):
    *refs, held, slopes, weights, sems = refs
    chunks, refs = chunks_of(refs, n_tp, held.shape[1])
    if layer == 0:
        state_ref, slope_ref, inverse_ref, hidden_ref, gain_ref = refs
    elif layer < LAYERS - 1:
        gain_ref, state_ref, slope_ref, inverse_ref, hidden_ref = refs
    else:
        gain_ref, digit_ref, state_ref, slope_ref, inverse_ref, hidden_ref = refs
    _, ch, width = held.shape
    wide = slopes.shape[2]
    channels = ch * n_tp
    reach = reach_of(layer)
    me, seq_at = meta[n_tp + n_seq], meta[n_tp + n_seq + 1]
    copy = pltpu.make_async_copy(w_ref.at[layer], weights, sems.at[0])
    copy.start()

    def add_power(j, acc):
        for _, ref, start, _ in chunks:
            x = ref[pl.ds(pl.multiple_of(start + j * ROWS, ROWS), ROWS), :].astype(F32)
            sq = x * x
            for i in range(0, ROWS, 8):
                acc = acc + sq[i : i + 8]
        return acc

    acc = lax.fori_loop(0, ch // (2 * ROWS), add_power, jnp.zeros((8, width), F32))
    power = jnp.sum(acc, axis=0, keepdims=True) / channels
    inverse = 1.0 / jnp.sqrt(power + EPSILON)
    inverse_ref[...] = jnp.broadcast_to(inverse, (8, width))

    def activate(j, carry):
        for m, ref, start, place in chunks:
            at = meta[m]
            x = ref[pl.ds(pl.multiple_of(start + j * ROWS, ROWS), ROWS), :].astype(F32)
            rows = pl.ds(pl.multiple_of(place + j * ROWS, ROWS), ROWS)
            if layer == 0:
                halo = x[:, length:]
                cols = [
                    halo[:, SPARE + l : SPARE + l + 1]
                    + (
                        halo[:, SPARE + LAYERS + l : SPARE + LAYERS + l + 1]
                        + halo[:, SPARE + 2 * LAYERS + l : SPARE + 2 * LAYERS + l + 1]
                    )
                    for l in range(LAYERS)
                ]
                lane = lax.broadcasted_iota(jnp.int32, (ROWS, 128), 1)
                gain_ref[at, rows, :] = jnp.where(lane == 0, cols[0], jnp.where(lane == 1, cols[1], cols[2]))
                gain = cols[0]
            else:
                gain = gain_ref[at, rows, layer : layer + 1]
            scaled = x * gain
            pre = scaled * inverse
            sq = pre * pre
            th = jnp.tanh(pre * (K0 + K1 * sq))
            half = 0.5 + 0.5 * th
            hidden = pre * half
            held[at, rows, :] = hidden.astype(BF16)
            slope = half + (hidden - hidden * th) * (K0 + (3.0 * K1) * sq)
            slopes[at, rows, :] = (slope * scaled)[:, :wide].astype(BF16)
        return carry

    lax.fori_loop(0, ch // (2 * ROWS), activate, 0)
    leave = pltpu.make_async_copy(slopes, slope_ref, sems.at[1])
    leave.start()
    hidden_ref[...] = held[me, :, :length]
    copy.wait()
    every = held[...].reshape(channels, width)
    total = own_ref[...].astype(F32)
    for tap in range(3):
        part = jnp.dot(weights[tap * ch : (tap + 1) * ch, :], every, preferred_element_type=F32)
        total = total + roll(part, (1 - tap) * reach)
    total = jnp.where(in_sequence(seq_at, width, length, n_seq * length), total, 0.0).astype(BF16)
    if layer < LAYERS - 1:
        state_ref[...] = total
    else:
        state_ref[:ch, :] = total[:, :length]
        state_ref[ch:, :] = digit_ref[...]
    leave.wait()


def send_back(layer, upstream, meta, weights, slopes, taps, grad_ref, out_refs, score, n_tp, n_seq, length):
    ch, width = upstream.shape
    wide = taps.shape[1]
    reach = reach_of(layer)
    me, seq_at = meta[n_tp + n_seq], meta[n_tp + n_seq + 1]
    grad = jnp.where(in_sequence(seq_at, width, length, n_seq * length), upstream, 0.0)
    grad = grad.astype(BF16).astype(F32)
    grad_ref[...] = grad[:, :length].astype(BF16)
    for tap in range(3):
        taps[tap * ch : (tap + 1) * ch, :] = roll(grad, (tap - 1) * reach)[:, :wide].astype(BF16)
    for copy in slopes[1:]:
        copy.wait()
    inner = jnp.zeros((8, wide), F32)
    parts = CHUNK // ch
    chunks = ch * n_tp // CHUNK
    for r in range(chunks):
        at = (me // 2) ^ r if n_tp == 8 else r
        cols = pl.ds(pl.multiple_of(at * CHUNK, 128), CHUNK)
        part = lax.dot_general(weights[:, cols], taps[...], (((0,), (0,)), ((), ())), preferred_element_type=F32)
        for q in range(parts):
            prod = part[q * ch : (q + 1) * ch] * slopes[0][at * parts + q].astype(F32)
            inner = inner + jnp.sum(prod.reshape(ch // 8, 8, wide), axis=0)
        if n_tp == 8:
            keep_ref, send_ref = out_refs
            zero = lax.rem(me, 2) == 0
            keep_ref[r] = jnp.where(zero, part[:ch], part[ch:]).astype(BF16)
            send_ref[r * ch : (r + 1) * ch, :] = jnp.where(zero, part[ch:], part[:ch]).astype(BF16)
        else:
            for q in range(parts):
                out_refs[0][at * parts + q] = part[q * ch : (q + 1) * ch].astype(BF16)
    row = lax.broadcasted_iota(jnp.int32, (8, wide), 0)
    extra = jnp.where(row == 0, jnp.sum(inner, axis=0, keepdims=True), 0.0)
    if score is not None:
        score = jnp.concatenate([score, jnp.zeros((1, wide - score.shape[1]), F32)], axis=1)
        extra = jnp.where(row == 1, score, extra)
    if n_tp == 8:
        out_refs[1][n_tp // 2 * ch :, :] = split_rows(extra)
    else:
        out_refs[1][...] = extra


def split_rows(x):
    high = x.astype(BF16).astype(F32)
    return jnp.concatenate([high, x - high], axis=0).astype(BF16)


def join_rows(x):
    x = x.astype(F32)
    return x[:8] + x[8:]


def bring(sources, targets, sems):
    copies = [pltpu.make_async_copy(source, target, sems.at[i]) for i, (source, target) in enumerate(zip(sources, targets))]
    for copy in copies:
        copy.start()
    return copies


def fetch(layer, w_ref, slope_ref, weights, slopes, sems):
    copies = [
        pltpu.make_async_copy(w_ref.at[layer], weights, sems.at[0]),
        pltpu.make_async_copy(slope_ref, slopes, sems.at[1]),
    ]
    for copy in copies:
        copy.start()
    return [slopes] + copies


def junction_kernel(meta, w_ref, slope_ref, tower_ref, halo_ref, table_ref, *refs, n_tp, n_seq, share, root):
    pieces, refs = refs[:n_seq], refs[n_seq:]
    before_ref, up_ref, both_ref, *refs = refs
    ch = before_ref.shape[0]
    both_ref[:ch, :] = before_ref[...]
    grad_ref = both_ref.at[ch:]
    *out_refs, weights, taps, slopes, donors, rec_ref, tower, columns, halo, tissues, sems, small_sems = refs
    ch, length = tower.shape
    width = length + 2 * EDGE
    count = share * n_seq
    copies = bring(
        [*pieces, table_ref, halo_ref, tower_ref],
        [columns.at[m] for m in range(n_seq)] + [tissues, halo, tower],
        small_sems,
    )
    seq_at = meta[n_tp + n_seq + 1]
    slopes = fetch(LAYERS - 1, w_ref, slope_ref, weights, slopes, sems)
    for copy in copies[: n_seq + 1]:
        copy.wait()
    for m in range(n_seq):
        at = meta[n_tp + m]
        digits = columns[m, ch:, :share].astype(F32)
        row = lax.broadcasted_iota(jnp.int32, (8, share), 0)
        first = (digits[0:1] * 256.0 + digits[1:2]) + (at * length).astype(F32)
        second = digits[2:3] * 256.0 + digits[3:4]
        third = digits[4:5] * 256.0 + digits[5:6]
        fourth = digits[6:7] + (digits[7:8] + digits[8:9])
        record = jnp.where(row == 0, first, jnp.where(row == 1, second, jnp.where(row == 2, third, fourth)))
        rec_ref[:, pl.ds(pl.multiple_of(at * share, 128), share)] = record
    table = tissues[...]
    high = table.astype(BF16)
    rest = table - high.astype(F32)
    middle = rest.astype(BF16)
    last = (rest - middle.astype(F32)).astype(BF16)
    hit = lax.broadcasted_iota(jnp.int32, (table.shape[0], count), 0) == rec_ref[2:3, :].astype(jnp.int32)
    hit = jnp.where(hit, 1.0, 0.0).astype(BF16)
    rows = sum(
        lax.dot_general(part, hit, (((0,), (0,)), ((), ())), preferred_element_type=F32)
        for part in (last, middle, high)
    )
    donor = rec_ref[0:1, :].astype(jnp.int32)
    accept = rec_ref[1:2, :].astype(jnp.int32)
    weight = rec_ref[3:4, :] / root
    place = lax.broadcasted_iota(jnp.int32, (length, count), 0)
    accepts = jnp.zeros((ch, count), F32)
    for m in range(n_seq):
        at = meta[n_tp + m]
        cols = pl.ds(pl.multiple_of(at * share, 128), share)
        block = columns[m, :ch, :]
        mine = rec_ref[0:1, cols].astype(jnp.int32) - at * length
        hit = lax.broadcasted_iota(jnp.int32, (length, share), 0) == mine
        donors[:, cols] = jnp.dot(block, jnp.where(hit, 1.0, 0.0).astype(BF16), preferred_element_type=F32)
        hit = place == accept - at * length
        accepts = accepts + jnp.dot(block, jnp.where(hit, 1.0, 0.0).astype(BF16), preferred_element_type=F32)
    product = donors[...] * accepts * rows
    scored = jnp.sum(product, axis=0, keepdims=True) / root
    score = jnp.zeros((1, share), F32)
    for m in range(n_seq):
        score = jnp.where(seq_at == m, scored[:, m * share : (m + 1) * share], score)
    scale = rows * weight
    for copy in copies[n_seq + 1 :]:
        copy.wait()
    upstream = jnp.concatenate([tower[...], halo[...]], axis=1)
    spot = position((width, count), 0, length) + seq_at * length
    for values, where in ((accepts * scale, donor), (donors[...] * scale, accept)):
        high = values.astype(BF16)
        low = (values - high.astype(F32)).astype(BF16)
        hit = jnp.where(spot == where, 1.0, 0.0).astype(BF16)
        both = lax.dot_general(
            jnp.concatenate([high, low], axis=0), hit, (((1,), (1,)), ((), ())), preferred_element_type=F32
        )
        upstream = upstream + (both[:ch] + both[ch:])
    up_ref[...] = upstream
    send_back(LAYERS - 1, upstream, meta, weights, slopes, taps, grad_ref, out_refs, score, n_tp, n_seq, length)


def pair_kernel(keep_ref, send_ref, got_ref, own_ref, rest_ref, *far_refs):
    count, ch, width = keep_ref.shape
    half = ch // 2
    extra = join_rows(send_ref[count * ch :, :]) + join_rows(got_ref[count * ch :, :])
    split = split_rows(extra)
    own_ref[ch:, :] = join_rows(split)

    def total(r, k):
        rows = slice(k * half, (k + 1) * half)
        got = got_ref[r * ch + k * half : r * ch + (k + 1) * half, :]
        return keep_ref[r, rows, :].astype(F32) + got.astype(F32)

    for k in range(2):
        own_ref[k * half : (k + 1) * half, :] = total(0, k)
        far_refs[k][:half, :] = total(1 + k, k).astype(BF16)
        far_refs[k][half:ch, :] = total(3, k).astype(BF16)
        far_refs[k][ch:, :] = split
        rest_ref[k * half : (k + 1) * half, :] = total(2 - k, k)


def relay_kernel(own_ref, rest_ref, x_ref, y_ref, sum_ref, *far_refs):
    ch = rest_ref.shape[0]
    half = ch // 2
    for k, ref in enumerate((x_ref, y_ref)):
        rows = slice(k * half, (k + 1) * half)
        sum_ref[rows, :] = own_ref[rows, :] + ref[:half, :].astype(F32)
        far_refs[k][:half, :] = (rest_ref[rows, :] + ref[half:ch, :].astype(F32)).astype(BF16)
    far_refs[0][half:, :] = x_ref[ch:, :]
    sum_ref[ch : ch + 8, :] = own_ref[ch:, :] + join_rows(x_ref[ch:, :])
    sum_ref[ch + 8 :, :] = join_rows(y_ref[ch:, :])


def backward_kernel(meta, *refs, layer, n_far, n_tp, n_seq, length):
    last = layer == 0
    if last:
        slopes = None
    else:
        w_ref, slope_ref, *refs = refs
        *refs, weights, taps, slopes, sems = refs
        slopes = fetch(layer - 1, w_ref, slope_ref, weights, slopes, sems)
    own_ref, refs = refs[0], refs[1:]
    far, refs = refs[:n_far], refs[n_far:]
    up_ref, state_ref, inverse_ref, gain_ref, *refs = refs
    out_ref, part_ref, *refs = refs
    if not last:
        grad_ref, *out_refs = refs
        if layer == LAYERS - 1:
            score_ref, *out_refs = out_refs
    ch, width = state_ref.shape
    channels = ch * n_tp
    half = ch // 2
    extra = own_ref[ch : ch + 8, :]
    if n_far:
        extra = extra + (own_ref[ch + 8 :, :] + join_rows(far[0][half:, :]))
    inner = extra[0:1, :]
    if layer == LAYERS - 1:
        score_ref[...] = extra
    inverse = inverse_ref[0:1, :width]
    gain = gain_ref[:, layer : layer + 1]
    back = own_ref[:ch, :]
    if n_far:
        back = back + jnp.concatenate([f[:half, :] for f in far], axis=0).astype(F32)
    x = state_ref[...].astype(F32)
    pre = x * gain * inverse
    sq = pre * pre
    th = jnp.tanh(pre * (K0 + K1 * sq))
    half = 0.5 + 0.5 * th
    back = back * (half + (pre * half) * (1.0 - th) * (K0 + (3.0 * K1) * sq))
    mine = back * x * inverse
    part = jnp.sum(mine[:, :length], axis=1, keepdims=True)
    part_ref[...] = jnp.broadcast_to(part, part_ref.shape)
    upstream = up_ref[:, :width] + (inverse * gain) * back - x * (inverse * inverse * inverse * inner / channels)
    out_ref[...] = upstream
    if not last:
        send_back(layer - 1, upstream, meta, weights, slopes, taps, grad_ref, out_refs, None, n_tp, n_seq, length)


def weight_kernel(meta, *refs, layer, path, n_tp, n_seq):
    pieces, refs = refs[:n_seq], refs[n_seq:]
    *sources, out_ref, whole, taps, held, done, in_sems, out_sems = refs
    ch, length = whole.shape[0], pieces[0].shape[1]
    start = pieces[0].shape[0] - ch
    reach = reach_of(layer)
    total = n_seq * length
    parts = CHUNK // ch
    chunks = ch * n_tp // CHUNK
    me = meta[n_tp + n_seq]
    core = lax.rem(me, 2)

    def chunk_at(r):
        return r if path == "whole" else (me // 2) ^ r

    def lanes(m):
        return pl.ds(pl.multiple_of(meta[n_tp + m] * length, 128), length)

    def arrive(r):
        copies = []

        def add(source, side, where):
            copies.append(
                pltpu.make_async_copy(source, held.at[r, side, :, where], in_sems.at[r, len(copies)])
            )

        if path == "whole":
            for s in range(n_seq):
                for q in range(parts):
                    add(sources[0].at[s, r * parts + q], q, pl.ds(s * length, length))
        else:
            for m in range(n_seq):
                for q in range(2):
                    source = sources[q].at[chunk_at(r), m]
                    add(source, core if q == 0 else 1 - core, lanes(m))
        return copies

    def leave(r):
        cols = pl.ds(pl.multiple_of(chunk_at(r) * CHUNK, 128), CHUNK)
        return pltpu.make_async_copy(done.at[r % 2], out_ref.at[layer, :, :, cols], out_sems.at[r % 2])

    for r in range(chunks):
        for copy in arrive(r):
            copy.start()
    for m in range(n_seq):
        whole[:, lanes(m)] = pieces[m][start:, :]
    grad = whole[...].astype(F32)
    lane = lax.broadcasted_iota(jnp.int32, (1, total), 1)
    taps[:ch, :] = jnp.where(lane < total - reach, roll(grad, -reach), 0.0).astype(BF16)
    taps[ch : 2 * ch, :] = whole[...]
    taps[2 * ch :, :] = jnp.where(lane >= reach, roll(grad, reach), 0.0).astype(BF16)
    for r in range(chunks):
        for copy in arrive(r):
            copy.wait()
        if r >= 2:
            leave(r - 2).wait()
        product = lax.dot_general(
            taps[...], held[r].reshape(CHUNK, total), (((1,), (1,)), ((), ())), preferred_element_type=F32
        )
        done[r % 2] = product.reshape(3, ch, CHUNK)
        leave(r).start()
    for r in range(max(0, chunks - 2), chunks):
        leave(r).wait()


def local(
    sequence_in,
    conv_weight,
    norm_gain,
    tissue_scale,
    donor_offset,
    acceptor_owner,
    acceptor_offset,
    tissue,
    tower_grad,
    score_grad,
):
    ch, length = sequence_in.shape
    n_tp, n_seq = size_of(TP), size_of("seq")
    channels, total = ch * n_tp, length * n_seq
    width = length + 2 * EDGE
    share = donor_offset.shape[0]
    count = share * n_seq
    paired = n_tp == 8
    n_far = 2 if paired else 0
    me = lax.axis_index(TP).astype(jnp.int32)
    seq_at = lax.axis_index("seq").astype(jnp.int32)
    meta = jnp.concatenate([tp_order(me), seq_order(seq_at), jnp.stack([me, seq_at])])
    sizes = dict(n_tp=n_tp, n_seq=n_seq)
    weights = conv_weight.transpose(0, 2, 1, 3).reshape(LAYERS, 3 * ch, channels)
    conv_flops = 6 * ch * channels * width

    def call(kernel, inputs, shapes, scratch=(), hbm_in=(), hbm_out=(), estimate=None, mib=24, **kw):
        inputs = [pltpu.with_memory_space_constraint(x, pltpu.HBM) if i in hbm_in else x for i, x in enumerate(inputs)]
        return pl.pallas_call(
            kernel,
            out_shape=[pltpu.HBM(x.shape, x.dtype) if i in hbm_out else x for i, x in enumerate(shapes)],
            in_specs=[SMEM] + [HBM if i in hbm_in else VMEM for i in range(len(inputs))],
            out_specs=[HBM if i in hbm_out else VMEM for i in range(len(shapes))],
            scratch_shapes=list(scratch),
            compiler_params=params(mib),
            cost_estimate=estimate,
            **kw,
        )(meta, *inputs)

    def array(shape, dtype=BF16):
        return jax.ShapeDtypeStruct(shape, dtype)

    edges = array((ch, 256))
    first, second = call(
        functools.partial(edge_kernel, **sizes),
        [sequence_in, tower_grad],
        [edges, edges],
        scratch=[pltpu.VMEM((2, ch, 128), BF16), pltpu.VMEM((2, ch, 128), F32), pltpu.SemaphoreType.DMA((4,))],
        hbm_in=(0, 1),
        name="edge",
    )
    pairs = [(i, i + 1) for i in range(1, n_seq - 1, 2)]
    first = lax.ppermute(first, "seq", [(i, i ^ 1) for i in range(n_seq)])
    second = lax.ppermute(second, "seq", pairs + [(j, i) for i, j in pairs])
    gain_cols = jnp.pad(norm_gain.T, ((0, 0), (0, 128 - LAYERS)))
    state, halo_grad = call(
        functools.partial(window_kernel, **sizes),
        [sequence_in, first, second, gain_cols],
        [array((ch, width)), array((ch, 128), F32)],
        scratch=[pltpu.VMEM((ch, length), BF16), pltpu.SemaphoreType.DMA],
        hbm_in=(0,),
        name="window",
    )

    record = pl.pallas_call(
        functools.partial(record_kernel, span=length),
        out_shape=array((16, length)),
        in_specs=[VMEM] * 5,
        out_specs=VMEM,
        compiler_params=params(),
        name="record",
    )(*(x.reshape(1, share) for x in (donor_offset, acceptor_owner, acceptor_offset, tissue, score_grad)))
    table = lax.dynamic_slice_in_dim(tissue_scale, me * ch, ch, 1)
    table = jnp.pad(table, ((0, -table.shape[0] % 128), (0, 0)))

    def forward(layer, own, extra, blocks=None):
        wide = length if layer == 0 else width
        final = layer == LAYERS - 1
        shapes = [
            array((ch + 16, length) if final else (ch, width)),
            array((n_tp, ch, wide)),
            array((8, width), F32),
            array((ch, length)),
        ]
        if layer == 0:
            shapes.append(array((n_tp, ch, 128), F32))
        return call(
            functools.partial(forward_kernel, layer=layer, length=length, **sizes),
            [weights, own, *(gather_tp(own) if blocks is None else blocks), *extra],
            shapes,
            scratch=[
                pltpu.VMEM((n_tp, ch, width), BF16),
                pltpu.VMEM((n_tp, ch, wide), BF16),
                pltpu.VMEM((3 * ch, channels), BF16),
                pltpu.SemaphoreType.DMA((2,)),
            ],
            hbm_in=(0,),
            hbm_out=(1,),
            estimate=cost(1, 1),
            name="forward",
        )

    state1, slope0, inverse0, hidden0, gains = forward(0, state, [])
    planned = paired and n_seq == 4
    blocks = gather_tp(state1)
    if planned:
        seq0 = gather_seq(hidden0)
        blocks, seq0[1:3] = tie(blocks, seq0[1:3])
        seq0[3] = swap(seq0[2], "seq", 1)
    state2, slope1, inverse1, hidden1 = forward(1, state1, [gains], blocks)
    def collect(blocks):
        block = pl.pallas_call(
            stack_kernel,
            out_shape=pltpu.HBM((n_seq * ch, length), BF16),
            in_specs=[pl.BlockSpec(memory_space=pl.ANY)] * n_seq,
            out_specs=HBM,
            scratch_shapes=[pltpu.SemaphoreType.DMA((n_seq,))],
            compiler_params=params(),
            cost_estimate=cost(1, 1),
            name="stack",
        )(*blocks)
        return lax.all_gather(block, "pair", axis=0).reshape(n_tp // 2, n_seq, ch, length)

    if planned:
        seq0, _ = tie(seq0, [state2])
        every0 = collect(seq0)
    blocks = gather_tp(state2)
    if planned:
        seq1 = gather_seq(hidden1)
        blocks, seq1[1:3] = tie(blocks, seq1[1:3])
        seq1[3] = swap(seq1[2], "seq", 1)
    state3, slope2, inverse2, hidden2 = forward(2, state2, [gains, record], blocks)
    slopes = [slope0, slope1, slope2]
    stored = [(sequence_in, inverse0), (state1, inverse1), (state2, inverse2)]
    if planned:
        one, two = swap(state3, "seq", 1), swap(state3, "seq", 2)
        (two,), (one,) = tie([two], [one])
        pieces = [state3, one, two, swap(two, "seq", 1)]
        seq1, pieces[2:3] = tie(seq1, pieces[2:3])
        every1 = collect(seq1)
    else:
        pieces = gather_seq(state3)
        everything = [
            [lax.all_gather(h, ("seq",) + TP, axis=0).reshape(n_seq, n_tp, ch, length)]
            for h in (hidden0, hidden1, hidden2)
        ]

    def product_shapes(layer):
        wide = length if layer == 0 else width
        if paired:
            return [array((n_tp // 2, ch, wide)), array((n_tp // 2 * ch + 16, wide))]
        return [array((n_tp, ch, wide)), array((8, wide), F32)]

    def scratch(layer):
        wide = length if layer == 0 else width
        return [
            pltpu.VMEM((3 * ch, channels), BF16),
            pltpu.VMEM((3 * ch, wide), BF16),
            pltpu.VMEM((n_tp, ch, wide), BF16),
        ]

    def reduce_tp(products):
        if not paired:
            whole, extra = products
            own = lax.psum_scatter(whole.reshape(channels, -1), TP, scatter_dimension=0, tiled=True)
            return [jnp.concatenate([own.astype(F32), lax.psum(extra, TP)], axis=0)]
        keep, send = products
        wide = keep.shape[2]
        got = swap(send, TP, 1)
        far, rest = array((ch + 16, wide)), array((ch, wide), F32)

        def step(kernel, inputs, shapes, name):
            return pl.pallas_call(
                kernel,
                out_shape=shapes,
                in_specs=[VMEM] * len(inputs),
                out_specs=[VMEM] * len(shapes),
                compiler_params=params(),
                cost_estimate=cost(1, 1),
                name=name,
            )(*inputs)

        own, rest, x, y = step(pair_kernel, [keep, send, got], [array((ch + 8, wide), F32), rest, far, far], "pair")
        shapes = [array((ch + 16, wide), F32), array((ch // 2 + 16, wide)), array((ch // 2, wide))]
        own, y, x = step(relay_kernel, [own, rest, swap(x, TP, 2), swap(y, TP, 4)], shapes, "relay")
        return [own, swap(y, TP, 4), swap(x, TP, 2)]

    upstream, grad2, *products = call(
        functools.partial(junction_kernel, share=share, root=math.sqrt(channels), **sizes),
        [weights, slopes[2], tower_grad, halo_grad, table, *pieces, hidden2],
        [array((ch, width), F32), array((2 * ch, length))] + product_shapes(2),
        scratch=scratch(2)
        + [
            pltpu.VMEM((ch, count), F32),
            pltpu.VMEM((8, count), F32),
            pltpu.VMEM((ch, length), F32),
            pltpu.VMEM((n_seq, ch + 16, length), BF16),
            pltpu.VMEM((ch, 128), F32),
            pltpu.VMEM(table.shape, F32),
            pltpu.SemaphoreType.DMA((2,)),
            pltpu.SemaphoreType.DMA((n_seq + 3,)),
        ],
        hbm_in=range(5 + n_seq),
        estimate=cost(1, 1),
        mib=32,
        name="junction",
    )

    def backward(layer, sums, upstream):
        state, inverse = stored[layer]
        wide = length if layer == 0 else width
        inputs = [*sums, upstream, state, inverse, gain_cols]
        shapes = [array((ch, wide), F32), array((ch, 128), F32)]
        extra, hbm = [], ()
        if layer > 0:
            inputs = [weights, slopes[layer - 1], *inputs]
            hbm = (0, 1)
            shapes.append(array((ch, length)))
            if layer == LAYERS - 1:
                shapes.append(array((8, width), F32))
            shapes += product_shapes(layer - 1)
            extra = scratch(layer - 1) + [pltpu.SemaphoreType.DMA((2,))]
        return call(
            functools.partial(backward_kernel, layer=layer, n_far=n_far, length=length, **sizes),
            inputs,
            shapes,
            scratch=extra,
            hbm_in=hbm,
            estimate=cost(1, 1),
            name="backward",
        )

    def weigh(layer, path, grads, sources, before):
        inputs = [*grads, *sources, *before]
        return call(
            functools.partial(weight_kernel, layer=layer, path=path, **sizes),
            inputs,
            [array((LAYERS, 3, ch, channels), F32)],
            scratch=[
                pltpu.VMEM((ch, total), BF16),
                pltpu.VMEM((3 * ch, total), BF16),
                pltpu.VMEM((channels // CHUNK, CHUNK // ch, ch, total), BF16),
                pltpu.VMEM((2, 3, ch, CHUNK), F32),
                pltpu.SemaphoreType.DMA((channels // CHUNK, n_seq * (CHUNK // ch))),
                pltpu.SemaphoreType.DMA((2,)),
            ],
            hbm_in=range(n_seq, len(inputs)),
            hbm_out=(0,),
            estimate=cost(6 * ch * channels * total, 2 * channels * total),
            mib=32,
            input_output_aliases={len(inputs): 0} if before else {},
            name="weight",
        )[0]

    sums = reduce_tp(products)
    grads2 = gather_seq(grad2)
    if planned:
        sums, grads2[1:3] = tie(sums, grads2[1:3])
    upstream, part2, grad1, score_rows, *products = backward(2, sums, upstream)
    scores = score_rows[1, :share]

    grads1 = gather_seq(grad1)
    sums = reduce_tp(products)
    if planned:
        near0 = swap(every0, TP, 1)
        sums, got = tie(sums, [every0, near0, *grads2, *grads1[1:3]])
        (every0, near0), grads2, grads1[1:3] = got[:2], got[2 : 2 + n_seq], got[2 + n_seq :]
        every2 = collect(grads2)
    upstream, part1, grad0, *products = backward(1, sums, upstream)

    sums = reduce_tp(products)
    if planned:
        near1 = swap(every1, TP, 1)
        sums, got = tie(sums, [*grads1, every1, near1])
        grads1, (every1, near1) = got[:n_seq], got[n_seq:]
    input_grad, part0 = backward(0, sums, upstream)

    columns = jnp.pad(jnp.stack([p[:, 0] for p in (part0, part1, part2)]), ((0, 8 - LAYERS), (0, 0)))
    pieces = gather_seq(columns)
    if len(pieces) == 4:
        gain_grad = (pieces[0] + pieces[1]) + (pieces[2] + pieces[3])
    else:
        gain_grad = sum(pieces)

    grads0 = gather_seq(grad0)
    if planned:
        grads1, _ = tie(grads1, [part0])
        weight_grad = weigh(1, "pair", grads1, [every1, near1], [])
        grads0, (gain_grad,) = tie(grads0, [gain_grad])
        weight_grad = weigh(0, "pair", grads0, [every0, near0], [weight_grad])
        (every2,), (weight_grad,) = tie([every2], [weight_grad])
        weight_grad = weigh(2, "pair", grads2, [every2, swap(every2, TP, 1)], [weight_grad])
    else:
        weight_grad = weigh(0, "whole", grads0, everything[0], [])
        weight_grad = weigh(1, "whole", grads1, everything[1], [weight_grad])
        weight_grad = weigh(2, "whole", grads2, everything[2], [weight_grad])
    return (scores, input_grad, weight_grad.transpose(0, 2, 1, 3), gain_grad[:LAYERS])


def solution(mesh):
    tp = mesh.shape["tp"]
    pairs = jax.sharding.Mesh(mesh.devices.reshape(mesh.shape["seq"], tp // 2, 2), ("seq",) + TP)
    return jax.shard_map(
        local,
        mesh=pairs,
        in_specs=(
            P(TP, "seq"),
            P(None, TP, None, None),
            P(None, TP),
            P(),
            P("seq"),
            P("seq", None),
            P("seq"),
            P("seq"),
            P(TP, "seq"),
            P("seq"),
        ),
        out_specs=(P("seq"), P(TP, "seq"), P(None, TP, None, None), P(None, TP)),
        check_vma=False,
    )
```

```python
import functools
import math

import jax
import jax.numpy as jnp
from jax import lax
from jax.experimental import pallas as pl
from jax.experimental.pallas import tpu as pltpu
from jax.sharding import PartitionSpec as P

LAYERS = 3
EPSILON = 1e-06
EDGE = 64
SPARE = 56
CHUNK = 384
ROWS = 16
K0 = math.sqrt(2.0 / math.pi)
K1 = K0 * 0.044715
F32 = jnp.float32
BF16 = jnp.bfloat16

VMEM = pl.BlockSpec(memory_space=pltpu.VMEM)
SMEM = pl.BlockSpec(memory_space=pltpu.SMEM)
HBM = pl.BlockSpec(memory_space=pltpu.HBM)

TP = ("pair", "side")


def params(mib=24):
    return pltpu.CompilerParams(vmem_limit_bytes=mib * 1024 * 1024)


def cost(flops, nbytes, special=0):
    return pl.CostEstimate(flops=flops, bytes_accessed=nbytes, transcendentals=special)


def tie(first, then):
    out = lax.optimization_barrier((tuple(first), tuple(then)))
    return list(out[0]), list(out[1])


def reach_of(layer):
    return 2 ** (layer + 3)


def size_of(axis):
    return math.prod(lax.axis_size(name) for name in axis) if isinstance(axis, tuple) else lax.axis_size(axis)


def swap(x, axis, mask):
    return lax.ppermute(x, axis, [(i, i ^ mask) for i in range(size_of(axis))])


def gather_tp(x):
    if size_of(TP) == 8:
        half = x.shape[0] // 2
        along_x, along_y = swap(x, TP, 2), swap(x, TP, 4)
        corner = [swap(along_x[:half], TP, 4), swap(along_y[half:], TP, 2)]
        far = [x, along_x, along_y, *corner]
        near = [swap(v, TP, 1) for v in far]
        return far + near
    whole = lax.all_gather(x, TP, axis=0)
    return [whole[i] for i in range(whole.shape[0])]


def tp_order(me):
    count = size_of(TP)
    steps = jnp.arange(count, dtype=jnp.int32)
    return me ^ steps if count == 8 else steps


def gather_seq(x):
    if size_of("seq") == 4:
        one, two = swap(x, "seq", 1), swap(x, "seq", 2)
        return [x, one, two, swap(two, "seq", 1)]
    whole = lax.all_gather(x, "seq", axis=0)
    return [whole[i] for i in range(whole.shape[0])]


def seq_order(me):
    count = size_of("seq")
    steps = jnp.arange(count, dtype=jnp.int32)
    return me ^ steps if count == 4 else steps


def roll(x, shift):
    shift = shift % x.shape[1]
    return x if shift == 0 else pltpu.roll(x, shift, 1)


def position(shape, dim, length):
    at = lax.broadcasted_iota(jnp.int32, shape, dim)
    return jnp.where(at < length + EDGE, at, at - (length + 2 * EDGE))


def in_sequence(seq_at, width, length, total):
    at = position((1, width), 1, length) + seq_at * length
    return (at >= 0) & (at < total)


def stack_kernel(*refs):
    *pieces, out_ref, sems = refs
    rows = out_ref.shape[0] // len(pieces)
    copies = [
        pltpu.make_async_copy(piece.at[:rows], out_ref.at[i * rows : (i + 1) * rows], sems.at[i])
        for i, piece in enumerate(pieces)
    ]
    for copy in copies:
        copy.start()
    for copy in copies:
        copy.wait()


def record_kernel(donor_ref, owner_ref, accept_ref, tissue_ref, grad_ref, out_ref, *, span):
    row = lax.broadcasted_iota(jnp.int32, (16, out_ref.shape[1]), 0)
    out = jnp.zeros(row.shape, F32)
    values = []
    for x in (donor_ref[...], owner_ref[...] * span + accept_ref[...], tissue_ref[...]):
        values += [(x >> 8).astype(F32), (x & 255).astype(F32)]
    grad = grad_ref[...]
    high = grad.astype(BF16).astype(F32)
    middle = (grad - high).astype(BF16).astype(F32)
    values += [high, middle, grad - high - middle]
    for k, value in enumerate(values):
        value = jnp.concatenate([value, jnp.zeros((1, row.shape[1] - value.shape[1]), F32)], axis=1)
        out = jnp.where(row == k, value, out)
    out_ref[...] = out.astype(BF16)


def edge_kernel(meta, seq_ref, tower_ref, first_ref, second_ref, states, grads, sems, *, n_tp, n_seq):
    ch, length = seq_ref.shape
    copies = []
    for i, start in enumerate((0, length - 128)):
        copies.append(pltpu.make_async_copy(seq_ref.at[:, start : start + 128], states.at[i], sems.at[2 * i]))
        copies.append(pltpu.make_async_copy(tower_ref.at[:, start : start + 128], grads.at[i], sems.at[2 * i + 1]))
    for copy in copies:
        copy.start()
    for copy in copies:
        copy.wait()
    even = lax.rem(meta[n_tp + n_seq + 1], 2) == 0
    low = lax.broadcasted_iota(jnp.int32, (ch, 128), 1) < EDGE

    def pack(state, grad):
        high = grad.astype(BF16).astype(F32)
        return [jnp.where(low, state, roll(high, EDGE)), jnp.where(low, grad - high, 0.0)]

    left = pack(states[0].astype(F32), grads[0])
    right = pack(roll(states[1].astype(F32), EDGE), roll(grads[1], EDGE))
    for i in range(2):
        first_ref[:, i * 128 : (i + 1) * 128] = jnp.where(even, right[i], left[i]).astype(BF16)
        second_ref[:, i * 128 : (i + 1) * 128] = jnp.where(even, left[i], right[i]).astype(BF16)


def window_kernel(
    meta, seq_ref, first_ref, second_ref, gain_ref, state_ref, halo_ref, held, sem, *, n_tp, n_seq
):
    ch, length = held.shape
    copy = pltpu.make_async_copy(seq_ref, held, sem)
    copy.start()
    even = lax.rem(meta[n_tp + n_seq + 1], 2) == 0
    first = first_ref[...].astype(F32)
    second = second_ref[...].astype(F32)
    right = jnp.where(even, first, second)
    left = jnp.where(even, second, first)
    lane = lax.broadcasted_iota(jnp.int32, (ch, 128), 1)
    low = lane < EDGE
    halo = jnp.where(low, right[:, :128], roll(left[:, :128], EDGE))
    gains = gain_ref[...]
    high = gains.astype(BF16).astype(F32)
    rest = gains - high
    middle = rest.astype(BF16).astype(F32)
    for k, part in enumerate((high, middle, rest - middle)):
        for layer in range(LAYERS):
            halo = jnp.where(lane == SPARE + k * LAYERS + layer, part[:, layer : layer + 1], halo)
    state_ref[:, length:] = halo.astype(BF16)
    th = jnp.where(low, roll(right[:, :128], EDGE), left[:, :128])
    tl = jnp.where(low, right[:, 128:], roll(left[:, 128:], EDGE))
    halo_ref[...] = th + tl
    copy.wait()
    state_ref[:, :length] = held[...]


def chunks_of(refs, n_tp, ch):
    half = ch // 2
    count = 10 if n_tp == 8 else n_tp
    places = (0, 2, 4, 6, 6, 1, 3, 5, 7, 7) if n_tp == 8 else range(n_tp)
    chunks = []
    for i, place in enumerate(places):
        if refs[i].shape[0] == ch:
            chunks += [(place, refs[i], 0, 0), (place, refs[i], half, half)]
        else:
            chunks.append((place, refs[i], 0, half * (i % 5 - 3)))
    return chunks, refs[count:]


def forward_kernel(meta, w_ref, own_ref, *refs, layer, n_tp, n_seq, length):
    *refs, held, slopes, weights, sems = refs
    chunks, refs = chunks_of(refs, n_tp, held.shape[1])
    if layer == 0:
        state_ref, slope_ref, inverse_ref, hidden_ref, gain_ref = refs
    elif layer < LAYERS - 1:
        gain_ref, state_ref, slope_ref, inverse_ref, hidden_ref = refs
    else:
        gain_ref, digit_ref, state_ref, slope_ref, inverse_ref, hidden_ref = refs
    _, ch, width = held.shape
    wide = slopes.shape[2]
    channels = ch * n_tp
    reach = reach_of(layer)
    me, seq_at = meta[n_tp + n_seq], meta[n_tp + n_seq + 1]
    copy = pltpu.make_async_copy(w_ref.at[layer], weights, sems.at[0])
    copy.start()

    def add_power(j, acc):
        for _, ref, start, _ in chunks:
            x = ref[pl.ds(pl.multiple_of(start + j * ROWS, ROWS), ROWS), :].astype(F32)
            sq = x * x
            for i in range(0, ROWS, 8):
                acc = acc + sq[i : i + 8]
        return acc

    acc = lax.fori_loop(0, ch // (2 * ROWS), add_power, jnp.zeros((8, width), F32))
    power = jnp.sum(acc, axis=0, keepdims=True) / channels
    inverse = 1.0 / jnp.sqrt(power + EPSILON)
    inverse_ref[...] = jnp.broadcast_to(inverse, (8, width))

    def activate(j, carry):
        for m, ref, start, place in chunks:
            at = meta[m]
            x = ref[pl.ds(pl.multiple_of(start + j * ROWS, ROWS), ROWS), :].astype(F32)
            rows = pl.ds(pl.multiple_of(place + j * ROWS, ROWS), ROWS)
            if layer == 0:
                halo = x[:, length:]
                cols = [
                    halo[:, SPARE + l : SPARE + l + 1]
                    + (
                        halo[:, SPARE + LAYERS + l : SPARE + LAYERS + l + 1]
                        + halo[:, SPARE + 2 * LAYERS + l : SPARE + 2 * LAYERS + l + 1]
                    )
                    for l in range(LAYERS)
                ]
                lane = lax.broadcasted_iota(jnp.int32, (ROWS, 128), 1)
                gain_ref[at, rows, :] = jnp.where(lane == 0, cols[0], jnp.where(lane == 1, cols[1], cols[2]))
                gain = cols[0]
            else:
                gain = gain_ref[at, rows, layer : layer + 1]
            scaled = x * gain
            pre = scaled * inverse
            sq = pre * pre
            th = jnp.tanh(pre * (K0 + K1 * sq))
            half = 0.5 + 0.5 * th
            hidden = pre * half
            held[at, rows, :] = hidden.astype(BF16)
            slope = half + (hidden - hidden * th) * (K0 + (3.0 * K1) * sq)
            slopes[at, rows, :] = (slope * scaled)[:, :wide].astype(BF16)
        return carry

    lax.fori_loop(0, ch // (2 * ROWS), activate, 0)
    leave = pltpu.make_async_copy(slopes, slope_ref, sems.at[1])
    leave.start()
    hidden_ref[...] = held[me, :, :length]
    copy.wait()
    every = held[...].reshape(channels, width)
    total = own_ref[...].astype(F32)
    for tap in range(3):
        part = jnp.dot(weights[tap * ch : (tap + 1) * ch, :], every, preferred_element_type=F32)
        total = total + roll(part, (1 - tap) * reach)
    total = jnp.where(in_sequence(seq_at, width, length, n_seq * length), total, 0.0).astype(BF16)
    if layer < LAYERS - 1:
        state_ref[...] = total
    else:
        state_ref[:ch, :] = total[:, :length]
        state_ref[ch:, :] = digit_ref[...]
    leave.wait()


def send_back(layer, upstream, meta, weights, slopes, taps, grad_ref, out_refs, score, n_tp, n_seq, length):
    ch, width = upstream.shape
    wide = taps.shape[1]
    reach = reach_of(layer)
    me, seq_at = meta[n_tp + n_seq], meta[n_tp + n_seq + 1]
    grad = jnp.where(in_sequence(seq_at, width, length, n_seq * length), upstream, 0.0)
    grad = grad.astype(BF16).astype(F32)
    grad_ref[...] = grad[:, :length].astype(BF16)
    for tap in range(3):
        taps[tap * ch : (tap + 1) * ch, :] = roll(grad, (tap - 1) * reach)[:, :wide].astype(BF16)
    for copy in slopes[1:]:
        copy.wait()
    inner = jnp.zeros((8, wide), F32)
    parts = CHUNK // ch
    chunks = ch * n_tp // CHUNK
    for r in range(chunks):
        at = (me // 2) ^ r if n_tp == 8 else r
        cols = pl.ds(pl.multiple_of(at * CHUNK, 128), CHUNK)
        part = lax.dot_general(weights[:, cols], taps[...], (((0,), (0,)), ((), ())), preferred_element_type=F32)
        for q in range(parts):
            prod = part[q * ch : (q + 1) * ch] * slopes[0][at * parts + q].astype(F32)
            inner = inner + jnp.sum(prod.reshape(ch // 8, 8, wide), axis=0)
        if n_tp == 8:
            keep_ref, send_ref = out_refs
            zero = lax.rem(me, 2) == 0
            keep_ref[r] = jnp.where(zero, part[:ch], part[ch:]).astype(BF16)
            send_ref[r * ch : (r + 1) * ch, :] = jnp.where(zero, part[ch:], part[:ch]).astype(BF16)
        else:
            for q in range(parts):
                out_refs[0][at * parts + q] = part[q * ch : (q + 1) * ch].astype(BF16)
    row = lax.broadcasted_iota(jnp.int32, (8, wide), 0)
    extra = jnp.where(row == 0, jnp.sum(inner, axis=0, keepdims=True), 0.0)
    if score is not None:
        score = jnp.concatenate([score, jnp.zeros((1, wide - score.shape[1]), F32)], axis=1)
        extra = jnp.where(row == 1, score, extra)
    if n_tp == 8:
        out_refs[1][n_tp // 2 * ch :, :] = split_rows(extra)
    else:
        out_refs[1][...] = extra


def split_rows(x):
    high = x.astype(BF16).astype(F32)
    return jnp.concatenate([high, x - high], axis=0).astype(BF16)


def join_rows(x):
    x = x.astype(F32)
    return x[:8] + x[8:]


def bring(sources, targets, sems):
    copies = [pltpu.make_async_copy(source, target, sems.at[i]) for i, (source, target) in enumerate(zip(sources, targets))]
    for copy in copies:
        copy.start()
    return copies


def fetch(layer, w_ref, slope_ref, weights, slopes, sems):
    copies = [
        pltpu.make_async_copy(w_ref.at[layer], weights, sems.at[0]),
        pltpu.make_async_copy(slope_ref, slopes, sems.at[1]),
    ]
    for copy in copies:
        copy.start()
    return [slopes] + copies


def junction_kernel(meta, w_ref, slope_ref, tower_ref, halo_ref, table_ref, *refs, n_tp, n_seq, share, root):
    pieces, refs = refs[:n_seq], refs[n_seq:]
    up_ref, grad_ref, *refs = refs
    *out_refs, weights, taps, slopes, donors, rec_ref, tower, columns, halo, tissues, sems, small_sems = refs
    ch, length = tower.shape
    width = length + 2 * EDGE
    count = share * n_seq
    copies = bring(
        [*pieces, table_ref, halo_ref, tower_ref],
        [columns.at[m] for m in range(n_seq)] + [tissues, halo, tower],
        small_sems,
    )
    seq_at = meta[n_tp + n_seq + 1]
    slopes = fetch(LAYERS - 1, w_ref, slope_ref, weights, slopes, sems)
    for copy in copies[: n_seq + 1]:
        copy.wait()
    for m in range(n_seq):
        at = meta[n_tp + m]
        digits = columns[m, ch:, :share].astype(F32)
        row = lax.broadcasted_iota(jnp.int32, (8, share), 0)
        first = (digits[0:1] * 256.0 + digits[1:2]) + (at * length).astype(F32)
        second = digits[2:3] * 256.0 + digits[3:4]
        third = digits[4:5] * 256.0 + digits[5:6]
        fourth = digits[6:7] + (digits[7:8] + digits[8:9])
        record = jnp.where(row == 0, first, jnp.where(row == 1, second, jnp.where(row == 2, third, fourth)))
        rec_ref[:, pl.ds(pl.multiple_of(at * share, 128), share)] = record
    table = tissues[...]
    high = table.astype(BF16)
    rest = table - high.astype(F32)
    middle = rest.astype(BF16)
    last = (rest - middle.astype(F32)).astype(BF16)
    hit = lax.broadcasted_iota(jnp.int32, (table.shape[0], count), 0) == rec_ref[2:3, :].astype(jnp.int32)
    hit = jnp.where(hit, 1.0, 0.0).astype(BF16)
    rows = sum(
        lax.dot_general(part, hit, (((0,), (0,)), ((), ())), preferred_element_type=F32)
        for part in (last, middle, high)
    )
    donor = rec_ref[0:1, :].astype(jnp.int32)
    accept = rec_ref[1:2, :].astype(jnp.int32)
    weight = rec_ref[3:4, :] / root
    place = lax.broadcasted_iota(jnp.int32, (length, count), 0)
    accepts = jnp.zeros((ch, count), F32)
    for m in range(n_seq):
        at = meta[n_tp + m]
        cols = pl.ds(pl.multiple_of(at * share, 128), share)
        block = columns[m, :ch, :]
        mine = rec_ref[0:1, cols].astype(jnp.int32) - at * length
        hit = lax.broadcasted_iota(jnp.int32, (length, share), 0) == mine
        donors[:, cols] = jnp.dot(block, jnp.where(hit, 1.0, 0.0).astype(BF16), preferred_element_type=F32)
        hit = place == accept - at * length
        accepts = accepts + jnp.dot(block, jnp.where(hit, 1.0, 0.0).astype(BF16), preferred_element_type=F32)
    product = donors[...] * accepts * rows
    scored = jnp.sum(product, axis=0, keepdims=True) / root
    score = jnp.zeros((1, share), F32)
    for m in range(n_seq):
        score = jnp.where(seq_at == m, scored[:, m * share : (m + 1) * share], score)
    scale = rows * weight
    for copy in copies[n_seq + 1 :]:
        copy.wait()
    upstream = jnp.concatenate([tower[...], halo[...]], axis=1)
    spot = position((width, count), 0, length) + seq_at * length
    for values, where in ((accepts * scale, donor), (donors[...] * scale, accept)):
        high = values.astype(BF16)
        low = (values - high.astype(F32)).astype(BF16)
        hit = jnp.where(spot == where, 1.0, 0.0).astype(BF16)
        both = lax.dot_general(
            jnp.concatenate([high, low], axis=0), hit, (((1,), (1,)), ((), ())), preferred_element_type=F32
        )
        upstream = upstream + (both[:ch] + both[ch:])
    up_ref[...] = upstream
    send_back(LAYERS - 1, upstream, meta, weights, slopes, taps, grad_ref, out_refs, score, n_tp, n_seq, length)


def pair_kernel(keep_ref, send_ref, got_ref, own_ref, rest_ref, *far_refs):
    count, ch, width = keep_ref.shape
    half = ch // 2
    extra = join_rows(send_ref[count * ch :, :]) + join_rows(got_ref[count * ch :, :])
    split = split_rows(extra)
    own_ref[ch:, :] = join_rows(split)

    def total(r, k):
        rows = slice(k * half, (k + 1) * half)
        got = got_ref[r * ch + k * half : r * ch + (k + 1) * half, :]
        return keep_ref[r, rows, :].astype(F32) + got.astype(F32)

    for k in range(2):
        own_ref[k * half : (k + 1) * half, :] = total(0, k)
        far_refs[k][:half, :] = total(1 + k, k).astype(BF16)
        far_refs[k][half:ch, :] = total(3, k).astype(BF16)
        far_refs[k][ch:, :] = split
        rest_ref[k * half : (k + 1) * half, :] = total(2 - k, k)


def relay_kernel(own_ref, rest_ref, x_ref, y_ref, sum_ref, *far_refs):
    ch = rest_ref.shape[0]
    half = ch // 2
    for k, ref in enumerate((x_ref, y_ref)):
        rows = slice(k * half, (k + 1) * half)
        sum_ref[rows, :] = own_ref[rows, :] + ref[:half, :].astype(F32)
        far_refs[k][:half, :] = (rest_ref[rows, :] + ref[half:ch, :].astype(F32)).astype(BF16)
    far_refs[0][half:, :] = x_ref[ch:, :]
    sum_ref[ch : ch + 8, :] = own_ref[ch:, :] + join_rows(x_ref[ch:, :])
    sum_ref[ch + 8 :, :] = join_rows(y_ref[ch:, :])


def backward_kernel(meta, *refs, layer, n_far, n_tp, n_seq, length):
    last = layer == 0
    if last:
        slopes = None
    else:
        w_ref, slope_ref, *refs = refs
        *refs, weights, taps, slopes, sems = refs
        slopes = fetch(layer - 1, w_ref, slope_ref, weights, slopes, sems)
    own_ref, refs = refs[0], refs[1:]
    far, refs = refs[:n_far], refs[n_far:]
    up_ref, state_ref, inverse_ref, gain_ref, *refs = refs
    out_ref, part_ref, *refs = refs
    if not last:
        grad_ref, *out_refs = refs
        if layer == LAYERS - 1:
            score_ref, *out_refs = out_refs
    ch, width = state_ref.shape
    channels = ch * n_tp
    half = ch // 2
    extra = own_ref[ch : ch + 8, :]
    if n_far:
        extra = extra + (own_ref[ch + 8 :, :] + join_rows(far[0][half:, :]))
    inner = extra[0:1, :]
    if layer == LAYERS - 1:
        score_ref[...] = extra
    inverse = inverse_ref[0:1, :width]
    gain = gain_ref[:, layer : layer + 1]
    back = own_ref[:ch, :]
    if n_far:
        back = back + jnp.concatenate([f[:half, :] for f in far], axis=0).astype(F32)
    x = state_ref[...].astype(F32)
    pre = x * gain * inverse
    sq = pre * pre
    th = jnp.tanh(pre * (K0 + K1 * sq))
    half = 0.5 + 0.5 * th
    back = back * (half + (pre * half) * (1.0 - th) * (K0 + (3.0 * K1) * sq))
    mine = back * x * inverse
    part = jnp.sum(mine[:, :length], axis=1, keepdims=True)
    part_ref[...] = jnp.broadcast_to(part, part_ref.shape)
    upstream = up_ref[:, :width] + (inverse * gain) * back - x * (inverse * inverse * inverse * inner / channels)
    out_ref[...] = upstream
    if not last:
        send_back(layer - 1, upstream, meta, weights, slopes, taps, grad_ref, out_refs, None, n_tp, n_seq, length)


def weight_kernel(meta, *refs, layer, path, n_tp, n_seq):
    pieces, refs = refs[:n_seq], refs[n_seq:]
    *sources, out_ref, whole, taps, held, done, in_sems, out_sems = refs
    ch, length = whole.shape[0], pieces[0].shape[1]
    start = pieces[0].shape[0] - ch
    reach = reach_of(layer)
    total = n_seq * length
    parts = CHUNK // ch
    chunks = ch * n_tp // CHUNK
    me = meta[n_tp + n_seq]
    core = lax.rem(me, 2)

    def chunk_at(r):
        return r if path == "whole" else (me // 2) ^ r

    def lanes(m):
        return pl.ds(pl.multiple_of(meta[n_tp + m] * length, 128), length)

    def arrive(r):
        copies = []

        def add(source, side, where):
            copies.append(
                pltpu.make_async_copy(source, held.at[r, side, :, where], in_sems.at[r, len(copies)])
            )

        if path == "whole":
            for s in range(n_seq):
                for q in range(parts):
                    add(sources[0].at[s, r * parts + q], q, pl.ds(s * length, length))
        else:
            for m in range(n_seq):
                for q in range(2):
                    source = sources[q].at[chunk_at(r), m]
                    add(source, core if q == 0 else 1 - core, lanes(m))
        return copies

    def leave(r):
        cols = pl.ds(pl.multiple_of(chunk_at(r) * CHUNK, 128), CHUNK)
        return pltpu.make_async_copy(done.at[r % 2], out_ref.at[layer, :, :, cols], out_sems.at[r % 2])

    for r in range(chunks):
        for copy in arrive(r):
            copy.start()
    for m in range(n_seq):
        whole[:, lanes(m)] = pieces[m][start:, :]
    grad = whole[...].astype(F32)
    lane = lax.broadcasted_iota(jnp.int32, (1, total), 1)
    taps[:ch, :] = jnp.where(lane < total - reach, roll(grad, -reach), 0.0).astype(BF16)
    taps[ch : 2 * ch, :] = whole[...]
    taps[2 * ch :, :] = jnp.where(lane >= reach, roll(grad, reach), 0.0).astype(BF16)
    for r in range(chunks):
        for copy in arrive(r):
            copy.wait()
        if r >= 2:
            leave(r - 2).wait()
        product = lax.dot_general(
            taps[...], held[r].reshape(CHUNK, total), (((1,), (1,)), ((), ())), preferred_element_type=F32
        )
        done[r % 2] = product.reshape(3, ch, CHUNK)
        leave(r).start()
    for r in range(max(0, chunks - 2), chunks):
        leave(r).wait()


def local(
    sequence_in,
    conv_weight,
    norm_gain,
    tissue_scale,
    donor_offset,
    acceptor_owner,
    acceptor_offset,
    tissue,
    tower_grad,
    score_grad,
):
    ch, length = sequence_in.shape
    n_tp, n_seq = size_of(TP), size_of("seq")
    channels, total = ch * n_tp, length * n_seq
    width = length + 2 * EDGE
    share = donor_offset.shape[0]
    count = share * n_seq
    paired = n_tp == 8
    n_far = 2 if paired else 0
    me = lax.axis_index(TP).astype(jnp.int32)
    seq_at = lax.axis_index("seq").astype(jnp.int32)
    meta = jnp.concatenate([tp_order(me), seq_order(seq_at), jnp.stack([me, seq_at])])
    sizes = dict(n_tp=n_tp, n_seq=n_seq)
    weights = conv_weight.transpose(0, 2, 1, 3).reshape(LAYERS, 3 * ch, channels)
    conv_flops = 6 * ch * channels * width

    def call(kernel, inputs, shapes, scratch=(), hbm_in=(), hbm_out=(), estimate=None, mib=24, **kw):
        inputs = [pltpu.with_memory_space_constraint(x, pltpu.HBM) if i in hbm_in else x for i, x in enumerate(inputs)]
        return pl.pallas_call(
            kernel,
            out_shape=[pltpu.HBM(x.shape, x.dtype) if i in hbm_out else x for i, x in enumerate(shapes)],
            in_specs=[SMEM] + [HBM if i in hbm_in else VMEM for i in range(len(inputs))],
            out_specs=[HBM if i in hbm_out else VMEM for i in range(len(shapes))],
            scratch_shapes=list(scratch),
            compiler_params=params(mib),
            cost_estimate=estimate,
            **kw,
        )(meta, *inputs)

    def array(shape, dtype=BF16):
        return jax.ShapeDtypeStruct(shape, dtype)

    edges = array((ch, 256))
    first, second = call(
        functools.partial(edge_kernel, **sizes),
        [sequence_in, tower_grad],
        [edges, edges],
        scratch=[pltpu.VMEM((2, ch, 128), BF16), pltpu.VMEM((2, ch, 128), F32), pltpu.SemaphoreType.DMA((4,))],
        hbm_in=(0, 1),
        name="edge",
    )
    pairs = [(i, i + 1) for i in range(1, n_seq - 1, 2)]
    first = lax.ppermute(first, "seq", [(i, i ^ 1) for i in range(n_seq)])
    second = lax.ppermute(second, "seq", pairs + [(j, i) for i, j in pairs])
    gain_cols = jnp.pad(norm_gain.T, ((0, 0), (0, 128 - LAYERS)))
    state, halo_grad = call(
        functools.partial(window_kernel, **sizes),
        [sequence_in, first, second, gain_cols],
        [array((ch, width)), array((ch, 128), F32)],
        scratch=[pltpu.VMEM((ch, length), BF16), pltpu.SemaphoreType.DMA],
        hbm_in=(0,),
        name="window",
    )

    record = pl.pallas_call(
        functools.partial(record_kernel, span=length),
        out_shape=array((16, length)),
        in_specs=[VMEM] * 5,
        out_specs=VMEM,
        compiler_params=params(),
        name="record",
    )(*(x.reshape(1, share) for x in (donor_offset, acceptor_owner, acceptor_offset, tissue, score_grad)))
    table = lax.dynamic_slice_in_dim(tissue_scale, me * ch, ch, 1)
    table = jnp.pad(table, ((0, -table.shape[0] % 128), (0, 0)))

    def forward(layer, own, extra, blocks=None):
        wide = length if layer == 0 else width
        final = layer == LAYERS - 1
        shapes = [
            array((ch + 16, length) if final else (ch, width)),
            array((n_tp, ch, wide)),
            array((8, width), F32),
            array((ch, length)),
        ]
        if layer == 0:
            shapes.append(array((n_tp, ch, 128), F32))
        return call(
            functools.partial(forward_kernel, layer=layer, length=length, **sizes),
            [weights, own, *(gather_tp(own) if blocks is None else blocks), *extra],
            shapes,
            scratch=[
                pltpu.VMEM((n_tp, ch, width), BF16),
                pltpu.VMEM((n_tp, ch, wide), BF16),
                pltpu.VMEM((3 * ch, channels), BF16),
                pltpu.SemaphoreType.DMA((2,)),
            ],
            hbm_in=(0,),
            hbm_out=(1,),
            estimate=cost(1, 1),
            name="forward",
        )

    state1, slope0, inverse0, hidden0, gains = forward(0, state, [])
    planned = paired and n_seq == 4
    blocks = gather_tp(state1)
    if planned:
        seq0 = gather_seq(hidden0)
        blocks, seq0[1:3] = tie(blocks, seq0[1:3])
        seq0[3] = swap(seq0[2], "seq", 1)
    state2, slope1, inverse1, hidden1 = forward(1, state1, [gains], blocks)
    def collect(blocks):
        block = pl.pallas_call(
            stack_kernel,
            out_shape=pltpu.HBM((n_seq * ch, length), BF16),
            in_specs=[pl.BlockSpec(memory_space=pl.ANY)] * n_seq,
            out_specs=HBM,
            scratch_shapes=[pltpu.SemaphoreType.DMA((n_seq,))],
            compiler_params=params(),
            cost_estimate=cost(1, 1),
            name="stack",
        )(*blocks)
        return lax.all_gather(block, "pair", axis=0).reshape(n_tp // 2, n_seq, ch, length)

    if planned:
        seq0, _ = tie(seq0, [state2])
        every0 = collect(seq0)
    blocks = gather_tp(state2)
    if planned:
        seq1 = gather_seq(hidden1)
        blocks, seq1[1:3] = tie(blocks, seq1[1:3])
        seq1[3] = swap(seq1[2], "seq", 1)
    state3, slope2, inverse2, hidden2 = forward(2, state2, [gains, record], blocks)
    slopes = [slope0, slope1, slope2]
    stored = [(sequence_in, inverse0), (state1, inverse1), (state2, inverse2)]
    if planned:
        one, two = swap(state3, "seq", 1), swap(state3, "seq", 2)
        (two,), (one,) = tie([two], [one])
        pieces = [state3, one, two, swap(two, "seq", 1)]
        seq1, pieces[2:3] = tie(seq1, pieces[2:3])
        every1 = collect(seq1)
        pieces, (hidden2,) = tie(pieces, [hidden2])
        seq2 = gather_seq(hidden2)
    else:
        pieces = gather_seq(state3)
        everything = [
            [lax.all_gather(h, ("seq",) + TP, axis=0).reshape(n_seq, n_tp, ch, length)]
            for h in (hidden0, hidden1, hidden2)
        ]

    def product_shapes(layer):
        wide = length if layer == 0 else width
        if paired:
            return [array((n_tp // 2, ch, wide)), array((n_tp // 2 * ch + 16, wide))]
        return [array((n_tp, ch, wide)), array((8, wide), F32)]

    def scratch(layer):
        wide = length if layer == 0 else width
        return [
            pltpu.VMEM((3 * ch, channels), BF16),
            pltpu.VMEM((3 * ch, wide), BF16),
            pltpu.VMEM((n_tp, ch, wide), BF16),
        ]

    def reduce_tp(products):
        if not paired:
            whole, extra = products
            own = lax.psum_scatter(whole.reshape(channels, -1), TP, scatter_dimension=0, tiled=True)
            return [jnp.concatenate([own.astype(F32), lax.psum(extra, TP)], axis=0)]
        keep, send = products
        wide = keep.shape[2]
        got = swap(send, TP, 1)
        far, rest = array((ch + 16, wide)), array((ch, wide), F32)

        def step(kernel, inputs, shapes, name):
            return pl.pallas_call(
                kernel,
                out_shape=shapes,
                in_specs=[VMEM] * len(inputs),
                out_specs=[VMEM] * len(shapes),
                compiler_params=params(),
                cost_estimate=cost(1, 1),
                name=name,
            )(*inputs)

        own, rest, x, y = step(pair_kernel, [keep, send, got], [array((ch + 8, wide), F32), rest, far, far], "pair")
        shapes = [array((ch + 16, wide), F32), array((ch // 2 + 16, wide)), array((ch // 2, wide))]
        own, y, x = step(relay_kernel, [own, rest, swap(x, TP, 2), swap(y, TP, 4)], shapes, "relay")
        return [own, swap(y, TP, 4), swap(x, TP, 2)]

    upstream, grad2, *products = call(
        functools.partial(junction_kernel, share=share, root=math.sqrt(channels), **sizes),
        [weights, slopes[2], tower_grad, halo_grad, table, *pieces],
        [array((ch, width), F32), array((ch, length))] + product_shapes(2),
        scratch=scratch(2)
        + [
            pltpu.VMEM((ch, count), F32),
            pltpu.VMEM((8, count), F32),
            pltpu.VMEM((ch, length), F32),
            pltpu.VMEM((n_seq, ch + 16, length), BF16),
            pltpu.VMEM((ch, 128), F32),
            pltpu.VMEM(table.shape, F32),
            pltpu.SemaphoreType.DMA((2,)),
            pltpu.SemaphoreType.DMA((n_seq + 3,)),
        ],
        hbm_in=range(5 + n_seq),
        estimate=cost(1, 1),
        mib=32,
        name="junction",
    )

    def backward(layer, sums, upstream):
        state, inverse = stored[layer]
        wide = length if layer == 0 else width
        inputs = [*sums, upstream, state, inverse, gain_cols]
        shapes = [array((ch, wide), F32), array((ch, 128), F32)]
        extra, hbm = [], ()
        if layer > 0:
            inputs = [weights, slopes[layer - 1], *inputs]
            hbm = (0, 1)
            shapes.append(array((ch, length)))
            if layer == LAYERS - 1:
                shapes.append(array((8, width), F32))
            shapes += product_shapes(layer - 1)
            extra = scratch(layer - 1) + [pltpu.SemaphoreType.DMA((2,))]
        return call(
            functools.partial(backward_kernel, layer=layer, n_far=n_far, length=length, **sizes),
            inputs,
            shapes,
            scratch=extra,
            hbm_in=hbm,
            estimate=cost(1, 1),
            name="backward",
        )

    def weigh(layer, path, grads, sources, before):
        inputs = [*grads, *sources, *before]
        return call(
            functools.partial(weight_kernel, layer=layer, path=path, **sizes),
            inputs,
            [array((LAYERS, 3, ch, channels), F32)],
            scratch=[
                pltpu.VMEM((ch, total), BF16),
                pltpu.VMEM((3 * ch, total), BF16),
                pltpu.VMEM((channels // CHUNK, CHUNK // ch, ch, total), BF16),
                pltpu.VMEM((2, 3, ch, CHUNK), F32),
                pltpu.SemaphoreType.DMA((channels // CHUNK, n_seq * (CHUNK // ch))),
                pltpu.SemaphoreType.DMA((2,)),
            ],
            hbm_in=range(n_seq, len(inputs)),
            hbm_out=(0,),
            estimate=cost(6 * ch * channels * total, 2 * channels * total),
            mib=32,
            input_output_aliases={len(inputs): 0} if before else {},
            name="weight",
        )[0]

    sums = reduce_tp(products)
    grads2 = gather_seq(grad2)
    if planned:
        sums, seq2[1:3] = tie(sums, seq2[1:3])
        seq2[3] = swap(seq2[2], "seq", 1)
    upstream, part2, grad1, score_rows, *products = backward(2, sums, upstream)
    scores = score_rows[1, :share]

    grads1 = gather_seq(grad1)
    sums = reduce_tp(products)
    if planned:
        near0 = swap(every0, TP, 1)
        sums, got = tie(sums, [every0, near0, *seq2, *grads1[1:3]])
        (every0, near0), seq2, grads1[1:3] = got[:2], got[2 : 2 + n_seq], got[2 + n_seq :]
        grads1[3] = swap(grads1[2], "seq", 1)
        every2 = collect(seq2)
    upstream, part1, grad0, *products = backward(1, sums, upstream)

    grads0 = gather_seq(grad0)
    sums = reduce_tp(products)
    if planned:
        near1 = swap(every1, TP, 1)
        sums, got = tie(sums, [*grads1, every1, near1, *grads0[1:3]])
        grads1, (every1, near1), grads0[1:3] = got[:n_seq], got[n_seq : n_seq + 2], got[n_seq + 2 :]
        grads0[3] = swap(grads0[2], "seq", 1)
    input_grad, part0 = backward(0, sums, upstream)

    columns = jnp.pad(jnp.stack([p[:, 0] for p in (part0, part1, part2)]), ((0, 8 - LAYERS), (0, 0)))
    pieces = gather_seq(columns)
    if len(pieces) == 4:
        gain_grad = (pieces[0] + pieces[1]) + (pieces[2] + pieces[3])
    else:
        gain_grad = sum(pieces)

    if planned:
        grads1, _ = tie(grads1, [part0])
        weight_grad = weigh(1, "pair", grads1, [every1, near1], [])
        (every2, *grads2[1:3]), (weight_grad,) = tie([every2, *grads2[1:3]], [weight_grad])
        grads0, got = tie(grads0, [gain_grad, every2, *grads2[1:3]])
        (gain_grad, every2), grads2[1:3] = got[:2], got[2:]
        grads2[3] = swap(grads2[2], "seq", 1)
        weight_grad = weigh(0, "pair", grads0, [every0, near0], [weight_grad])
        weight_grad = weigh(2, "pair", grads2, [every2, swap(every2, TP, 1)], [weight_grad])
    else:
        weight_grad = weigh(0, "whole", grads0, everything[0], [])
        weight_grad = weigh(1, "whole", grads1, everything[1], [weight_grad])
        weight_grad = weigh(2, "whole", grads2, everything[2], [weight_grad])
    return (scores, input_grad, weight_grad.transpose(0, 2, 1, 3), gain_grad[:LAYERS])


def solution(mesh):
    tp = mesh.shape["tp"]
    pairs = jax.sharding.Mesh(mesh.devices.reshape(mesh.shape["seq"], tp // 2, 2), ("seq",) + TP)
    return jax.shard_map(
        local,
        mesh=pairs,
        in_specs=(
            P(TP, "seq"),
            P(None, TP, None, None),
            P(None, TP),
            P(),
            P("seq"),
            P("seq", None),
            P("seq"),
            P("seq"),
            P(TP, "seq"),
            P("seq"),
        ),
        out_specs=(P("seq"), P(TP, "seq"), P(None, TP, None, None), P(None, TP)),
        check_vma=False,
    )
```

```python
import functools
import math

import jax
import jax.numpy as jnp
from jax import lax
from jax.experimental import pallas as pl
from jax.experimental.pallas import tpu as pltpu
from jax.sharding import PartitionSpec as P

LAYERS = 3
EPSILON = 1e-06
EDGE = 64
SPARE = 56
CHUNK = 384
ROWS = 16
K0 = math.sqrt(2.0 / math.pi)
K1 = K0 * 0.044715
F32 = jnp.float32
BF16 = jnp.bfloat16

VMEM = pl.BlockSpec(memory_space=pltpu.VMEM)
SMEM = pl.BlockSpec(memory_space=pltpu.SMEM)
HBM = pl.BlockSpec(memory_space=pltpu.HBM)

TP = ("pair", "side")


def params(mib=24):
    return pltpu.CompilerParams(vmem_limit_bytes=mib * 1024 * 1024)


def cost(flops, nbytes, special=0):
    return pl.CostEstimate(flops=flops, bytes_accessed=nbytes, transcendentals=special)


def tie(first, then):
    out = lax.optimization_barrier((tuple(first), tuple(then)))
    return list(out[0]), list(out[1])


def reach_of(layer):
    return 2 ** (layer + 3)


def size_of(axis):
    return math.prod(lax.axis_size(name) for name in axis) if isinstance(axis, tuple) else lax.axis_size(axis)


def swap(x, axis, mask):
    return lax.ppermute(x, axis, [(i, i ^ mask) for i in range(size_of(axis))])


def gather_tp(x):
    if size_of(TP) == 8:
        half = x.shape[0] // 2
        along_x, along_y = swap(x, TP, 2), swap(x, TP, 4)
        corner = [swap(along_x[:half], TP, 4), swap(along_y[half:], TP, 2)]
        far = [x, along_x, along_y, *corner]
        near = [swap(v, TP, 1) for v in far]
        return far + near
    whole = lax.all_gather(x, TP, axis=0)
    return [whole[i] for i in range(whole.shape[0])]


def tp_order(me):
    count = size_of(TP)
    steps = jnp.arange(count, dtype=jnp.int32)
    return me ^ steps if count == 8 else steps


def gather_seq(x):
    if size_of("seq") == 4:
        one, two = swap(x, "seq", 1), swap(x, "seq", 2)
        return [x, one, two, swap(two, "seq", 1)]
    whole = lax.all_gather(x, "seq", axis=0)
    return [whole[i] for i in range(whole.shape[0])]


def seq_order(me):
    count = size_of("seq")
    steps = jnp.arange(count, dtype=jnp.int32)
    return me ^ steps if count == 4 else steps


def roll(x, shift):
    shift = shift % x.shape[1]
    return x if shift == 0 else pltpu.roll(x, shift, 1)


def position(shape, dim, length):
    at = lax.broadcasted_iota(jnp.int32, shape, dim)
    return jnp.where(at < length + EDGE, at, at - (length + 2 * EDGE))


def in_sequence(seq_at, width, length, total):
    at = position((1, width), 1, length) + seq_at * length
    return (at >= 0) & (at < total)


def stack_kernel(*refs):
    *pieces, out_ref, sems = refs
    rows = out_ref.shape[0] // len(pieces)
    copies = [
        pltpu.make_async_copy(piece.at[:rows], out_ref.at[i * rows : (i + 1) * rows], sems.at[i])
        for i, piece in enumerate(pieces)
    ]
    for copy in copies:
        copy.start()
    for copy in copies:
        copy.wait()


def record_kernel(donor_ref, owner_ref, accept_ref, tissue_ref, grad_ref, out_ref, *, span):
    row = lax.broadcasted_iota(jnp.int32, (16, out_ref.shape[1]), 0)
    out = jnp.zeros(row.shape, F32)
    values = []
    for x in (donor_ref[...], owner_ref[...] * span + accept_ref[...], tissue_ref[...]):
        values += [(x >> 8).astype(F32), (x & 255).astype(F32)]
    grad = grad_ref[...]
    high = grad.astype(BF16).astype(F32)
    middle = (grad - high).astype(BF16).astype(F32)
    values += [high, middle, grad - high - middle]
    for k, value in enumerate(values):
        value = jnp.concatenate([value, jnp.zeros((1, row.shape[1] - value.shape[1]), F32)], axis=1)
        out = jnp.where(row == k, value, out)
    out_ref[...] = out.astype(BF16)


def edge_kernel(meta, seq_ref, tower_ref, first_ref, second_ref, states, grads, sems, *, n_tp, n_seq):
    ch, length = seq_ref.shape
    copies = []
    for i, start in enumerate((0, length - 128)):
        copies.append(pltpu.make_async_copy(seq_ref.at[:, start : start + 128], states.at[i], sems.at[2 * i]))
        copies.append(pltpu.make_async_copy(tower_ref.at[:, start : start + 128], grads.at[i], sems.at[2 * i + 1]))
    for copy in copies:
        copy.start()
    for copy in copies:
        copy.wait()
    even = lax.rem(meta[n_tp + n_seq + 1], 2) == 0
    low = lax.broadcasted_iota(jnp.int32, (ch, 128), 1) < EDGE

    def pack(state, grad):
        high = grad.astype(BF16).astype(F32)
        return [jnp.where(low, state, roll(high, EDGE)), jnp.where(low, grad - high, 0.0)]

    left = pack(states[0].astype(F32), grads[0])
    right = pack(roll(states[1].astype(F32), EDGE), roll(grads[1], EDGE))
    for i in range(2):
        first_ref[:, i * 128 : (i + 1) * 128] = jnp.where(even, right[i], left[i]).astype(BF16)
        second_ref[:, i * 128 : (i + 1) * 128] = jnp.where(even, left[i], right[i]).astype(BF16)


def window_kernel(
    meta, seq_ref, first_ref, second_ref, gain_ref, state_ref, halo_ref, held, sem, *, n_tp, n_seq
):
    ch, length = held.shape
    copy = pltpu.make_async_copy(seq_ref, held, sem)
    copy.start()
    even = lax.rem(meta[n_tp + n_seq + 1], 2) == 0
    first = first_ref[...].astype(F32)
    second = second_ref[...].astype(F32)
    right = jnp.where(even, first, second)
    left = jnp.where(even, second, first)
    lane = lax.broadcasted_iota(jnp.int32, (ch, 128), 1)
    low = lane < EDGE
    halo = jnp.where(low, right[:, :128], roll(left[:, :128], EDGE))
    gains = gain_ref[...]
    high = gains.astype(BF16).astype(F32)
    rest = gains - high
    middle = rest.astype(BF16).astype(F32)
    for k, part in enumerate((high, middle, rest - middle)):
        for layer in range(LAYERS):
            halo = jnp.where(lane == SPARE + k * LAYERS + layer, part[:, layer : layer + 1], halo)
    state_ref[:, length:] = halo.astype(BF16)
    th = jnp.where(low, roll(right[:, :128], EDGE), left[:, :128])
    tl = jnp.where(low, right[:, 128:], roll(left[:, 128:], EDGE))
    halo_ref[...] = th + tl
    copy.wait()
    state_ref[:, :length] = held[...]


def chunks_of(refs, n_tp, ch):
    half = ch // 2
    count = 10 if n_tp == 8 else n_tp
    places = (0, 2, 4, 6, 6, 1, 3, 5, 7, 7) if n_tp == 8 else range(n_tp)
    chunks = []
    for i, place in enumerate(places):
        if refs[i].shape[0] == ch:
            chunks += [(place, refs[i], 0, 0), (place, refs[i], half, half)]
        else:
            chunks.append((place, refs[i], 0, half * (i % 5 - 3)))
    return chunks, refs[count:]


def forward_kernel(meta, w_ref, own_ref, *refs, layer, n_tp, n_seq, length):
    *refs, held, slopes, weights, sems = refs
    chunks, refs = chunks_of(refs, n_tp, held.shape[1])
    if layer == 0:
        state_ref, slope_ref, inverse_ref, hidden_ref, gain_ref = refs
    elif layer < LAYERS - 1:
        gain_ref, state_ref, slope_ref, inverse_ref, hidden_ref = refs
    else:
        gain_ref, digit_ref, state_ref, slope_ref, inverse_ref, hidden_ref = refs
    _, ch, width = held.shape
    wide = slopes.shape[2]
    channels = ch * n_tp
    reach = reach_of(layer)
    me, seq_at = meta[n_tp + n_seq], meta[n_tp + n_seq + 1]
    copy = pltpu.make_async_copy(w_ref.at[layer], weights, sems.at[0])
    copy.start()

    def add_power(j, acc):
        for _, ref, start, _ in chunks:
            x = ref[pl.ds(pl.multiple_of(start + j * ROWS, ROWS), ROWS), :].astype(F32)
            sq = x * x
            for i in range(0, ROWS, 8):
                acc = acc + sq[i : i + 8]
        return acc

    acc = lax.fori_loop(0, ch // (2 * ROWS), add_power, jnp.zeros((8, width), F32))
    power = jnp.sum(acc, axis=0, keepdims=True) / channels
    inverse = 1.0 / jnp.sqrt(power + EPSILON)
    inverse_ref[...] = jnp.broadcast_to(inverse, (8, width))

    def activate(j, carry):
        for m, ref, start, place in chunks:
            at = meta[m]
            x = ref[pl.ds(pl.multiple_of(start + j * ROWS, ROWS), ROWS), :].astype(F32)
            rows = pl.ds(pl.multiple_of(place + j * ROWS, ROWS), ROWS)
            if layer == 0:
                halo = x[:, length:]
                cols = [
                    halo[:, SPARE + l : SPARE + l + 1]
                    + (
                        halo[:, SPARE + LAYERS + l : SPARE + LAYERS + l + 1]
                        + halo[:, SPARE + 2 * LAYERS + l : SPARE + 2 * LAYERS + l + 1]
                    )
                    for l in range(LAYERS)
                ]
                lane = lax.broadcasted_iota(jnp.int32, (ROWS, 128), 1)
                gain_ref[at, rows, :] = jnp.where(lane == 0, cols[0], jnp.where(lane == 1, cols[1], cols[2]))
                gain = cols[0]
            else:
                gain = gain_ref[at, rows, layer : layer + 1]
            scaled = x * gain
            pre = scaled * inverse
            sq = pre * pre
            th = jnp.tanh(pre * (K0 + K1 * sq))
            half = 0.5 + 0.5 * th
            hidden = pre * half
            held[at, rows, :] = hidden.astype(BF16)
            slope = half + (hidden - hidden * th) * (K0 + (3.0 * K1) * sq)
            slopes[at, rows, :] = (slope * scaled)[:, :wide].astype(BF16)
        return carry

    lax.fori_loop(0, ch // (2 * ROWS), activate, 0)
    leave = pltpu.make_async_copy(slopes, slope_ref, sems.at[1])
    leave.start()
    hidden_ref[...] = held[me, :, :length]
    copy.wait()
    every = held[...].reshape(channels, width)
    total = own_ref[...].astype(F32)
    for tap in range(3):
        part = jnp.dot(weights[tap * ch : (tap + 1) * ch, :], every, preferred_element_type=F32)
        total = total + roll(part, (1 - tap) * reach)
    total = jnp.where(in_sequence(seq_at, width, length, n_seq * length), total, 0.0).astype(BF16)
    if layer < LAYERS - 1:
        state_ref[...] = total
    else:
        state_ref[:ch, :] = total[:, :length]
        state_ref[ch:, :] = digit_ref[...]
    leave.wait()


def send_back(layer, upstream, meta, weights, slopes, taps, grad_ref, out_refs, score, n_tp, n_seq, length):
    ch, width = upstream.shape
    wide = taps.shape[1]
    reach = reach_of(layer)
    me, seq_at = meta[n_tp + n_seq], meta[n_tp + n_seq + 1]
    grad = jnp.where(in_sequence(seq_at, width, length, n_seq * length), upstream, 0.0)
    grad = grad.astype(BF16).astype(F32)
    grad_ref[...] = grad[:, :length].astype(BF16)
    for tap in range(3):
        taps[tap * ch : (tap + 1) * ch, :] = roll(grad, (tap - 1) * reach)[:, :wide].astype(BF16)
    for copy in slopes[1:]:
        copy.wait()
    inner = jnp.zeros((8, wide), F32)
    parts = CHUNK // ch
    chunks = ch * n_tp // CHUNK
    for r in range(chunks):
        at = (me // 2) ^ r if n_tp == 8 else r
        cols = pl.ds(pl.multiple_of(at * CHUNK, 128), CHUNK)
        part = lax.dot_general(weights[:, cols], taps[...], (((0,), (0,)), ((), ())), preferred_element_type=F32)
        for q in range(parts):
            prod = part[q * ch : (q + 1) * ch] * slopes[0][at * parts + q].astype(F32)
            inner = inner + jnp.sum(prod.reshape(ch // 8, 8, wide), axis=0)
        if n_tp == 8:
            keep_ref, send_ref = out_refs
            zero = lax.rem(me, 2) == 0
            keep_ref[r] = jnp.where(zero, part[:ch], part[ch:]).astype(BF16)
            send_ref[r * ch : (r + 1) * ch, :] = jnp.where(zero, part[ch:], part[:ch]).astype(BF16)
        else:
            for q in range(parts):
                out_refs[0][at * parts + q] = part[q * ch : (q + 1) * ch].astype(BF16)
    row = lax.broadcasted_iota(jnp.int32, (8, wide), 0)
    extra = jnp.where(row == 0, jnp.sum(inner, axis=0, keepdims=True), 0.0)
    if score is not None:
        score = jnp.concatenate([score, jnp.zeros((1, wide - score.shape[1]), F32)], axis=1)
        extra = jnp.where(row == 1, score, extra)
    if n_tp == 8:
        out_refs[1][n_tp // 2 * ch :, :] = split_rows(extra)
    else:
        out_refs[1][...] = extra


def split_rows(x):
    high = x.astype(BF16).astype(F32)
    return jnp.concatenate([high, x - high], axis=0).astype(BF16)


def join_rows(x):
    x = x.astype(F32)
    return x[:8] + x[8:]


def bring(sources, targets, sems):
    copies = [pltpu.make_async_copy(source, target, sems.at[i]) for i, (source, target) in enumerate(zip(sources, targets))]
    for copy in copies:
        copy.start()
    return copies


def fetch(layer, w_ref, slope_ref, weights, slopes, sems):
    copies = [
        pltpu.make_async_copy(w_ref.at[layer], weights, sems.at[0]),
        pltpu.make_async_copy(slope_ref, slopes, sems.at[1]),
    ]
    for copy in copies:
        copy.start()
    return [slopes] + copies


def junction_kernel(meta, w_ref, slope_ref, tower_ref, halo_ref, table_ref, *refs, n_tp, n_seq, share, root):
    pieces, refs = refs[:n_seq], refs[n_seq:]
    up_ref, grad_ref, *refs = refs
    *out_refs, weights, taps, slopes, donors, rec_ref, tower, columns, halo, tissues, sems, small_sems = refs
    ch, length = tower.shape
    width = length + 2 * EDGE
    count = share * n_seq
    copies = bring(
        [*pieces, table_ref, halo_ref, tower_ref],
        [columns.at[m] for m in range(n_seq)] + [tissues, halo, tower],
        small_sems,
    )
    seq_at = meta[n_tp + n_seq + 1]
    slopes = fetch(LAYERS - 1, w_ref, slope_ref, weights, slopes, sems)
    for copy in copies[: n_seq + 1]:
        copy.wait()
    for m in range(n_seq):
        at = meta[n_tp + m]
        digits = columns[m, ch:, :share].astype(F32)
        row = lax.broadcasted_iota(jnp.int32, (8, share), 0)
        first = (digits[0:1] * 256.0 + digits[1:2]) + (at * length).astype(F32)
        second = digits[2:3] * 256.0 + digits[3:4]
        third = digits[4:5] * 256.0 + digits[5:6]
        fourth = digits[6:7] + (digits[7:8] + digits[8:9])
        record = jnp.where(row == 0, first, jnp.where(row == 1, second, jnp.where(row == 2, third, fourth)))
        rec_ref[:, pl.ds(pl.multiple_of(at * share, 128), share)] = record
    table = tissues[...]
    high = table.astype(BF16)
    rest = table - high.astype(F32)
    middle = rest.astype(BF16)
    last = (rest - middle.astype(F32)).astype(BF16)
    hit = lax.broadcasted_iota(jnp.int32, (table.shape[0], count), 0) == rec_ref[2:3, :].astype(jnp.int32)
    hit = jnp.where(hit, 1.0, 0.0).astype(BF16)
    rows = sum(
        lax.dot_general(part, hit, (((0,), (0,)), ((), ())), preferred_element_type=F32)
        for part in (last, middle, high)
    )
    donor = rec_ref[0:1, :].astype(jnp.int32)
    accept = rec_ref[1:2, :].astype(jnp.int32)
    weight = rec_ref[3:4, :] / root
    place = lax.broadcasted_iota(jnp.int32, (length, count), 0)
    accepts = jnp.zeros((ch, count), F32)
    for m in range(n_seq):
        at = meta[n_tp + m]
        cols = pl.ds(pl.multiple_of(at * share, 128), share)
        block = columns[m, :ch, :]
        mine = rec_ref[0:1, cols].astype(jnp.int32) - at * length
        hit = lax.broadcasted_iota(jnp.int32, (length, share), 0) == mine
        donors[:, cols] = jnp.dot(block, jnp.where(hit, 1.0, 0.0).astype(BF16), preferred_element_type=F32)
        hit = place == accept - at * length
        accepts = accepts + jnp.dot(block, jnp.where(hit, 1.0, 0.0).astype(BF16), preferred_element_type=F32)
    product = donors[...] * accepts * rows
    scored = jnp.sum(product, axis=0, keepdims=True) / root
    score = jnp.zeros((1, share), F32)
    for m in range(n_seq):
        score = jnp.where(seq_at == m, scored[:, m * share : (m + 1) * share], score)
    scale = rows * weight
    for copy in copies[n_seq + 1 :]:
        copy.wait()
    upstream = jnp.concatenate([tower[...], halo[...]], axis=1)
    spot = position((width, count), 0, length) + seq_at * length
    for values, where in ((accepts * scale, donor), (donors[...] * scale, accept)):
        high = values.astype(BF16)
        low = (values - high.astype(F32)).astype(BF16)
        hit = jnp.where(spot == where, 1.0, 0.0).astype(BF16)
        both = lax.dot_general(
            jnp.concatenate([high, low], axis=0), hit, (((1,), (1,)), ((), ())), preferred_element_type=F32
        )
        upstream = upstream + (both[:ch] + both[ch:])
    up_ref[...] = upstream
    send_back(LAYERS - 1, upstream, meta, weights, slopes, taps, grad_ref, out_refs, score, n_tp, n_seq, length)


def pair_kernel(keep_ref, send_ref, got_ref, own_ref, rest_ref, *far_refs):
    count, ch, width = keep_ref.shape
    half = ch // 2
    extra = join_rows(send_ref[count * ch :, :]) + join_rows(got_ref[count * ch :, :])
    split = split_rows(extra)
    own_ref[ch:, :] = join_rows(split)

    def total(r, k):
        rows = slice(k * half, (k + 1) * half)
        got = got_ref[r * ch + k * half : r * ch + (k + 1) * half, :]
        return keep_ref[r, rows, :].astype(F32) + got.astype(F32)

    for k in range(2):
        own_ref[k * half : (k + 1) * half, :] = total(0, k)
        far_refs[k][:half, :] = total(1 + k, k).astype(BF16)
        far_refs[k][half:ch, :] = total(3, k).astype(BF16)
        far_refs[k][ch:, :] = split
        rest_ref[k * half : (k + 1) * half, :] = total(2 - k, k)


def relay_kernel(own_ref, rest_ref, x_ref, y_ref, sum_ref, *far_refs):
    ch = rest_ref.shape[0]
    half = ch // 2
    for k, ref in enumerate((x_ref, y_ref)):
        rows = slice(k * half, (k + 1) * half)
        sum_ref[rows, :] = own_ref[rows, :] + ref[:half, :].astype(F32)
        far_refs[k][:half, :] = (rest_ref[rows, :] + ref[half:ch, :].astype(F32)).astype(BF16)
    far_refs[0][half:, :] = x_ref[ch:, :]
    sum_ref[ch : ch + 8, :] = own_ref[ch:, :] + join_rows(x_ref[ch:, :])
    sum_ref[ch + 8 :, :] = join_rows(y_ref[ch:, :])


def backward_kernel(meta, *refs, layer, n_far, n_tp, n_seq, length):
    last = layer == 0
    if last:
        slopes = None
    else:
        w_ref, slope_ref, *refs = refs
        *refs, weights, taps, slopes, sems = refs
        slopes = fetch(layer - 1, w_ref, slope_ref, weights, slopes, sems)
    own_ref, refs = refs[0], refs[1:]
    far, refs = refs[:n_far], refs[n_far:]
    up_ref, state_ref, inverse_ref, gain_ref, *refs = refs
    out_ref, part_ref, *refs = refs
    if not last:
        grad_ref, *out_refs = refs
        if layer == LAYERS - 1:
            score_ref, *out_refs = out_refs
    ch, width = state_ref.shape
    channels = ch * n_tp
    half = ch // 2
    extra = own_ref[ch : ch + 8, :]
    if n_far:
        extra = extra + (own_ref[ch + 8 :, :] + join_rows(far[0][half:, :]))
    inner = extra[0:1, :]
    if layer == LAYERS - 1:
        score_ref[...] = extra
    inverse = inverse_ref[0:1, :width]
    gain = gain_ref[:, layer : layer + 1]
    back = own_ref[:ch, :]
    if n_far:
        back = back + jnp.concatenate([f[:half, :] for f in far], axis=0).astype(F32)
    x = state_ref[...].astype(F32)
    pre = x * gain * inverse
    sq = pre * pre
    th = jnp.tanh(pre * (K0 + K1 * sq))
    half = 0.5 + 0.5 * th
    back = back * (half + (pre * half) * (1.0 - th) * (K0 + (3.0 * K1) * sq))
    mine = back * x * inverse
    part = jnp.sum(mine[:, :length], axis=1, keepdims=True)
    part_ref[...] = jnp.broadcast_to(part, part_ref.shape)
    upstream = up_ref[:, :width] + (inverse * gain) * back - x * (inverse * inverse * inverse * inner / channels)
    out_ref[...] = upstream
    if not last:
        send_back(layer - 1, upstream, meta, weights, slopes, taps, grad_ref, out_refs, None, n_tp, n_seq, length)


def weight_kernel(meta, *refs, layer, path, n_tp, n_seq):
    pieces, refs = refs[:n_seq], refs[n_seq:]
    *sources, out_ref, whole, taps, held, done, in_sems, out_sems = refs
    ch, length = whole.shape[0], pieces[0].shape[1]
    start = pieces[0].shape[0] - ch
    reach = reach_of(layer)
    total = n_seq * length
    parts = CHUNK // ch
    chunks = ch * n_tp // CHUNK
    me = meta[n_tp + n_seq]
    core = lax.rem(me, 2)

    def chunk_at(r):
        return r if path == "whole" else (me // 2) ^ r

    def lanes(m):
        return pl.ds(pl.multiple_of(meta[n_tp + m] * length, 128), length)

    def arrive(r):
        copies = []

        def add(source, side, where):
            copies.append(
                pltpu.make_async_copy(source, held.at[r, side, :, where], in_sems.at[r, len(copies)])
            )

        if path == "whole":
            for s in range(n_seq):
                for q in range(parts):
                    add(sources[0].at[s, r * parts + q], q, pl.ds(s * length, length))
        else:
            for m in range(n_seq):
                for q in range(2):
                    source = sources[q].at[chunk_at(r), m]
                    add(source, core if q == 0 else 1 - core, lanes(m))
        return copies

    def leave(r):
        cols = pl.ds(pl.multiple_of(chunk_at(r) * CHUNK, 128), CHUNK)
        return pltpu.make_async_copy(done.at[r % 2], out_ref.at[layer, :, :, cols], out_sems.at[r % 2])

    for r in range(chunks):
        for copy in arrive(r):
            copy.start()
    for m in range(n_seq):
        whole[:, lanes(m)] = pieces[m][start:, :]
    grad = whole[...].astype(F32)
    lane = lax.broadcasted_iota(jnp.int32, (1, total), 1)
    taps[:ch, :] = jnp.where(lane < total - reach, roll(grad, -reach), 0.0).astype(BF16)
    taps[ch : 2 * ch, :] = whole[...]
    taps[2 * ch :, :] = jnp.where(lane >= reach, roll(grad, reach), 0.0).astype(BF16)
    for r in range(chunks):
        for copy in arrive(r):
            copy.wait()
        if r >= 2:
            leave(r - 2).wait()
        product = lax.dot_general(
            taps[...], held[r].reshape(CHUNK, total), (((1,), (1,)), ((), ())), preferred_element_type=F32
        )
        done[r % 2] = product.reshape(3, ch, CHUNK)
        leave(r).start()
    for r in range(max(0, chunks - 2), chunks):
        leave(r).wait()


def local(
    sequence_in,
    conv_weight,
    norm_gain,
    tissue_scale,
    donor_offset,
    acceptor_owner,
    acceptor_offset,
    tissue,
    tower_grad,
    score_grad,
):
    ch, length = sequence_in.shape
    n_tp, n_seq = size_of(TP), size_of("seq")
    channels, total = ch * n_tp, length * n_seq
    width = length + 2 * EDGE
    share = donor_offset.shape[0]
    count = share * n_seq
    paired = n_tp == 8
    n_far = 2 if paired else 0
    me = lax.axis_index(TP).astype(jnp.int32)
    seq_at = lax.axis_index("seq").astype(jnp.int32)
    meta = jnp.concatenate([tp_order(me), seq_order(seq_at), jnp.stack([me, seq_at])])
    sizes = dict(n_tp=n_tp, n_seq=n_seq)
    weights = conv_weight.transpose(0, 2, 1, 3).reshape(LAYERS, 3 * ch, channels)
    conv_flops = 6 * ch * channels * width

    def call(kernel, inputs, shapes, scratch=(), hbm_in=(), hbm_out=(), estimate=None, mib=24, **kw):
        inputs = [pltpu.with_memory_space_constraint(x, pltpu.HBM) if i in hbm_in else x for i, x in enumerate(inputs)]
        return pl.pallas_call(
            kernel,
            out_shape=[pltpu.HBM(x.shape, x.dtype) if i in hbm_out else x for i, x in enumerate(shapes)],
            in_specs=[SMEM] + [HBM if i in hbm_in else VMEM for i in range(len(inputs))],
            out_specs=[HBM if i in hbm_out else VMEM for i in range(len(shapes))],
            scratch_shapes=list(scratch),
            compiler_params=params(mib),
            cost_estimate=estimate,
            **kw,
        )(meta, *inputs)

    def array(shape, dtype=BF16):
        return jax.ShapeDtypeStruct(shape, dtype)

    edges = array((ch, 256))
    first, second = call(
        functools.partial(edge_kernel, **sizes),
        [sequence_in, tower_grad],
        [edges, edges],
        scratch=[pltpu.VMEM((2, ch, 128), BF16), pltpu.VMEM((2, ch, 128), F32), pltpu.SemaphoreType.DMA((4,))],
        hbm_in=(0, 1),
        name="edge",
    )
    pairs = [(i, i + 1) for i in range(1, n_seq - 1, 2)]
    first = lax.ppermute(first, "seq", [(i, i ^ 1) for i in range(n_seq)])
    second = lax.ppermute(second, "seq", pairs + [(j, i) for i, j in pairs])
    gain_cols = jnp.pad(norm_gain.T, ((0, 0), (0, 128 - LAYERS)))
    state, halo_grad = call(
        functools.partial(window_kernel, **sizes),
        [sequence_in, first, second, gain_cols],
        [array((ch, width)), array((ch, 128), F32)],
        scratch=[pltpu.VMEM((ch, length), BF16), pltpu.SemaphoreType.DMA],
        hbm_in=(0,),
        name="window",
    )

    record = pl.pallas_call(
        functools.partial(record_kernel, span=length),
        out_shape=array((16, length)),
        in_specs=[VMEM] * 5,
        out_specs=VMEM,
        compiler_params=params(),
        name="record",
    )(*(x.reshape(1, share) for x in (donor_offset, acceptor_owner, acceptor_offset, tissue, score_grad)))
    table = lax.dynamic_slice_in_dim(tissue_scale, me * ch, ch, 1)
    table = jnp.pad(table, ((0, -table.shape[0] % 128), (0, 0)))

    def forward(layer, own, extra, blocks=None):
        wide = length if layer == 0 else width
        final = layer == LAYERS - 1
        shapes = [
            array((ch + 16, length) if final else (ch, width)),
            array((n_tp, ch, wide)),
            array((8, width), F32),
            array((ch, length)),
        ]
        if layer == 0:
            shapes.append(array((n_tp, ch, 128), F32))
        return call(
            functools.partial(forward_kernel, layer=layer, length=length, **sizes),
            [weights, own, *(gather_tp(own) if blocks is None else blocks), *extra],
            shapes,
            scratch=[
                pltpu.VMEM((n_tp, ch, width), BF16),
                pltpu.VMEM((n_tp, ch, wide), BF16),
                pltpu.VMEM((3 * ch, channels), BF16),
                pltpu.SemaphoreType.DMA((2,)),
            ],
            hbm_in=(0,),
            hbm_out=(1,),
            estimate=cost(1, 1),
            name="forward",
        )

    state1, slope0, inverse0, hidden0, gains = forward(0, state, [])
    planned = paired and n_seq == 4
    blocks = gather_tp(state1)
    if planned:
        seq0 = gather_seq(hidden0)
        blocks, seq0[1:3] = tie(blocks, seq0[1:3])
        seq0[3] = swap(seq0[2], "seq", 1)
    state2, slope1, inverse1, hidden1 = forward(1, state1, [gains], blocks)
    def collect(blocks):
        block = pl.pallas_call(
            stack_kernel,
            out_shape=pltpu.HBM((n_seq * ch, length), BF16),
            in_specs=[pl.BlockSpec(memory_space=pl.ANY)] * n_seq,
            out_specs=HBM,
            scratch_shapes=[pltpu.SemaphoreType.DMA((n_seq,))],
            compiler_params=params(),
            cost_estimate=cost(1, 1),
            name="stack",
        )(*blocks)
        return lax.all_gather(block, "pair", axis=0).reshape(n_tp // 2, n_seq, ch, length)

    if planned:
        seq0, _ = tie(seq0, [state2])
        every0 = collect(seq0)
    blocks = gather_tp(state2)
    if planned:
        seq1 = gather_seq(hidden1)
        blocks, seq1[1:3] = tie(blocks, seq1[1:3])
        seq1[3] = swap(seq1[2], "seq", 1)
    state3, slope2, inverse2, hidden2 = forward(2, state2, [gains, record], blocks)
    slopes = [slope0, slope1, slope2]
    stored = [(sequence_in, inverse0), (state1, inverse1), (state2, inverse2)]
    if planned:
        one, two = swap(state3, "seq", 1), swap(state3, "seq", 2)
        (two,), (one,) = tie([two], [one])
        pieces = [state3, one, two, swap(two, "seq", 1)]
        seq1, pieces[2:3] = tie(seq1, pieces[2:3])
        every1 = collect(seq1)
        pieces, (hidden2,) = tie(pieces, [hidden2])
        seq2 = gather_seq(hidden2)
    else:
        pieces = gather_seq(state3)
        everything = [
            [lax.all_gather(h, ("seq",) + TP, axis=0).reshape(n_seq, n_tp, ch, length)]
            for h in (hidden0, hidden1, hidden2)
        ]

    def product_shapes(layer):
        wide = length if layer == 0 else width
        if paired:
            return [array((n_tp // 2, ch, wide)), array((n_tp // 2 * ch + 16, wide))]
        return [array((n_tp, ch, wide)), array((8, wide), F32)]

    def scratch(layer):
        wide = length if layer == 0 else width
        return [
            pltpu.VMEM((3 * ch, channels), BF16),
            pltpu.VMEM((3 * ch, wide), BF16),
            pltpu.VMEM((n_tp, ch, wide), BF16),
        ]

    def reduce_tp(products):
        if not paired:
            whole, extra = products
            own = lax.psum_scatter(whole.reshape(channels, -1), TP, scatter_dimension=0, tiled=True)
            return [jnp.concatenate([own.astype(F32), lax.psum(extra, TP)], axis=0)]
        keep, send = products
        wide = keep.shape[2]
        got = swap(send, TP, 1)
        far, rest = array((ch + 16, wide)), array((ch, wide), F32)

        def step(kernel, inputs, shapes, name):
            return pl.pallas_call(
                kernel,
                out_shape=shapes,
                in_specs=[VMEM] * len(inputs),
                out_specs=[VMEM] * len(shapes),
                compiler_params=params(),
                cost_estimate=cost(1, 1),
                name=name,
            )(*inputs)

        own, rest, x, y = step(pair_kernel, [keep, send, got], [array((ch + 8, wide), F32), rest, far, far], "pair")
        shapes = [array((ch + 16, wide), F32), array((ch // 2 + 16, wide)), array((ch // 2, wide))]
        own, y, x = step(relay_kernel, [own, rest, swap(x, TP, 2), swap(y, TP, 4)], shapes, "relay")
        return [own, swap(y, TP, 4), swap(x, TP, 2)]

    upstream, grad2, *products = call(
        functools.partial(junction_kernel, share=share, root=math.sqrt(channels), **sizes),
        [weights, slopes[2], tower_grad, halo_grad, table, *pieces],
        [array((ch, width), F32), array((ch, length))] + product_shapes(2),
        scratch=scratch(2)
        + [
            pltpu.VMEM((ch, count), F32),
            pltpu.VMEM((8, count), F32),
            pltpu.VMEM((ch, length), F32),
            pltpu.VMEM((n_seq, ch + 16, length), BF16),
            pltpu.VMEM((ch, 128), F32),
            pltpu.VMEM(table.shape, F32),
            pltpu.SemaphoreType.DMA((2,)),
            pltpu.SemaphoreType.DMA((n_seq + 3,)),
        ],
        hbm_in=range(5 + n_seq),
        estimate=cost(1, 1),
        mib=32,
        name="junction",
    )

    def backward(layer, sums, upstream):
        state, inverse = stored[layer]
        wide = length if layer == 0 else width
        inputs = [*sums, upstream, state, inverse, gain_cols]
        shapes = [array((ch, wide), F32), array((ch, 128), F32)]
        extra, hbm = [], ()
        if layer > 0:
            inputs = [weights, slopes[layer - 1], *inputs]
            hbm = (0, 1)
            shapes.append(array((ch, length)))
            if layer == LAYERS - 1:
                shapes.append(array((8, width), F32))
            shapes += product_shapes(layer - 1)
            extra = scratch(layer - 1) + [pltpu.SemaphoreType.DMA((2,))]
        return call(
            functools.partial(backward_kernel, layer=layer, n_far=n_far, length=length, **sizes),
            inputs,
            shapes,
            scratch=extra,
            hbm_in=hbm,
            estimate=cost(1, 1),
            name="backward",
        )

    def weigh(layer, path, grads, sources, before):
        inputs = [*grads, *sources, *before]
        return call(
            functools.partial(weight_kernel, layer=layer, path=path, **sizes),
            inputs,
            [array((LAYERS, 3, ch, channels), F32)],
            scratch=[
                pltpu.VMEM((ch, total), BF16),
                pltpu.VMEM((3 * ch, total), BF16),
                pltpu.VMEM((channels // CHUNK, CHUNK // ch, ch, total), BF16),
                pltpu.VMEM((2, 3, ch, CHUNK), F32),
                pltpu.SemaphoreType.DMA((channels // CHUNK, n_seq * (CHUNK // ch))),
                pltpu.SemaphoreType.DMA((2,)),
            ],
            hbm_in=range(n_seq, len(inputs)),
            hbm_out=(0,),
            estimate=cost(6 * ch * channels * total, 2 * channels * total),
            mib=32,
            input_output_aliases={len(inputs): 0} if before else {},
            name="weight",
        )[0]

    sums = reduce_tp(products)
    grads2 = gather_seq(grad2)
    if planned:
        sums, seq2[1:3] = tie(sums, seq2[1:3])
        seq2[3] = swap(seq2[2], "seq", 1)
    upstream, part2, grad1, score_rows, *products = backward(2, sums, upstream)
    scores = score_rows[1, :share]

    grads1 = gather_seq(grad1)
    sums = reduce_tp(products)
    if planned:
        near0 = swap(every0, TP, 1)
        sums, got = tie(sums, [every0, near0, *seq2, *grads1[1:3]])
        (every0, near0), seq2, grads1[1:3] = got[:2], got[2 : 2 + n_seq], got[2 + n_seq :]
        grads1[3] = swap(grads1[2], "seq", 1)
        every2 = collect(seq2)
    upstream, part1, grad0, *products = backward(1, sums, upstream)

    grads0 = gather_seq(grad0)
    sums = reduce_tp(products)
    if planned:
        near1 = swap(every1, TP, 1)
        sums, got = tie(sums, [*grads1, every1, near1, *grads0[1:3]])
        grads1, (every1, near1), grads0[1:3] = got[:n_seq], got[n_seq : n_seq + 2], got[n_seq + 2 :]
        grads0[3] = swap(grads0[2], "seq", 1)
    input_grad, part0 = backward(0, sums, upstream)

    columns = jnp.pad(jnp.stack([p[:, 0] for p in (part0, part1, part2)]), ((0, 8 - LAYERS), (0, 0)))
    if n_seq == 4:
        gain_grad = columns + swap(columns, "seq", 1)
        gain_grad = gain_grad + swap(gain_grad, "seq", 2)
    else:
        gain_grad = sum(gather_seq(columns))

    if planned:
        grads1, _ = tie(grads1, [part0])
        weight_grad = weigh(1, "pair", grads1, [every1, near1], [])
        (every2, *grads2[1:3]), (weight_grad,) = tie([every2, *grads2[1:3]], [weight_grad])
        grads0, got = tie(grads0, [gain_grad, every2, *grads2[1:3]])
        (gain_grad, every2), grads2[1:3] = got[:2], got[2:]
        grads2[3] = swap(grads2[2], "seq", 1)
        weight_grad = weigh(0, "pair", grads0, [every0, near0], [weight_grad])
        weight_grad = weigh(2, "pair", grads2, [every2, swap(every2, TP, 1)], [weight_grad])
    else:
        weight_grad = weigh(0, "whole", grads0, everything[0], [])
        weight_grad = weigh(1, "whole", grads1, everything[1], [weight_grad])
        weight_grad = weigh(2, "whole", grads2, everything[2], [weight_grad])
    return (scores, input_grad, weight_grad.transpose(0, 2, 1, 3), gain_grad[:LAYERS])


def solution(mesh):
    tp = mesh.shape["tp"]
    pairs = jax.sharding.Mesh(mesh.devices.reshape(mesh.shape["seq"], tp // 2, 2), ("seq",) + TP)
    return jax.shard_map(
        local,
        mesh=pairs,
        in_specs=(
            P(TP, "seq"),
            P(None, TP, None, None),
            P(None, TP),
            P(),
            P("seq"),
            P("seq", None),
            P("seq"),
            P("seq"),
            P(TP, "seq"),
            P("seq"),
        ),
        out_specs=(P("seq"), P(TP, "seq"), P(None, TP, None, None), P(None, TP)),
        check_vma=False,
    )
```
